32 devices in a mesh: dp: 4 (over y, core), blk: 8 (over z, x).
Axes of the slice: x: 2, y: 2, z: 4, core: 2. Of those that a mesh axis runs over, the one named last changes fastest.
Arguments:
- tokens: bfloat16 [4, 32, 256, 768], P('dp', None, 'blk'), may hold values from -6 to 6
- frame_seg: int32 [4, 32], P('dp'), may hold values from 0 to 7, never falling along the last dimension, each value on 1 to 16 neighbouring positions
- clip_class: int32 [4, 8], P('dp'), may hold values from 0 to 999
- class_table: float32 [1000, 768], replicated, may hold values from -6 to 6
- mod_weight: bfloat16 [768, 6912], replicated, may hold values from -0.109375 to 0.109375
- mod_bias: float32 [6912], replicated, may hold values from -4 to 4
- qkv_space: bfloat16 [768, 2304], replicated, may hold values from -0.21875 to 0.21875
- out_space: bfloat16 [768, 768], replicated, may hold values from -1.25 to 1.25
- qkv_time: bfloat16 [768, 2304], replicated, may hold values from -0.21875 to 0.21875
- out_time: bfloat16 [768, 768], replicated, may hold values from -0.4375 to 0.4375
- up_weight: bfloat16 [768, 3072], replicated, may hold values from -0.21875 to 0.21875
- down_weight: bfloat16 [3072, 768], replicated, may hold values from -0.21875 to 0.21875
- cotangent: bfloat16 [4, 32, 256, 768], P('dp', None, 'blk'), may hold values from -6 to 6
Outputs:
- mixed: bfloat16 [4, 32, 256, 768], P('dp', None, 'blk')
- input_grad: bfloat16 [4, 32, 256, 768], P('dp', None, 'blk')
- grad_class_table: float32 [1000, 768], P('blk')
- grad_mod_weight: float32 [768, 6912], P('blk')
- grad_mod_bias: float32 [6912], P('blk')
- grad_qkv_space: float32 [768, 2304], P('blk')
- grad_out_space: float32 [768, 768], P('blk')
- grad_qkv_time: float32 [768, 2304], P('blk')
- grad_out_time: float32 [768, 768], P('blk')
- grad_up_weight: float32 [768, 3072], P('blk')
- grad_down_weight: float32 [3072, 768], P('blk')
The draws below stay inside these ranges and needn't reach their ends.
Inputs may be any that keep to these rules, and one draw needn't show every extreme that they name: `frame_seg`: frame clip numbers never fall along a sample's frames; each clip has 1 to 16 frames and one has exactly 16.
All inputs are finite; a program needn't handle non-finite values.
Results may differ from the reference program's by a relative error of at most 0.02.
Values may be sent and summed in bfloat16 or wider, within the bound.
No kernel may reach another device: no remote copies, remote signals or barrier semaphores. Data moves between devices by JAX's collectives and lax.ppermute only.
A program may use at most 320 MiB of HBM per device.

```python
import math
import jax
import jax.numpy as jnp
import numpy as np
from jax import lax

D = 768
HEADS = 12
HEAD_DIM = 64
FF = 3072
NCLASS = 1000
PATCH = 256
FRAMES = 32
BUDGETS = 4
CLIPS = 8
MAXCLIP = 16


def place_ends(drawn, key, low, top_value):
    longest = drawn.shape.index(max(drawn.shape))
    spots = []
    for shift in (0, 1):
        where = [jax.random.randint(jax.random.fold_in(key, axis), (), 0, length) for axis, length in enumerate(drawn.shape)]
        where[longest] = (where[longest] + shift) % drawn.shape[longest]
        spots.append(tuple(where))
    return drawn.at[spots[0]].set(low).at[spots[1]].set(top_value)


def steps_of(key, extent, cuts, smallest, high):
    factor_of, own = 1.0, jax.random.fold_in(key, 6)
    for position, parts in cuts:
        draws = jnp.exp(jax.random.uniform(jax.random.fold_in(own, position), (parts,), jnp.float32, smallest / len(cuts), high / len(cuts)))
        factor_of = factor_of * jnp.repeat(draws, extent[position] // parts).reshape([-1 if axis == position else 1 for axis in range(len(extent))])
    return factor_of


def length_profile(amount, total, reach, skew):
    weights = [(1 << 20) // math.isqrt(grade ** skew) + 1 for grade in range(2, amount + 1)]
    surplus, given = total - reach - (amount - 1), [1] * (amount - 1)
    while surplus > 0:
        movable = [i for i in range(amount - 1) if given[i] < reach]
        whole, budget = sum([weights[i] for i in movable]), surplus
        for i in movable:
            addition = min(reach - given[i], max(1, budget * weights[i] // whole), surplus)
            given[i] = given[i] + addition
            surplus = surplus - addition
    return np.array([reach] + given)


def ragged(own_key, count, total, limit, slope):
    if count == 2:
        one = jax.random.randint(own_key, (), max(1, total - limit), min(limit, total - 1) + 1)
        return jnp.stack([one, total - one])
    tallies = jnp.asarray(length_profile(count, total, limit, slope), jnp.int32)
    couples = (count - 1) // 2
    donor, taker = tallies[1:1 + 2 * couples:2], tallies[2:2 + 2 * couples:2]
    room = jnp.minimum(donor - 1, limit - taker)
    moved = jax.random.randint(jax.random.fold_in(own_key, 1), (couples,), 0, 1 << 20) % (room + 1)
    tallies = tallies.at[1:1 + 2 * couples:2].set(donor - moved).at[2:2 + 2 * couples:2].set(taker + moved)
    return tallies[jax.random.permutation(jax.random.fold_in(own_key, 2), count)]


def normal_values(key, shape, width, bound, shards=(), dtype=jnp.bfloat16):
    gain = steps_of(key, shape, shards, -0.22, 0.18) if shards else 1.0
    drawn = jax.random.normal(key, shape, jnp.float32) * width * gain
    return jnp.minimum(jnp.maximum(drawn, -bound), bound).astype(dtype)


def setup_inputs(seed: int = 0) -> dict:
    streams_of = jax.random.split(jax.random.key(seed), 14)
    return {
        "tokens": normal_values(streams_of[0], (BUDGETS, FRAMES, PATCH, D), 1.0, 6.0, ((0, 4), (2, 8))),
        "frame_seg": jax.vmap(lambda own: jnp.searchsorted(jnp.cumsum(ragged(own, CLIPS, FRAMES, MAXCLIP, 1)), jnp.arange(FRAMES), side="right"))(jax.random.split(streams_of[1], BUDGETS)).reshape((BUDGETS, FRAMES)).astype(jnp.int32),
        "clip_class": place_ends(jax.random.randint(streams_of[2], (BUDGETS, CLIPS), 0, NCLASS), jax.random.fold_in(streams_of[2], 1), 0, NCLASS - 1).astype(jnp.int32),
        "class_table": normal_values(streams_of[3], (NCLASS, D), 1.0, 6.0, (), jnp.float32),
        "mod_weight": normal_values(streams_of[4], (D, 9 * D), (4 * D) ** -0.5, 0.109375),
        "mod_bias": normal_values(streams_of[5], (9 * D,), 0.3, 4.0, (), jnp.float32),
        "qkv_space": normal_values(streams_of[6], (D, 3 * D), D ** -0.5, 0.21875),
        "out_space": normal_values(streams_of[7], (D, D), (D // 32) ** -0.5, 1.25),
        "qkv_time": normal_values(streams_of[8], (D, 3 * D), D ** -0.5, 0.21875),
        "out_time": normal_values(streams_of[9], (D, D), (D // 4) ** -0.5, 0.4375),
        "up_weight": normal_values(streams_of[10], (D, FF), D ** -0.5, 0.21875),
        "down_weight": normal_values(streams_of[11], (FF, D), (FF // 4) ** -0.5, 0.21875),
        "cotangent": normal_values(streams_of[12], (BUDGETS, FRAMES, PATCH, D), 1.0, 6.0, ((0, 4), (2, 8))),
    }


@jax.custom_vjp
def low(v):
    return lax.optimization_barrier(v.astype(jnp.bfloat16)).astype(jnp.float32)

@jax.custom_vjp
def low_back(v):
    return v

def low_keep(v):
    return (low(v), None)

def low_pass(kept, grad):
    return (grad,)

def back_keep(v):
    return (v, None)

def back_low(kept, grad):
    return (low(grad),)
low.defvjp(low_keep, low_pass)
low_back.defvjp(back_keep, back_low)
exact_mode = lax.Precision.HIGHEST

def rounded_both(tensor):
    return low(low_back(tensor))

def split_heads(tensor):
    return tensor.reshape(tensor.shape[:-1] + (HEADS, HEAD_DIM))

def project(tensor, weight):
    return jnp.einsum('fpd,de->fpe', tensor, weight, precision=exact_mode)

def layer_norm_mod(values, shift_by, scale_by):
    center_mean = lax.optimization_barrier(jnp.mean(values, -1, keepdims=True))
    centered = values - center_mean
    variance = lax.optimization_barrier(jnp.mean(centered * centered, -1, keepdims=True))
    return centered * lax.rsqrt(variance + 1e-06) * (1.0 + scale_by[:, None, :]) + shift_by[:, None, :]

def space_attend(normed, weight):
    projected = rounded_both(project(normed, weight))
    queries, key_rows, value_rows = [split_heads(section) for section in jnp.split(projected, 3, -1)]
    scores = low_back(0.125 * jnp.einsum('fphd,fkhd->fhpk', queries, key_rows, precision=exact_mode))
    soft_prob = low(jax.nn.softmax(scores, -1))
    attended = jnp.einsum('fhpk,fkhd->fphd', soft_prob, value_rows, precision=exact_mode)
    return rounded_both(attended.reshape(normed.shape))

def time_attend(normed, weight, segment):
    projected = rounded_both(project(normed, weight))
    queries, key_rows, value_rows = [split_heads(section) for section in jnp.split(projected, 3, -1)]
    same_clip = segment[:, None] == segment[None, :]
    scores = low_back(0.125 * jnp.einsum('fphd,gphd->phfg', queries, key_rows, precision=exact_mode))
    scores = jnp.where(same_clip[None, None], scores, -1e+30)
    soft_prob = low(jax.nn.softmax(scores, -1))
    attended = jnp.einsum('phfg,gphd->fphd', soft_prob, value_rows, precision=exact_mode)
    return rounded_both(attended.reshape(normed.shape))

def forward_budget(tokens_in, segment, classes, class_table, mod_weight, mod_bias, qkv_space, out_space, qkv_time, out_time, up_weight, down_weight):
    frame_class = classes[segment]
    embedded = low(jax.nn.silu(class_table[frame_class]))
    modulation = jnp.dot(embedded, mod_weight, precision=exact_mode) + mod_bias
    pieces = jnp.split(modulation, 9, -1)
    normed = low(layer_norm_mod(tokens_in, pieces[0], pieces[1]))
    branch = low_back(project(space_attend(normed, qkv_space), out_space))
    first = tokens_in + pieces[2][:, None, :] * branch
    normed = low(layer_norm_mod(first, pieces[3], pieces[4]))
    branch = low_back(project(time_attend(normed, qkv_time, segment), out_time))
    second = first + pieces[5][:, None, :] * branch
    normed = low(layer_norm_mod(second, pieces[6], pieces[7]))
    hidden = low(jax.nn.gelu(low_back(project(normed, up_weight)), approximate=True))
    branch = low_back(project(hidden, down_weight))
    return second + pieces[8][:, None, :] * branch

def reference(tokens, frame_seg, clip_class, class_table, mod_weight, mod_bias, qkv_space, out_space, qkv_time, out_time, up_weight, down_weight, cotangent):
    params = (class_table.astype(jnp.float32), mod_weight.astype(jnp.float32), mod_bias.astype(jnp.float32), qkv_space.astype(jnp.float32), out_space.astype(jnp.float32), qkv_time.astype(jnp.float32), out_time.astype(jnp.float32), up_weight.astype(jnp.float32), down_weight.astype(jnp.float32))

    def one_budget(totals, inputs):
        budget_tokens, budget_seg, budget_class, budget_cot = inputs

        def forward(tokens_in, *weights):
            return forward_budget(tokens_in, budget_seg, budget_class, *weights)
        result, pullback = jax.vjp(forward, budget_tokens.astype(jnp.float32), *params)
        gradients = pullback(budget_cot.astype(jnp.float32))
        totals = jax.tree.map(jnp.add, totals, tuple(gradients[1:]))
        return (totals, (result.astype(jnp.bfloat16), gradients[0].astype(jnp.bfloat16)))
    zero_grads = tuple((jnp.zeros_like(weight) for weight in params))
    totals, outputs = lax.scan(one_budget, zero_grads, (tokens, frame_seg, clip_class, cotangent))
    return (outputs[0], outputs[1]) + tuple(totals)
```

```python
from functools import partial

import jax
import jax.numpy as jnp
from jax import lax
from jax.experimental import pallas as pl
from jax.experimental.pallas import tpu as pltpu
from jax.sharding import PartitionSpec as P

HEADS = 12
HEAD_DIM = 64
D = HEADS * HEAD_DIM
PAIRS = HEADS // 2
BF = jnp.bfloat16
F32 = jnp.float32
exact_mode = lax.Precision.HIGHEST
masked_score = -1e30
EPS = 1e-6
GELU_C = 0.7978845608028654
GELU_A = 0.044715
VMEM_LIMIT = 60 * 1024 * 1024


def mm(a, b):
    return lax.dot_general(a, b, (((1,), (0,)), ((), ())), preferred_element_type=F32)


def mm_nt(a, b):
    return lax.dot_general(a, b, (((1,), (1,)), ((), ())), preferred_element_type=F32)


def mm_tn(a, b):
    return lax.dot_general(a, b, (((0,), (0,)), ((), ())), preferred_element_type=F32)


def first_head():
    return lax.broadcasted_iota(jnp.int32, (1, 2 * HEAD_DIM), 1) < HEAD_DIM


def norm_stats(x):
    mean = jnp.mean(x, -1, keepdims=True)
    xc = x - mean
    var = jnp.mean(xc * xc, -1, keepdims=True)
    rstd = lax.rsqrt(var + EPS)
    return xc * rstd, rstd


def norm_back(dn, xhat, rstd, scale):
    e = dn * (1.0 + scale)
    return rstd * (
        e - jnp.mean(e, -1, keepdims=True) - xhat * jnp.mean(e * xhat, -1, keepdims=True)
    )


def attend_pair(q2, k2, v2, mask, bias):
    zero, one = jnp.zeros_like(q2), jnp.ones_like(v2)
    scaled = q2 * jnp.asarray(0.125, BF)

    def head(q, v):
        s = mm_nt(q, k2)
        if bias is not None:
            s = s + bias
        e = jnp.exp(s - jnp.max(s, -1, keepdims=True)).astype(BF)
        return mm(e, v)

    ra = head(jnp.where(mask, scaled, zero), jnp.where(mask, v2, one))
    rb = head(jnp.where(mask, zero, scaled), jnp.where(mask, one, v2))
    total = pltpu.roll(jnp.where(mask, rb, ra), HEAD_DIM, 1)
    return jnp.where(mask, ra, rb) / total


def attend_pair_back(q2, k2, v2, do2, mask, bias):
    zero = jnp.zeros_like(q2)
    scaled = q2 * jnp.asarray(0.125, BF)

    def head(q, do):
        s = mm_nt(k2, q)
        if bias is not None:
            s = s + bias
        e = jnp.exp(s - jnp.max(s, 0, keepdims=True))
        p = e * (1.0 / jnp.sum(e, 0, keepdims=True))
        dp = mm_nt(v2, do)
        ds = p * (dp - jnp.sum(p * dp, 0, keepdims=True))
        return p.astype(BF), ds.astype(BF)

    qa, qb = jnp.where(mask, scaled, zero), jnp.where(mask, zero, scaled)
    da, db = jnp.where(mask, do2, zero), jnp.where(mask, zero, do2)
    ka, kb = jnp.where(mask, k2, zero), jnp.where(mask, zero, k2)
    pa, dsa = head(qa, da)
    pb, dsb = head(qb, db)
    dv2 = mm(pa, da) + mm(pb, db)
    dk2 = mm(dsa, qa) + mm(dsb, qb)
    dq2 = 0.125 * (mm_tn(dsa, ka) + mm_tn(dsb, kb))
    return dq2, dk2, dv2


def space_forward_kernel(stripes, chunks, *refs):
    x_refs = refs[:stripes]
    mod_ref, w_ref = refs[stripes : stripes + 2]
    att_refs = refs[stripes + 2 : stripes + 2 + stripes * chunks]
    n1_ref, qkv_ref = refs[stripes + 2 + stripes * chunks :]
    rows = x_refs[0].shape[1]
    part = rows // chunks
    for j in range(stripes):
        x = x_refs[j][0].astype(F32)
        xhat, _ = norm_stats(x)
        n1_ref[0, j * rows : (j + 1) * rows, :] = (
            xhat * (1.0 + mod_ref[0, 1:2, :]) + mod_ref[0, 0:1, :]
        ).astype(BF)
    for s in range(3):
        qkv_ref[0, :, s * D : (s + 1) * D] = mm(
            n1_ref[0], w_ref[:, s * D : (s + 1) * D]
        ).astype(BF)
    mask = first_head()
    for h in range(PAIRS):
        q2, k2, v2 = (
            qkv_ref[0, :, s * D + h * 128 : s * D + (h + 1) * 128] for s in range(3)
        )
        att = attend_pair(q2, k2, v2, mask, None).astype(BF)
        for j in range(stripes):
            for c in range(chunks):
                at = j * rows + c * part
                att_refs[j * chunks + c][0, :, h * 128 : (h + 1) * 128] = att[at : at + part]


def space_forward(blocks, mod_own, weight, chunks):
    stripes = len(blocks)
    frames, rows, _ = blocks[0].shape
    part, whole = rows // chunks, rows * stripes
    outs = pl.pallas_call(
        partial(space_forward_kernel, stripes, chunks),
        grid=(frames,),
        in_specs=[pl.BlockSpec((1, rows, D), lambda f: (f, 0, 0))] * stripes
        + [
            pl.BlockSpec((1,) + mod_own.shape[1:], lambda f: (f, 0, 0)),
            pl.BlockSpec(weight.shape, lambda f: (0, 0)),
        ],
        out_specs=[pl.BlockSpec((1, part, D), lambda f: (f, 0, 0))] * (stripes * chunks)
        + [
            pl.BlockSpec((1, whole, D), lambda f: (f, 0, 0)),
            pl.BlockSpec((1, whole, 3 * D), lambda f: (f, 0, 0)),
        ],
        out_shape=[jax.ShapeDtypeStruct((frames, part, D), BF)] * (stripes * chunks)
        + [
            jax.ShapeDtypeStruct((frames, whole, D), BF),
            jax.ShapeDtypeStruct((frames, whole, 3 * D), BF),
        ],
        compiler_params=pltpu.CompilerParams(vmem_limit_bytes=VMEM_LIMIT),
        name="space_forward",
    )(*blocks, mod_own, weight)
    sends = [[outs[j * chunks + c] for j in range(stripes)] for c in range(chunks)]
    return sends, outs[-2], outs[-1]


def space_backward_kernel(stripes, chunks, *refs):
    x_refs = refs[:stripes]
    d_refs = refs[stripes : stripes * (1 + chunks)]
    mod_ref, w_ref, qkv_ref = refs[stripes * (1 + chunks) : stripes * (1 + chunks) + 3]
    dv_refs = refs[stripes * (1 + chunks) + 3 : stripes * (2 + chunks) + 3]
    dqkv_ref, dmod_ref, datt_ref = refs[stripes * (2 + chunks) + 3 :]
    rows = x_refs[0].shape[1]
    part = rows // chunks
    for j in range(stripes):
        for c in range(chunks):
            at = j * rows + c * part
            datt_ref[at : at + part, :] = d_refs[c * stripes + j][0]
    mask = first_head()
    for h in range(PAIRS):
        q2, k2, v2 = (
            qkv_ref[0, :, s * D + h * 128 : s * D + (h + 1) * 128] for s in range(3)
        )
        grads = attend_pair_back(q2, k2, v2, datt_ref[:, h * 128 : (h + 1) * 128], mask, None)
        for s in range(3):
            dqkv_ref[0, :, s * D + h * 128 : s * D + (h + 1) * 128] = grads[s].astype(BF)
    dn = mm_nt(dqkv_ref[0], w_ref[...])
    shift_sum = jnp.zeros((1, D), F32)
    scale_sum = jnp.zeros((1, D), F32)
    for j in range(stripes):
        xhat, rstd = norm_stats(x_refs[j][0].astype(F32))
        d = dn[j * rows : (j + 1) * rows]
        dv_refs[j][0] = norm_back(d, xhat, rstd, mod_ref[0, 1:2, :]).astype(BF)
        shift_sum = shift_sum + jnp.sum(d, 0, keepdims=True)
        scale_sum = scale_sum + jnp.sum(d * xhat, 0, keepdims=True)
    dmod_ref[0, 0:1, :] = shift_sum
    dmod_ref[0, 1:2, :] = scale_sum


def space_backward(blocks, grads, mod_own, weight, qkv):
    stripes, chunks = len(blocks), len(grads)
    frames, rows, _ = blocks[0].shape
    part, whole = rows // chunks, rows * stripes
    flat = [g for chunk in grads for g in chunk]
    outs = pl.pallas_call(
        partial(space_backward_kernel, stripes, chunks),
        grid=(frames,),
        in_specs=[pl.BlockSpec((1, rows, D), lambda f: (f, 0, 0))] * stripes
        + [pl.BlockSpec((1, part, D), lambda f: (f, 0, 0))] * (stripes * chunks)
        + [
            pl.BlockSpec((1,) + mod_own.shape[1:], lambda f: (f, 0, 0)),
            pl.BlockSpec(weight.shape, lambda f: (0, 0)),
            pl.BlockSpec((1, whole, 3 * D), lambda f: (f, 0, 0)),
        ],
        out_specs=[pl.BlockSpec((1, rows, D), lambda f: (f, 0, 0))] * stripes
        + [
            pl.BlockSpec((1, whole, 3 * D), lambda f: (f, 0, 0)),
            pl.BlockSpec((1, 2, D), lambda f: (f, 0, 0)),
        ],
        out_shape=[jax.ShapeDtypeStruct((frames, rows, D), BF)] * stripes
        + [
            jax.ShapeDtypeStruct((frames, whole, 3 * D), BF),
            jax.ShapeDtypeStruct((frames, 2, D), F32),
        ],
        scratch_shapes=[pltpu.VMEM((whole, D), BF)],
        compiler_params=pltpu.CompilerParams(vmem_limit_bytes=VMEM_LIMIT),
        name="space_backward",
    )(*blocks, *flat, mod_own, weight, qkv)
    return outs[:stripes], outs[-2], outs[-1]


def middle_kernel(stripes, *refs):
    me_ref, bias_ref, mod_ref = refs[:3]
    a_refs = refs[3 : 3 + stripes]
    tok_ref, cot_ref, wos, wqkv, wot, wu, wd = refs[3 + stripes : 10 + stripes]
    outs = refs[10 + stripes :]
    mixed_ref, dfirst_ref = outs[:2]
    datt_refs = outs[2 : 2 + stripes]
    (
        att1_ref,
        db1_ref,
        n2_ref,
        dqkv_ref,
        att2_ref,
        db2_ref,
        n3_ref,
        dup_ref,
        hid_ref,
        db3_ref,
        dmod_ref,
        nat_ref,
        b1_ref,
        first_ref,
        b2_ref,
        second_ref,
        b3_ref,
        dn_ref,
        up_ref,
        dh_ref,
        qkv_ref,
    ) = outs[2 + stripes :]
    frames, patches, _ = tok_ref.shape
    groups = patches // 8
    rows = frames * patches
    rows_g = frames * 8
    per = frames // stripes
    ff = wu.shape[1]
    me = me_ref[0]
    mask = first_head()

    for j in range(stripes):
        s = lax.bitwise_xor(me, j)
        start = pl.multiple_of(s * (per * patches), per * patches)
        att1_ref[pl.ds(start, per * patches), :] = a_refs[j][...].reshape(per * patches, D)
    nat_ref[...] = mm(att1_ref[...], wos[...]).reshape(frames, patches, D)

    step = 4

    def spots(i, g):
        fs = pl.ds(i * step, step)
        at = pl.ds(pl.multiple_of(g * rows_g + i * step * 8, step * 8), step * 8)
        return fs, at

    def as3(x):
        return x.reshape(step, 8, D)

    def as2(x):
        return x.reshape(step * 8, D)

    def over_patches(terms):
        total = terms[0]
        for t in terms[1:]:
            total = total + t
        return jnp.sum(total, 1, keepdims=True)

    def stage_one(i, carry):
        for g in range(groups):
            fs, at = spots(i, g)
            tok = tok_ref[fs].astype(F32)[:, 8 * g : 8 * g + 8]
            b1 = nat_ref[fs, 8 * g : 8 * g + 8, :]
            first = tok + mod_ref[fs, 2:3, :] * b1
            xhat, _ = norm_stats(first)
            n2 = xhat * (1.0 + mod_ref[fs, 4:5, :]) + mod_ref[fs, 3:4, :]
            b1_ref[at, :] = as2(b1)
            first_ref[at, :] = as2(first)
            n2_ref[at, :] = as2(n2).astype(BF)
        return carry

    lax.fori_loop(0, frames // step, stage_one, 0)

    for s in range(3):
        qkv_ref[:, s * D : (s + 1) * D] = mm(n2_ref[...], wqkv[:, s * D : (s + 1) * D]).astype(BF)

    def time_attend(g, carry):
        at = pl.ds(pl.multiple_of(g * rows_g, rows_g), rows_g)
        for h in range(PAIRS):
            q2, k2, v2 = (
                qkv_ref[at, s * D + h * 128 : s * D + (h + 1) * 128] for s in range(3)
            )
            att2_ref[at, h * 128 : (h + 1) * 128] = attend_pair(
                q2, k2, v2, mask, bias_ref[...]
            ).astype(BF)
        return carry

    lax.fori_loop(0, groups, time_attend, 0)
    b2_ref[...] = mm(att2_ref[...], wot[...])

    def stage_two(i, carry):
        for g in range(groups):
            fs, at = spots(i, g)
            second = as3(first_ref[at, :]) + mod_ref[fs, 5:6, :] * as3(b2_ref[at, :])
            xhat, _ = norm_stats(second)
            n3 = xhat * (1.0 + mod_ref[fs, 7:8, :]) + mod_ref[fs, 6:7, :]
            cot = cot_ref[fs].astype(F32)[:, 8 * g : 8 * g + 8]
            second_ref[at, :] = as2(second)
            n3_ref[at, :] = as2(n3).astype(BF)
            db3_ref[at, :] = as2(mod_ref[fs, 8:9, :] * cot).astype(BF)
        return carry

    lax.fori_loop(0, frames // step, stage_two, 0)

    wide = up_ref.shape[1]
    b3_ref[...] = jnp.zeros_like(b3_ref)
    dn_ref[...] = jnp.zeros_like(dn_ref)

    def feed(b, carry):
        cols = pl.ds(pl.multiple_of(b * wide, wide), wide)
        up_ref[...] = mm(n3_ref[...], wu[:, cols])
        dh_ref[...] = mm_nt(db3_ref[...], wd[cols, :])

        def piece(r, inner):
            at = pl.ds(pl.multiple_of(r * 32, 32), 32)
            u = up_ref[at, :]
            u2 = u * u
            t = jnp.tanh(u * (GELU_C + (GELU_C * GELU_A) * u2))
            half = 0.5 + 0.5 * t
            slope = half + (0.5 * u) * ((1.0 - t * t) * (GELU_C + (3.0 * GELU_C * GELU_A) * u2))
            hid_ref[at, cols] = (u * half).astype(BF)
            dup_ref[at, cols] = (dh_ref[at, :] * slope).astype(BF)
            return inner

        lax.fori_loop(0, rows // 32, piece, 0)
        b3_ref[...] += mm(hid_ref[:, cols], wd[cols, :])
        dn_ref[...] += mm_nt(dup_ref[:, cols], wu[:, cols])
        return carry

    lax.fori_loop(0, ff // wide, feed, 0)

    def stage_three(i, carry):
        parts = [[] for _ in range(4)]
        for g in range(groups):
            fs, at = spots(i, g)
            cot = cot_ref[fs].astype(F32)[:, 8 * g : 8 * g + 8]
            second = as3(second_ref[at, :])
            b3 = as3(b3_ref[at, :])
            dn = as3(dn_ref[at, :])
            xhat, rstd = norm_stats(second)
            dsecond = cot + norm_back(dn, xhat, rstd, mod_ref[fs, 7:8, :])
            nat_ref[fs, 8 * g : 8 * g + 8, :] = second + mod_ref[fs, 8:9, :] * b3
            second_ref[at, :] = as2(dsecond)
            db2_ref[at, :] = as2(mod_ref[fs, 5:6, :] * dsecond).astype(BF)
            for k, t in enumerate((dsecond * as3(b2_ref[at, :]), dn, dn * xhat, cot * b3)):
                parts[k].append(t)
        fs, _ = spots(i, 0)
        for k in range(4):
            dmod_ref[fs, 3 + k : 4 + k, :] = over_patches(parts[k])
        mixed_ref[fs] = nat_ref[fs].astype(BF)
        return carry

    lax.fori_loop(0, frames // step, stage_three, 0)

    up_ref[...] = mm_nt(db2_ref[...], wot[...])

    def time_back(g, carry):
        at = pl.ds(pl.multiple_of(g * rows_g, rows_g), rows_g)
        for h in range(PAIRS):
            q2, k2, v2 = (
                qkv_ref[at, s * D + h * 128 : s * D + (h + 1) * 128] for s in range(3)
            )
            do2 = up_ref[at, h * 128 : (h + 1) * 128].astype(BF)
            grads = attend_pair_back(q2, k2, v2, do2, mask, bias_ref[...])
            for s in range(3):
                dqkv_ref[at, s * D + h * 128 : s * D + (h + 1) * 128] = grads[s].astype(BF)
        return carry

    lax.fori_loop(0, groups, time_back, 0)
    dn_ref[...] = mm_nt(dqkv_ref[...], wqkv[...])

    def stage_four(i, carry):
        parts = [[] for _ in range(3)]
        for g in range(groups):
            fs, at = spots(i, g)
            dn = as3(dn_ref[at, :])
            xhat, rstd = norm_stats(as3(first_ref[at, :]))
            dfirst = as3(second_ref[at, :]) + norm_back(dn, xhat, rstd, mod_ref[fs, 4:5, :])
            nat_ref[fs, 8 * g : 8 * g + 8, :] = dfirst
            for k, t in enumerate((dfirst * as3(b1_ref[at, :]), dn, dn * xhat)):
                parts[k].append(t)
        fs, _ = spots(i, 0)
        for k in range(3):
            dmod_ref[fs, k : k + 1, :] = over_patches(parts[k])
        dfirst = nat_ref[fs]
        dfirst_ref[fs] = dfirst.astype(BF)
        span = step * patches
        db1_ref[pl.ds(pl.multiple_of(i * span, span), span), :] = (
            (mod_ref[fs, 2:3, :] * dfirst).astype(BF).reshape(span, D)
        )
        return carry

    lax.fori_loop(0, frames // step, stage_four, 0)

    nat_ref[...] = mm_nt(db1_ref[...], wos[...]).reshape(frames, patches, D)
    for j in range(stripes):
        s = lax.bitwise_xor(me, j)
        datt_refs[j][...] = nat_ref[pl.ds(s * per, per)].astype(BF)


def middle(me, bias, modulation, attended, tokens, cotangent, weights):
    stripes = len(attended)
    frames, patches, _ = tokens.shape
    rows = frames * patches
    ff = weights[3].shape[1]
    vmem = pl.BlockSpec(memory_space=pltpu.VMEM)
    bf = lambda *shape: jax.ShapeDtypeStruct(shape, BF)
    wide = 768
    outs = pl.pallas_call(
        partial(middle_kernel, stripes),
        in_specs=[pl.BlockSpec(memory_space=pltpu.SMEM)] + [vmem] * (9 + stripes),
        out_specs=[vmem] * (13 + stripes),
        out_shape=[bf(frames, patches, D), bf(frames, patches, D)]
        + [bf(frames // stripes, patches, D)] * stripes
        + [
            bf(rows, D),
            bf(rows, D),
            bf(rows, D),
            bf(rows, 3 * D),
            bf(rows, D),
            bf(rows, D),
            bf(rows, D),
            bf(rows, ff),
            bf(rows, ff),
            bf(rows, D),
            jax.ShapeDtypeStruct((frames, 7, D), F32),
        ],
        scratch_shapes=[pltpu.VMEM((frames, patches, D), F32)]
        + [pltpu.VMEM((rows, D), F32)] * 6
        + [pltpu.VMEM((rows, wide), F32)] * 2
        + [pltpu.VMEM((rows, 3 * D), BF)],
        compiler_params=pltpu.CompilerParams(vmem_limit_bytes=VMEM_LIMIT),
        name="middle",
    )(me, bias, modulation, *attended, tokens, cotangent, *weights)
    return outs[0], outs[1], outs[2 : 2 + stripes], outs[2 + stripes : -1], outs[-1]


def finish_kernel(stripes, chunks, me_ref, *refs):
    dv_refs = refs[:stripes]
    first_refs = refs[stripes : stripes + chunks]
    out_ref = refs[-1]
    per = dv_refs[0].shape[0]
    part = first_refs[0].shape[1]
    for j in range(stripes):
        fs = pl.ds(lax.bitwise_xor(me_ref[0], j) * per, per)
        for c in range(chunks):
            spot = pl.ds(c * part, part)
            out_ref[fs, spot, :] = (
                dv_refs[j][:, spot, :].astype(F32) + first_refs[c][fs].astype(F32)
            ).astype(BF)


def finish(me, dvs, firsts):
    stripes, chunks = len(dvs), len(firsts)
    frames, part, _ = firsts[0].shape
    vmem = pl.BlockSpec(memory_space=pltpu.VMEM)
    return pl.pallas_call(
        partial(finish_kernel, stripes, chunks),
        in_specs=[pl.BlockSpec(memory_space=pltpu.SMEM)] + [vmem] * (stripes + chunks),
        out_specs=vmem,
        out_shape=jax.ShapeDtypeStruct((frames, part * chunks, D), BF),
        compiler_params=pltpu.CompilerParams(vmem_limit_bytes=VMEM_LIMIT),
        name="finish",
    )(me, *dvs, *firsts)


def flip(x, axis, bit):
    size = lax.axis_size(axis)
    return lax.ppermute(x, axis, [(i, i ^ bit) for i in range(size)])


def exchange(blocks):
    return [blocks[0]] + [flip(blocks[j], "blk", j) for j in range(1, len(blocks))]


def halve(x, axis, bit, dim):
    own = (lax.axis_index(axis) // bit) % 2
    half = x.shape[dim] // 2
    keep = lax.dynamic_slice_in_dim(x, own * half, half, dim)
    send = lax.dynamic_slice_in_dim(x, (1 - own) * half, half, dim)
    got = flip(send, axis, bit)
    return (keep.astype(F32) + got.astype(F32)).astype(BF)


def double(x, axis, bit, dim):
    own = (lax.axis_index(axis) // bit) % 2
    got = flip(x, axis, bit)
    low = jnp.where(own == 0, x, got)
    high = jnp.where(own == 0, got, x)
    return jnp.concatenate([low, high], dim)


def bits_of(size):
    return [1 << b for b in range(size.bit_length() - 1)]


def reduce_units(units):
    stripes = units.shape[0]
    dims = []
    for bit in bits_of(lax.axis_size("dp")):
        dim = 2 if bit == 1 else 3
        units = halve(units, "dp", bit, dim)
        dims.append((bit, dim))
    x = units
    for bit in bits_of(stripes):
        shape = x.shape
        x = halve(x.reshape((shape[0] // 2, 2) + shape[1:]), "blk", bit, 1).reshape(
            (shape[0] // 2,) + shape[1:]
        )
    for bit, dim in reversed(dims):
        x = double(x, "dp", bit, dim)
    return x[0].astype(F32)


def to_units(grad, stripes):
    rows, cols = grad.shape[0] // stripes, grad.shape[1] // D
    small = D // stripes
    x = grad.reshape(stripes, rows // small, small, cols, D)
    return jnp.transpose(x, (0, 1, 3, 2, 4)).reshape(stripes, -1, small, D)


def from_units(units, rows, cols):
    small = units.shape[1]
    x = units.reshape(rows // small, cols // D, small, D)
    return jnp.transpose(x, (0, 2, 1, 3)).reshape(rows, cols)


def reduce_weights(grads):
    stripes = lax.axis_size("blk")
    units = [to_units(g, stripes) for g in grads]
    total = reduce_units(jnp.concatenate(units, 1))
    outs, at = [], 0
    for g, u in zip(grads, units):
        n = u.shape[1]
        outs.append(from_units(total[at : at + n], g.shape[0] // stripes, g.shape[1]))
        at += n
    return outs


def shards(
    tokens,
    frame_seg,
    clip_class,
    class_table,
    mod_weight,
    mod_bias,
    qkv_space,
    out_space,
    qkv_time,
    out_time,
    up_weight,
    down_weight,
    cotangent,
):
    stripes = lax.axis_size("blk")
    stripe = lax.axis_index("blk")
    me = stripe.astype(jnp.int32).reshape(1)
    tokens, cotangent = tokens[0], cotangent[0]
    frames, patches, _ = tokens.shape
    per = frames // stripes
    chunks = 2
    part = patches // chunks
    classes = class_table.shape[0]

    blocks = [
        lax.dynamic_slice_in_dim(tokens, (stripe ^ j) * per, per, 0) for j in range(stripes)
    ]
    blocks = exchange(blocks)

    segment = frame_seg[0]
    clip_ids = clip_class[0]
    clip_hit = segment[:, None] == jnp.arange(clip_ids.shape[0], dtype=jnp.int32)[None, :]
    frame_class = jnp.sum(jnp.where(clip_hit, clip_ids[None, :], 0), axis=1)
    class_hit = (
        frame_class[:, None] == jnp.arange(classes, dtype=jnp.int32)[None, :]
    ).astype(F32)
    embedded = jnp.dot(class_hit, class_table, precision=exact_mode)
    cond = jax.nn.silu(embedded).astype(BF)
    modulation = jnp.dot(cond, mod_weight, preferred_element_type=F32) + mod_bias
    modulation = modulation.reshape(frames, 9, D)
    mod_own = lax.dynamic_slice_in_dim(modulation, stripe * per, per, 0)[:, :2]
    spot_frame = jnp.repeat(jnp.arange(frames), 8)
    spot_patch = jnp.tile(jnp.arange(8), frames)
    spot_seg = jnp.repeat(segment, 8)
    bias = jnp.where(
        (spot_seg[:, None] == spot_seg[None, :]) & (spot_patch[:, None] == spot_patch[None, :]),
        0.0,
        masked_score,
    ).astype(F32)

    sends, normed_one, qkv_one = space_forward(blocks, mod_own, qkv_space, chunks)
    attended = [exchange(s) for s in sends]
    weights = (out_space, qkv_time, out_time, up_weight, down_weight)
    parts = []
    for c in range(chunks):
        here = slice(c * part, (c + 1) * part)
        parts.append(
            middle(me, bias, modulation, attended[c], tokens[:, here], cotangent[:, here], weights)
        )
    output = jnp.concatenate([p[0] for p in parts], 1)
    grads = [exchange(p[2]) for p in parts]

    def weight_grad(a, b):
        total = sum(mm_tn(p[3][a], p[3][b]) for p in parts)
        return total.astype(BF)

    grad_out_space = weight_grad(0, 1)
    grad_qkv_time = weight_grad(2, 3)
    grad_out_time = weight_grad(4, 5)
    grad_up = weight_grad(6, 7)
    grad_down = weight_grad(8, 9)
    grad_up, grad_down = reduce_weights([grad_up, grad_down])
    grad_qkv_time, grad_out_time, grad_out_space = reduce_weights(
        [grad_qkv_time, grad_out_time, grad_out_space]
    )

    late = sum(p[4] for p in parts).astype(BF).reshape(frames, 7 * D)
    late = lax.psum_scatter(late, "blk", scatter_dimension=0, tiled=True)

    dvs, dqkv_one, early = space_backward(blocks, grads, mod_own, qkv_space, qkv_one)
    grad_qkv_space = mm_tn(
        normed_one.reshape(-1, D), dqkv_one.reshape(-1, 3 * D)
    ).astype(BF)
    (grad_qkv_space,) = reduce_weights([grad_qkv_space])
    input_grad = finish(me, exchange(dvs), [p[1] for p in parts])

    mod_grad = jnp.concatenate([early.astype(BF).reshape(per, 2 * D), late], 1)
    mod_grad = lax.all_gather(mod_grad, ("dp", "blk"), tiled=True)
    class_all = lax.all_gather(frame_class, "dp", tiled=True)
    hit_all = (class_all[:, None] == jnp.arange(classes, dtype=jnp.int32)[None, :]).astype(F32)
    embedded_all = jnp.dot(hit_all, class_table, precision=exact_mode)
    cond_all, silu_back = jax.vjp(jax.nn.silu, embedded_all)
    cond_all = cond_all.astype(BF)
    width = D // stripes
    cond_own = lax.dynamic_slice_in_dim(cond_all, stripe * width, width, 1)
    grad_mod_weight = mm_tn(cond_own, mod_grad)
    share = mod_bias.shape[0] // stripes
    grad_mod_bias = jnp.sum(
        lax.dynamic_slice_in_dim(mod_grad, stripe * share, share, 1).astype(F32), 0
    )
    cond_grad = mm_nt(mod_grad, mod_weight)
    embed_grad = silu_back(cond_grad)[0]
    span = classes // stripes
    hit_own = lax.dynamic_slice_in_dim(hit_all, stripe * span, span, 1)
    grad_table = lax.dot_general(
        hit_own, embed_grad, (((0,), (0,)), ((), ())), precision=exact_mode
    )
    return (
        output[None],
        input_grad[None],
        grad_table,
        grad_mod_weight,
        grad_mod_bias,
        grad_qkv_space,
        grad_out_space,
        grad_qkv_time,
        grad_out_time,
        grad_up,
        grad_down,
    )


def solution(mesh):
    tile = P("dp", None, "blk", None)
    row = P("blk", None)
    in_specs = (tile, P("dp", None), P("dp", None)) + (P(),) * 9 + (tile,)
    out_specs = (tile, tile, row, row, P("blk")) + (row,) * 6
    return jax.shard_map(shards, mesh=mesh, in_specs=in_specs, out_specs=out_specs, check_vma=False)
```

```python
from functools import partial

import jax
import jax.numpy as jnp
from jax import lax
from jax.experimental import pallas as pl
from jax.experimental.pallas import tpu as pltpu
from jax.sharding import PartitionSpec as P

HEADS = 12
HEAD_DIM = 64
D = HEADS * HEAD_DIM
PAIRS = HEADS // 2
BF = jnp.bfloat16
F32 = jnp.float32
exact_mode = lax.Precision.HIGHEST
masked_score = -1e30
EPS = 1e-6
GELU_C = 0.7978845608028654
GELU_A = 0.044715
VMEM_LIMIT = 60 * 1024 * 1024


def mm(a, b):
    return lax.dot_general(a, b, (((1,), (0,)), ((), ())), preferred_element_type=F32)


def mm_nt(a, b):
    return lax.dot_general(a, b, (((1,), (1,)), ((), ())), preferred_element_type=F32)


def mm_tn(a, b):
    return lax.dot_general(a, b, (((0,), (0,)), ((), ())), preferred_element_type=F32)


CHEAP = pl.CostEstimate(flops=1, bytes_accessed=1, transcendentals=0)
ANYWHERE = pl.BlockSpec(memory_space=pl.ANY)


def call(kernel, operands, in_specs, deps=(), **options):
    inputs, extra = len(operands), len(deps)

    def body(*refs):
        kernel(*refs[:inputs], *refs[inputs + extra :])

    return pl.pallas_call(
        body,
        in_specs=list(in_specs) + [ANYWHERE] * extra,
        compiler_params=pltpu.CompilerParams(vmem_limit_bytes=VMEM_LIMIT),
        cost_estimate=CHEAP,
        **options,
    )(*operands, *deps)


def first_head():
    return lax.broadcasted_iota(jnp.int32, (1, 2 * HEAD_DIM), 1) < HEAD_DIM


def norm_stats(x):
    mean = jnp.mean(x, -1, keepdims=True)
    xc = x - mean
    var = jnp.mean(xc * xc, -1, keepdims=True)
    rstd = lax.rsqrt(var + EPS)
    return xc * rstd, rstd


def norm_back(dn, xhat, rstd, scale):
    e = dn * (1.0 + scale)
    return rstd * (
        e - jnp.mean(e, -1, keepdims=True) - xhat * jnp.mean(e * xhat, -1, keepdims=True)
    )


def attend_pair(q2, k2, v2, mask, bias):
    zero, one = jnp.zeros_like(q2), jnp.ones_like(v2)
    scaled = q2 * jnp.asarray(0.125, BF)

    def head(q, v):
        s = mm_nt(q, k2)
        if bias is not None:
            s = s + bias
        top = jnp.max(s, -1, keepdims=True)
        return mm(jnp.exp(s - top).astype(BF), v), top

    ra, ma = head(jnp.where(mask, scaled, zero), jnp.where(mask, v2, one))
    rb, mb = head(jnp.where(mask, zero, scaled), jnp.where(mask, one, v2))
    total = pltpu.roll(jnp.where(mask, rb, ra), HEAD_DIM, 1)
    return jnp.where(mask, ra, rb) / total, jnp.where(mask, ma, mb) + jnp.log(total)


def pair_rows(logs):
    lane = lax.broadcasted_iota(jnp.int32, (1, 2 * HEAD_DIM), 1) % HEAD_DIM
    both = logs[0]
    for h in range(1, PAIRS):
        both = jnp.where(lane == h, logs[h], both)
    both = both.T
    return both[:8], both[HEAD_DIM : HEAD_DIM + 8]


def head_sums(att, datt):
    prod = (att.astype(F32) * datt.astype(F32)).astype(BF)
    shape = (16, D)
    row, feature = (lax.broadcasted_iota(jnp.int32, shape, n) for n in (0, 1))
    hit = feature // HEAD_DIM == row % 8 * 2 + row // 8
    return mm_nt(jnp.where(hit, 1.0, 0.0).astype(BF), prod)


def attend_pair_back(q2, k2, v2, do2, lse, inner, mask, bias):
    zero = jnp.zeros_like(q2)
    scaled = q2 * jnp.asarray(0.125, BF)

    def head(q, do, n):
        s = mm_nt(k2, q)
        if bias is not None:
            s = s + bias
        p = jnp.exp(s - lse[n])
        ds = p * (mm_nt(v2, do) - inner[n])
        return p.astype(BF), ds.astype(BF)

    qa, qb = jnp.where(mask, scaled, zero), jnp.where(mask, zero, scaled)
    da, db = jnp.where(mask, do2, zero), jnp.where(mask, zero, do2)
    ka, kb = jnp.where(mask, k2, zero), jnp.where(mask, zero, k2)
    pa, dsa = head(qa, da, 0)
    pb, dsb = head(qb, db, 1)
    dv2 = mm(pa, da) + mm(pb, db)
    dk2 = mm(dsa, qa) + mm(dsb, qb)
    if DQ_FORM == 0:
        dq2 = 0.125 * (mm_tn(dsa, ka) + mm_tn(dsb, kb))
    else:
        dq2 = 0.125 * (mm_tn(ka, dsa) + mm_tn(kb, dsb)).T
    return dq2, dk2, dv2


DQ_FORM = 1


NEAR = 4


def pieces(stripes, rows, chunks):
    part = rows // chunks
    out = [(j, 0, rows) for j in range(NEAR)]
    for c in range(chunks):
        out += [(j, c * part, (c + 1) * part) for j in range(NEAR, stripes)]
    return out


def chunk_of(blocks, stripes, c):
    far = stripes - NEAR
    return list(blocks[:NEAR]) + list(blocks[NEAR + c * far : NEAR + (c + 1) * far])


def space_forward_kernel(stripes, chunks, *refs):
    x_refs = refs[:stripes]
    mod_ref, w_ref = refs[stripes : stripes + 2]
    att_refs = refs[stripes + 2 : -4]
    n1_ref, qkv_ref, att_ref, lse_ref = refs[-4:]
    rows = x_refs[0].shape[1]
    part = rows // chunks
    for j in range(stripes):
        x = x_refs[j][0].astype(F32)
        xhat, _ = norm_stats(x)
        n1_ref[0, j * rows : (j + 1) * rows, :] = (
            xhat * (1.0 + mod_ref[0, 1:2, :]) + mod_ref[0, 0:1, :]
        ).astype(BF)
    for s in range(3):
        qkv_ref[0, :, s * D : (s + 1) * D] = mm(
            n1_ref[0], w_ref[:, s * D : (s + 1) * D]
        ).astype(BF)
    mask = first_head()
    logs = []
    for h in range(PAIRS):
        q2, k2, v2 = (
            qkv_ref[0, :, s * D + h * 128 : s * D + (h + 1) * 128] for s in range(3)
        )
        att, log = attend_pair(q2, k2, v2, mask, None)
        logs.append(log)
        att = att.astype(BF)
        att_ref[0, :, h * 128 : (h + 1) * 128] = att
        for out, (j, low, high) in zip(att_refs, pieces(stripes, rows, chunks)):
            out[0, :, h * 128 : (h + 1) * 128] = att[j * rows + low : j * rows + high]
    lse_ref[0, 0:8, :], lse_ref[0, 8:16, :] = pair_rows(logs)


def space_forward(blocks, mod_own, weight, chunks):
    stripes = len(blocks)
    frames, rows, _ = blocks[0].shape
    whole = rows * stripes
    sizes = [high - low for _, low, high in pieces(stripes, rows, chunks)] + [whole]
    outs = call(
        partial(space_forward_kernel, stripes, chunks),
        (*blocks, mod_own, weight),
        [pl.BlockSpec((1, rows, D), lambda f: (f, 0, 0))] * stripes
        + [
            pl.BlockSpec((1,) + mod_own.shape[1:], lambda f: (f, 0, 0)),
            pl.BlockSpec(weight.shape, lambda f: (0, 0)),
        ],
        grid=(frames,),
        out_specs=[pl.BlockSpec((1, n, D), lambda f: (f, 0, 0)) for n in sizes]
        + [
            pl.BlockSpec((1, whole, 3 * D), lambda f: (f, 0, 0)),
            pl.BlockSpec((1, whole, D), lambda f: (f, 0, 0)),
            pl.BlockSpec((1, 16, whole), lambda f: (f, 0, 0)),
        ],
        out_shape=[jax.ShapeDtypeStruct((frames, n, D), BF) for n in sizes]
        + [
            jax.ShapeDtypeStruct((frames, whole, 3 * D), BF),
            jax.ShapeDtypeStruct((frames, whole, D), BF),
            jax.ShapeDtypeStruct((frames, 16, whole), F32),
        ],
        name="space_forward",
    )
    return outs[:-4], outs[-4], outs[-3:]


def space_backward_kernel(stripes, rows, chunks, *refs):
    place = pieces(stripes, rows, chunks)
    d_refs, refs = refs[: len(place)], refs[len(place) :]
    sum_refs, refs = refs[:stripes], refs[stripes:]
    core_ref, qkv_ref, att_ref, lse_ref, dqkv_ref, keep_ref, send_ref, late_ref, datt_ref = refs
    for d_ref, (j, low, high) in zip(d_refs, place):
        datt_ref[j * rows + low : j * rows + high, :] = d_ref[...]

    @pl.when(pl.program_id(0) == 0)
    def _():
        late = sum_refs[0][...].astype(F32)
        for r in sum_refs[1:]:
            late = late + r[...].astype(F32)
        late_ref[...] = late

    mask = first_head()
    inner = head_sums(att_ref[0], datt_ref[...])
    for h in range(PAIRS):
        q2, k2, v2 = (
            qkv_ref[0, :, s * D + h * 128 : s * D + (h + 1) * 128] for s in range(3)
        )
        do2 = datt_ref[:, h * 128 : (h + 1) * 128]
        lse = [lse_ref[0, n : n + 1, :] for n in (h, 8 + h)]
        sums = [inner[n : n + 1] for n in (h, 8 + h)]
        grads = attend_pair_back(q2, k2, v2, do2, lse, sums, mask, None)
        for s in range(3):
            dqkv_ref[0, :, s * D + h * 128 : s * D + (h + 1) * 128] = grads[s].astype(BF)
    half = dqkv_ref.shape[-1] // 2
    for ref, side in ((keep_ref, core_ref[0]), (send_ref, 1 - core_ref[0])):
        ref[...] = dqkv_ref[0, :, pl.ds(pl.multiple_of(side * half, half), half)]


def space_backward(core, grads, kept, stripes, chunks, deps):
    frames, whole, _ = kept[0].shape
    rows = whole // stripes
    extra = frames * 8
    place = pieces(stripes, rows, chunks)
    last = list(grads[:NEAR]) + list(grads[NEAR - stripes :])
    half = pl.BlockSpec((whole, 3 * D // 2), lambda f: (f, 0))
    return call(
        partial(space_backward_kernel, stripes, rows, chunks),
        (*grads, *last, core, *kept),
        [pl.BlockSpec((high - low, D), lambda f: (f, 0)) for _, low, high in place]
        + [
            pl.BlockSpec((extra, D), lambda f, n=g.shape[0] // extra - 1: (n, 0)) for g in last
        ]
        + [
            pl.BlockSpec(memory_space=pltpu.SMEM),
            pl.BlockSpec((1, whole, 3 * D), lambda f: (f, 0, 0)),
            pl.BlockSpec((1, whole, D), lambda f: (f, 0, 0)),
            pl.BlockSpec((1, 16, whole), lambda f: (f, 0, 0)),
        ],
        deps,
        grid=(frames,),
        out_specs=[
            pl.BlockSpec((1, whole, 3 * D), lambda f: (f, 0, 0)),
            half,
            half,
            pl.BlockSpec((extra, D), lambda f: (0, 0)),
        ],
        out_shape=[
            jax.ShapeDtypeStruct((frames, whole, 3 * D), BF),
            jax.ShapeDtypeStruct((frames * whole, 3 * D // 2), BF),
            jax.ShapeDtypeStruct((frames * whole, 3 * D // 2), BF),
            jax.ShapeDtypeStruct((extra, D), F32),
        ],
        scratch_shapes=[pltpu.VMEM((whole, D), BF)],
        name="space_backward",
    )


def space_norm_kernel(stripes, *refs):
    x_refs, (mod_ref, w_ref, dqkv_ref), refs = refs[:stripes], refs[stripes : stripes + 3], refs[stripes + 3 :]
    dv_refs, dmod_ref, dn_ref = refs[:stripes], refs[stripes], refs[stripes + 1]
    rows = x_refs[0].shape[1]
    dn_ref[...] = mm_nt(dqkv_ref[0], w_ref[...])
    shift_sum = jnp.zeros((1, D), F32)
    scale_sum = jnp.zeros((1, D), F32)
    for j in range(stripes):
        xhat, rstd = norm_stats(x_refs[j][0].astype(F32))
        d = dn_ref[j * rows : (j + 1) * rows, :]
        dv_refs[j][0] = norm_back(d, xhat, rstd, mod_ref[0, 1:2, :]).astype(BF)
        shift_sum = shift_sum + jnp.sum(d, 0, keepdims=True)
        scale_sum = scale_sum + jnp.sum(d * xhat, 0, keepdims=True)
    dmod_ref[0, 0:1, :] = shift_sum
    dmod_ref[0, 1:2, :] = scale_sum


def space_norm(blocks, mod_own, weight, dqkv, deps):
    stripes = len(blocks)
    frames, rows, _ = blocks[0].shape
    whole = rows * stripes
    block = pl.BlockSpec((1, rows, D), lambda f: (f, 0, 0))
    outs = call(
        partial(space_norm_kernel, stripes),
        (*blocks, mod_own, weight, dqkv),
        [block] * stripes
        + [
            pl.BlockSpec((1,) + mod_own.shape[1:], lambda f: (f, 0, 0)),
            pl.BlockSpec(weight.shape, lambda f: (0, 0)),
            pl.BlockSpec((1, whole, 3 * D), lambda f: (f, 0, 0)),
        ],
        deps,
        grid=(frames,),
        out_specs=[block] * stripes + [pl.BlockSpec((1, 2, D), lambda f: (f, 0, 0))],
        out_shape=[jax.ShapeDtypeStruct((frames, rows, D), BF)] * stripes
        + [jax.ShapeDtypeStruct((frames, 2, D), F32)],
        scratch_shapes=[pltpu.VMEM((whole, D), F32)],
        name="space_norm",
    )
    return outs[:-1], outs[-1]


STEP = 4


def spots(i, g, rows_g):
    fs = pl.ds(i * STEP, STEP)
    at = pl.ds(pl.multiple_of(g * rows_g + i * STEP * 8, STEP * 8), STEP * 8)
    return fs, at


def as3(x):
    return x.reshape(STEP, 8, D)


def as2(x):
    return x.reshape(STEP * 8, D)


def over_patches(terms):
    total = terms[0]
    for t in terms[1:]:
        total = total + t
    return jnp.sum(total, 1, keepdims=True)


def bring(source, target, sem):
    copy = pltpu.make_async_copy(source, target, sem)
    copy.start()
    return copy


def onward_kernel(stripes, chunk, *refs):
    me_ref, bias_ref, mod_ref = refs[:3]
    a_refs = refs[3 : 3 + stripes]
    tok_ref, cot_ref = refs[3 + stripes : 5 + stripes]
    weight_refs = refs[5 + stripes : 10 + stripes]
    (
        mixed_ref,
        dmod_ref,
        lse_ref,
        att1_out,
        n2_out,
        att2_out,
        n3_out,
        dup_out,
        hid_out,
        db3_out,
        db2_out,
        first_out,
        b1_out,
        dsecond_out,
        qkv_out,
    ) = refs[10 + stripes : 25 + stripes]
    (
        wos,
        wqkv,
        wot,
        wu,
        wd,
        att1_ref,
        n2_ref,
        att2_ref,
        n3_ref,
        dup_ref,
        hid_ref,
        db3_ref,
        db2_ref,
        first_ref,
        b1_ref,
        second_ref,
        qkv_ref,
        nat_ref,
        b2_ref,
        b3_ref,
        dn_ref,
        in_sems,
        out_sems,
    ) = refs[25 + stripes :]
    frames, patches, _ = tok_ref.shape
    groups = patches // 8
    rows = frames * patches
    rows_g = frames * 8
    per = frames // stripes
    ff = wu.shape[1]
    me = me_ref[0]
    mask = first_head()
    held = (wos, wqkv, wot, wu, wd)
    loads = [bring(w, v, in_sems.at[n]) for n, (w, v) in enumerate(zip(weight_refs, held))]
    stores = []

    def send(source, target):
        stores.append(bring(source, target, out_sems.at[len(stores)]))

    for j in range(stripes):
        s = lax.bitwise_xor(me, j)
        start = pl.multiple_of(s * (per * patches), per * patches)
        low = chunk * patches if a_refs[j].shape[1] > patches else 0
        att1_ref[pl.ds(start, per * patches), :] = a_refs[j][:, low : low + patches, :].reshape(
            per * patches, D
        )
    send(att1_ref, att1_out)
    loads[0].wait()
    nat_ref[...] = mm(att1_ref[...], wos[...]).reshape(frames, patches, D)

    def stage_one(i, carry):
        for g in range(groups):
            fs, at = spots(i, g, rows_g)
            tok = tok_ref[fs].astype(F32)[:, 8 * g : 8 * g + 8]
            b1 = nat_ref[fs, 8 * g : 8 * g + 8, :]
            first = tok + mod_ref[fs, 2:3, :] * b1
            xhat, _ = norm_stats(first)
            n2 = xhat * (1.0 + mod_ref[fs, 4:5, :]) + mod_ref[fs, 3:4, :]
            b1_ref[at, :] = as2(b1)
            first_ref[at, :] = as2(first)
            n2_ref[at, :] = as2(n2).astype(BF)
        return carry

    lax.fori_loop(0, frames // STEP, stage_one, 0, unroll=8)
    send(b1_ref, b1_out)
    send(first_ref, first_out)
    send(n2_ref, n2_out)

    loads[1].wait()
    for s in range(3):
        qkv_ref[:, s * D : (s + 1) * D] = mm(n2_ref[...], wqkv[:, s * D : (s + 1) * D]).astype(BF)
    send(qkv_ref, qkv_out)

    def time_attend(g, carry):
        at = pl.ds(pl.multiple_of(g * rows_g, rows_g), rows_g)
        logs = []
        for h in range(PAIRS):
            q2, k2, v2 = (
                qkv_ref[at, s * D + h * 128 : s * D + (h + 1) * 128] for s in range(3)
            )
            att, log = attend_pair(q2, k2, v2, mask, bias_ref[...])
            logs.append(log)
            att2_ref[at, h * 128 : (h + 1) * 128] = att.astype(BF)
        lse_ref[g, 0:8, :], lse_ref[g, 8:16, :] = pair_rows(logs)
        return carry

    lax.fori_loop(0, groups, time_attend, 0)
    send(att2_ref, att2_out)
    loads[2].wait()
    b2_ref[...] = mm(att2_ref[...], wot[...])

    def stage_two(i, carry):
        for g in range(groups):
            fs, at = spots(i, g, rows_g)
            second = as3(first_ref[at, :]) + mod_ref[fs, 5:6, :] * as3(b2_ref[at, :])
            xhat, _ = norm_stats(second)
            n3 = xhat * (1.0 + mod_ref[fs, 7:8, :]) + mod_ref[fs, 6:7, :]
            cot = cot_ref[fs].astype(F32)[:, 8 * g : 8 * g + 8]
            second_ref[at, :] = as2(second)
            n3_ref[at, :] = as2(n3).astype(BF)
            db3_ref[at, :] = as2(mod_ref[fs, 8:9, :] * cot).astype(BF)
        return carry

    lax.fori_loop(0, frames // STEP, stage_two, 0, unroll=8)
    send(n3_ref, n3_out)
    send(db3_ref, db3_out)

    loads[3].wait()
    loads[4].wait()
    b3_ref[...] = jnp.zeros_like(b3_ref)
    dn_ref[...] = jnp.zeros_like(dn_ref)
    wide = FEED_COLS
    part = FEED_ROWS

    def feed(b, carry):
        cols = pl.ds(pl.multiple_of(b * wide, wide), wide)
        for r in range(rows // part):
            at = pl.ds(r * part, part)
            u = mm(n3_ref[at, :], wu[:, cols])
            dh = mm_nt(db3_ref[at, :], wd[cols, :])
            u2 = u * u
            t = jnp.tanh(u * (GELU_C + (GELU_C * GELU_A) * u2))
            half = 0.5 + 0.5 * t
            slope = half + (0.5 * u) * ((1.0 - t * t) * (GELU_C + (3.0 * GELU_C * GELU_A) * u2))
            hid = (u * half).astype(BF)
            dup = (dh * slope).astype(BF)
            hid_ref[at, cols] = hid
            dup_ref[at, cols] = dup
            b3_ref[at, :] += mm(hid, wd[cols, :])
            dn_ref[at, :] += mm_nt(dup, wu[:, cols])
        return carry

    lax.fori_loop(0, ff // wide, feed, 0)
    send(hid_ref, hid_out)
    send(dup_ref, dup_out)

    def stage_three(i, carry):
        parts = [[] for _ in range(4)]
        for g in range(groups):
            fs, at = spots(i, g, rows_g)
            cot = cot_ref[fs].astype(F32)[:, 8 * g : 8 * g + 8]
            second = as3(second_ref[at, :])
            b3 = as3(b3_ref[at, :])
            dn = as3(dn_ref[at, :])
            xhat, rstd = norm_stats(second)
            dsecond = cot + norm_back(dn, xhat, rstd, mod_ref[fs, 7:8, :])
            nat_ref[fs, 8 * g : 8 * g + 8, :] = second + mod_ref[fs, 8:9, :] * b3
            second_ref[at, :] = as2(dsecond)
            db2_ref[at, :] = as2(mod_ref[fs, 5:6, :] * dsecond).astype(BF)
            for k, t in enumerate((dsecond * as3(b2_ref[at, :]), dn, dn * xhat, cot * b3)):
                parts[k].append(t)
        fs, _ = spots(i, 0, rows_g)
        for k in range(4):
            dmod_ref[fs, k : k + 1, :] = over_patches(parts[k])
        mixed_ref[fs] = nat_ref[fs].astype(BF)
        return carry

    lax.fori_loop(0, frames // STEP, stage_three, 0, unroll=8)
    send(second_ref, dsecond_out)
    send(db2_ref, db2_out)
    for copy in stores:
        copy.wait()


FEED_COLS = 1536
FEED_ROWS = 256


def onward(me, bias, modulation, attended, tokens, cotangent, weights, chunk=0, deps=()):
    stripes = len(attended)
    frames, patches, _ = tokens.shape
    rows = frames * patches
    ff = weights[3].shape[1]
    vmem, anywhere = pl.BlockSpec(memory_space=pltpu.VMEM), pl.BlockSpec(memory_space=pl.ANY)
    kept = [(D, BF), (D, BF), (D, BF), (D, BF), (ff, BF), (ff, BF), (D, BF), (D, BF)]
    kept += [(D, F32), (D, F32), (D, F32), (3 * D, BF)]
    outs = call(
        partial(onward_kernel, stripes, chunk),
        (me, bias, modulation, *attended, tokens, cotangent, *weights),
        [pl.BlockSpec(memory_space=pltpu.SMEM)] + [vmem] * (4 + stripes) + [anywhere] * 5,
        deps,
        out_specs=[vmem] * 3 + [anywhere] * len(kept),
        out_shape=[
            jax.ShapeDtypeStruct((frames, patches, D), BF),
            jax.ShapeDtypeStruct((frames, 4, D), F32),
            jax.ShapeDtypeStruct((patches // 8, 16, frames * 8), F32),
        ]
        + [jax.ShapeDtypeStruct((rows, cols), kind) for cols, kind in kept],
        scratch_shapes=[pltpu.VMEM(w.shape, BF) for w in weights]
        + [pltpu.VMEM((rows, cols), kind) for cols, kind in kept]
        + [pltpu.VMEM((frames, patches, D), F32)]
        + [pltpu.VMEM((rows, D), F32)] * 3
        + [pltpu.SemaphoreType.DMA((5,)), pltpu.SemaphoreType.DMA((len(kept),))],
        name="onward",
    )
    names = ("mixed", "dmod", "lse", "att1", "n2", "att2", "n3", "dup", "hid", "db3")
    names += ("db2", "first", "b1", "dsecond", "qkv")
    return dict(zip(names, outs))


def time_back_kernel(stripes, frames, last, *refs):
    me_ref, bias_ref, mod_ref, qkv_ref, db2_ref, att2_ref, lse_ref = refs[:7]
    late_ins, weight_refs = refs[7:10], refs[10:13]
    others = refs[13 : 13 + (NEAR + 3 if last else 0)]
    refs = refs[13 + len(others) :]
    dfirst_ref, dmod_ref = refs[:2]
    datt_refs = refs[2 : 2 + stripes]
    dqkv_out, db1_out = refs[2 + stripes : 4 + stripes]
    (
        first_ref,
        b1_ref,
        dsecond_ref,
        wqkv,
        wot,
        wos,
        dqkv_ref,
        db1_ref,
        nat_ref,
        dn_ref,
        do_ref,
        sums_ref,
        in_sems,
        out_sems,
    ) = refs[4 + stripes :]
    patches = nat_ref.shape[1]
    groups = patches // 8
    rows_g = frames * 8
    per = frames // stripes
    me = me_ref[0]
    mask = first_head()
    held = (wot, wqkv, first_ref, b1_ref, dsecond_ref, wos)
    sources = (weight_refs[1], weight_refs[0]) + tuple(late_ins) + (weight_refs[2],)
    loads = [bring(w, v, in_sems.at[n]) for n, (w, v) in enumerate(zip(sources, held))]
    loads[0].wait()
    do_ref[...] = mm_nt(db2_ref[...], wot[...]).astype(BF)

    def attend_back(g, carry):
        at = pl.ds(pl.multiple_of(g * rows_g, rows_g), rows_g)
        inner = head_sums(att2_ref[at, :], do_ref[at, :])
        for h in range(PAIRS):
            q2, k2, v2 = (
                qkv_ref[at, s * D + h * 128 : s * D + (h + 1) * 128] for s in range(3)
            )
            do2 = do_ref[at, h * 128 : (h + 1) * 128]
            lse = [lse_ref[g, n : n + 1, :] for n in (h, 8 + h)]
            sums = [inner[n : n + 1] for n in (h, 8 + h)]
            grads = attend_pair_back(q2, k2, v2, do2, lse, sums, mask, bias_ref[...])
            for s in range(3):
                dqkv_ref[at, s * D + h * 128 : s * D + (h + 1) * 128] = grads[s].astype(BF)
        return carry

    lax.fori_loop(0, groups, attend_back, 0)
    stores = [bring(dqkv_ref, dqkv_out, out_sems.at[0])]
    for copy in loads[1:]:
        copy.wait()
    dn_ref[...] = mm_nt(dqkv_ref[...], wqkv[...])

    def stage_four(i, carry):
        parts = [[] for _ in range(3)]
        for g in range(groups):
            fs, at = spots(i, g, rows_g)
            dn = as3(dn_ref[at, :])
            xhat, rstd = norm_stats(as3(first_ref[at, :]))
            dfirst = as3(dsecond_ref[at, :]) + norm_back(dn, xhat, rstd, mod_ref[fs, 4:5, :])
            nat_ref[fs, 8 * g : 8 * g + 8, :] = dfirst
            for k, t in enumerate((dfirst * as3(b1_ref[at, :]), dn, dn * xhat)):
                parts[k].append(t)
        fs, _ = spots(i, 0, rows_g)
        for k in range(3):
            dmod_ref[fs, k : k + 1, :] = over_patches(parts[k])
        dfirst = nat_ref[fs]
        dfirst_ref[fs] = dfirst.astype(BF)
        span = STEP * patches
        db1_ref[pl.ds(pl.multiple_of(i * span, span), span), :] = (
            (mod_ref[fs, 2:3, :] * dfirst).astype(BF).reshape(span, D)
        )
        return carry

    lax.fori_loop(0, frames // STEP, stage_four, 0, unroll=8)
    stores.append(bring(db1_ref, db1_out, out_sems.at[1]))
    nat_ref[...] = mm_nt(db1_ref[...], wos[...]).reshape(frames, patches, D)
    if last:
        back, one, two = others[NEAR:]
        sums_ref[:, 0:3, :] = dmod_ref[...] + back[...]
        sums_ref[:, 3:7, :] = one[...] + two[...]
        sums_ref[:, 7:8, :] = jnp.zeros((frames, 1, D), F32)
    for j in range(stripes):
        s = lax.bitwise_xor(me, j)
        mine = nat_ref[pl.ds(s * per, per)].astype(BF)
        if last:
            width = patches
            if j < NEAR:
                width = 2 * patches
                for f in range(per):
                    datt_refs[j][f * width : f * width + patches, :] = others[j][
                        f * patches : (f + 1) * patches, :
                    ]
                    datt_refs[j][f * width + patches : (f + 1) * width, :] = mine[f]
            else:
                datt_refs[j][: per * patches, :] = mine.reshape(per * patches, D)
            datt_refs[j][per * width :, :] = sums_ref[pl.ds(s * per, per)].reshape(
                per * 8, D
            ).astype(BF)
        else:
            datt_refs[j][...] = mine.reshape(per * patches, D)
    for copy in stores:
        copy.wait()


def time_back(me, bias, modulation, onward_outs, weights, stripes, others=(), deps=()):
    o = onward_outs
    frames, patches, _ = o["mixed"].shape
    rows = frames * patches
    per = frames // stripes
    last = bool(others)
    vmem, anywhere = pl.BlockSpec(memory_space=pltpu.VMEM), pl.BlockSpec(memory_space=pl.ANY)
    bf = lambda *shape: jax.ShapeDtypeStruct(shape, BF)
    sends = [
        bf(per * (patches * (2 if j < NEAR else 1) + 8) if last else per * patches, D)
        for j in range(stripes)
    ]
    outs = call(
        partial(time_back_kernel, stripes, frames, last),
        (me, bias, modulation, o["qkv"], o["db2"], o["att2"], o["lse"], o["first"], o["b1"])
        + (o["dsecond"], *weights, *others),
        [pl.BlockSpec(memory_space=pltpu.SMEM)] + [vmem] * 6 + [anywhere] * 6 + [vmem] * len(others),
        deps,
        out_specs=[vmem] * (2 + stripes) + [anywhere] * 2,
        out_shape=[bf(frames, patches, D), jax.ShapeDtypeStruct((frames, 3, D), F32)]
        + sends
        + [bf(rows, 3 * D), bf(rows, D)],
        scratch_shapes=[pltpu.VMEM((rows, D), F32)] * 3
        + [pltpu.VMEM(w.shape, BF) for w in weights]
        + [
            pltpu.VMEM((rows, 3 * D), BF),
            pltpu.VMEM((rows, D), BF),
            pltpu.VMEM((frames, patches, D), F32),
            pltpu.VMEM((rows, D), F32),
            pltpu.VMEM((rows, D), BF),
            pltpu.VMEM((frames, 8, D), F32),
            pltpu.SemaphoreType.DMA((6,)),
            pltpu.SemaphoreType.DMA((2,)),
        ],
        name="time_back",
    )
    return dict(
        dfirst=outs[0], dmod_back=outs[1], sends=outs[2 : 2 + stripes], dqkv=outs[-2], db1=outs[-1]
    )


def finish_kernel(stripes, chunks, me_ref, *refs):
    dv_refs = refs[:stripes]
    first_refs = refs[stripes : stripes + chunks]
    out_ref = refs[-1]
    per = dv_refs[0].shape[0]
    part = first_refs[0].shape[1]
    for j in range(stripes):
        fs = pl.ds(lax.bitwise_xor(me_ref[0], j) * per, per)
        for c in range(chunks):
            spot = pl.ds(c * part, part)
            out_ref[fs, spot, :] = (
                dv_refs[j][:, spot, :].astype(F32) + first_refs[c][fs].astype(F32)
            ).astype(BF)


def finish(me, dvs, firsts, deps=()):
    stripes, chunks = len(dvs), len(firsts)
    frames, part, _ = firsts[0].shape
    vmem = pl.BlockSpec(memory_space=pltpu.VMEM)
    return call(
        partial(finish_kernel, stripes, chunks),
        (me, *dvs, *firsts),
        [pl.BlockSpec(memory_space=pltpu.SMEM)] + [vmem] * (stripes + chunks),
        deps,
        out_specs=vmem,
        out_shape=jax.ShapeDtypeStruct((frames, part * chunks, D), BF),
        name="finish",
    )


def flip(x, axis, bit):
    size = lax.axis_size(axis)
    return lax.ppermute(x, axis, [(i, i ^ bit) for i in range(size)])


def exchange(blocks):
    return [blocks[0]] + [flip(blocks[j], "blk", j) for j in range(1, len(blocks))]


def double(x, axis, bit, dim):
    own = (lax.axis_index(axis) // bit) % 2
    got = flip(x, axis, bit)
    low = jnp.where(own == 0, x, got)
    high = jnp.where(own == 0, got, x)
    return jnp.concatenate([low, high], dim)


def bits_of(size):
    return [1 << b for b in range(size.bit_length() - 1)]


def weight_grad_kernel(pairs, by_rows, aliased, bit_ref, *refs):
    a_refs, b_refs = refs[:pairs], refs[pairs : 2 * pairs]
    keep_ref, *send_refs, total_ref = refs[2 * pairs + (2 if aliased else 0) :]
    total = mm_tn(a_refs[0][...], b_refs[0][...])
    for a, b in zip(a_refs[1:], b_refs[1:]):
        total = total + mm_tn(a[...], b[...])
    total_ref[...] = total.reshape(total_ref.shape)
    bit = bit_ref[0]
    if by_rows:
        keep_ref[...] = total_ref[:, :, bit].astype(BF)
        send_refs[0][...] = total_ref[:, :, 1 - bit].astype(BF)
    else:
        keep_ref[:, 0] = total_ref[:, bit].astype(BF)
        deep = send_refs[0].shape[0]
        for n, send_ref in enumerate(send_refs):
            send_ref[:, 0] = total_ref[n * deep : (n + 1) * deep, 1 - bit].astype(BF)


def weight_grad(bit, firsts, seconds, stripes, units, at, held, deps=(), cuts=1):
    pairs = len(firsts)
    rows, cols = firsts[0].shape[1], seconds[0].shape[1]
    small = D // stripes
    half = small // 2
    by_rows = rows > D
    tall = D if cols % D == 0 else D // 2
    steps = rows // D if by_rows else cols // tall
    if by_rows:
        deep = rows // D
        wide = stripes // steps
        shape, spot = (wide, deep, half, D), lambda t: (t, at // deep, 0, 0)
        total = (wide, deep, 2, half, D)
    else:
        shape, spot = (stripes, 1, half, tall), lambda t: (0, at + t, 0, 0)
        total = (stripes, 2, half, tall)
    moving, still = (lambda t: (0, t)), (lambda t: (0, 0))
    block = pl.BlockSpec(shape, spot)
    send = pl.BlockSpec((shape[0] // cuts,) + shape[1:], spot)
    group = [jax.ShapeDtypeStruct((stripes, units, half, tall), BF)]
    group += [jax.ShapeDtypeStruct((stripes // cuts, units, half, tall), BF)] * cuts
    aliased = held is not None
    return call(
        partial(weight_grad_kernel, pairs, by_rows, aliased),
        (bit, *firsts, *seconds, *(held or ())),
        [pl.BlockSpec(memory_space=pltpu.SMEM)]
        + [pl.BlockSpec((a.shape[0], D), moving if by_rows else still) for a in firsts]
        + [pl.BlockSpec((b.shape[0], tall), still if by_rows else moving) for b in seconds]
        + [ANYWHERE] * (2 if aliased else 0),
        deps,
        grid=(steps,),
        out_specs=[block] + [send] * cuts,
        scratch_shapes=[pltpu.VMEM(total, F32)],
        out_shape=group,
        input_output_aliases={2 * pairs + 1: 0, 2 * pairs + 2: 1} if aliased else {},
        name="weight_grad",
    )


def mod_grad_kernel(samples, *refs):
    g_refs, refs = refs[:samples], refs[samples:]
    w_ref, cond_ref, slope_ref, hit_ref, gw_ref, gb_ref, table_ref, total_ref = refs
    g = jnp.concatenate([r[...] for r in g_refs], 0)
    gw_ref[...] = mm_tn(cond_ref[...], g)
    gb_ref[0] = jnp.sum(g.astype(F32), 0, keepdims=True)
    part = mm_nt(g, w_ref[...])

    @pl.when(pl.program_id(0) == 0)
    def _():
        total_ref[...] = part

    @pl.when(pl.program_id(0) > 0)
    def _():
        total_ref[...] += part

    @pl.when(pl.program_id(0) == pl.num_programs(0) - 1)
    def _():
        e = total_ref[...] * slope_ref[...]
        high = e.astype(BF)
        low = (e - high.astype(F32)).astype(BF)
        table_ref[...] = mm(hit_ref[...], high) + mm(hit_ref[...], low)


def pack_kernel(first_ref, late_ref, out_ref):
    frames = first_ref.shape[0]
    for f in range(frames):
        both = [first_ref[f], late_ref[8 * f : 8 * f + 7, :]]
        out_ref[f] = jnp.concatenate(both, 0).astype(BF)


def pack(first_sums, late, deps):
    vmem = pl.BlockSpec(memory_space=pltpu.VMEM)
    frames = first_sums.shape[0]
    return call(
        pack_kernel,
        (first_sums, late),
        [vmem, vmem],
        deps,
        out_specs=vmem,
        out_shape=jax.ShapeDtypeStruct((frames, 9, D), BF),
        name="pack",
    )


def mod_grads(gs, weight, cond_own, slope, hit_own, deps):
    rows = slope.shape[0]
    still = lambda k: (0, 0)
    steps = weight.shape[1] // D
    wide, span = cond_own.shape[1], hit_own.shape[0]
    return call(
        partial(mod_grad_kernel, len(gs)),
        (*gs, weight, cond_own, slope, hit_own),
        [pl.BlockSpec((g.shape[0], D), lambda k: (0, k)) for g in gs]
        + [
            pl.BlockSpec((D, D), lambda k: (0, k)),
            pl.BlockSpec((rows, wide), still),
            pl.BlockSpec((rows, D), still),
            pl.BlockSpec((span, rows), still),
        ],
        deps,
        grid=(steps,),
        out_specs=[
            pl.BlockSpec((wide, D), lambda k: (0, k)),
            pl.BlockSpec((1, 1, D), lambda k: (k, 0, 0)),
            pl.BlockSpec((span, D), still),
        ],
        out_shape=[
            jax.ShapeDtypeStruct((wide, steps * D), F32),
            jax.ShapeDtypeStruct((steps, 1, D), F32),
            jax.ShapeDtypeStruct((span, D), F32),
        ],
        scratch_shapes=[pltpu.VMEM((rows, D), F32)],
        name="mod_grads",
    )


def of_samples(x):
    size = lax.axis_size("dp")
    if size == 4:
        return [x] + [flip(x, "dp", j) for j in (1, 2, 3)]
    return [lax.all_gather(x, "dp", tiled=True)]


def add_split_kernel(cut, parts, bit_ref, keep_ref, *refs):
    got_refs, outs = refs[:parts], refs[parts:]
    bit = bit_ref[0]
    for out, side in zip(outs, (bit, 1 - bit)):
        if cut == "stripe":
            spot = (0, side)
        else:
            half = keep_ref.shape[-1] // 2
            spot = (0, slice(None), slice(None), pl.ds(pl.multiple_of(side * half, half), half))
        got = got_refs[0][spot].astype(F32)
        if parts == 2:
            low = pl.program_id(0) < pl.num_programs(0) // 2
            got = jnp.where(low, got, got_refs[1][spot].astype(F32))
        out[0] = (keep_ref[spot].astype(F32) + got).astype(BF)


def add_split(bit, keep, got, cut, deps=()):
    count, units, rows, cols = keep.shape
    parts = len(got)
    if cut == "stripe":
        steps = count // 2
        keep, *got = (x.reshape(steps, 2, units, rows, cols) for x in (keep, *got))
        out = (steps, units, rows, cols)
        in_spec = pl.BlockSpec((1, 2, units, rows, cols), lambda i: (i, 0, 0, 0, 0))
        got_specs = [in_spec]
        out_block = pl.BlockSpec((1, units, rows, cols), lambda i: (i, 0, 0, 0))
    else:
        steps = count
        out = (count, units, rows, cols // 2)
        shape = (1, units, rows, cols)
        in_spec = pl.BlockSpec(shape, lambda i: (i, 0, 0, 0))
        got_specs = [in_spec]
        if parts == 2:
            half = steps // 2
            got_specs = [
                pl.BlockSpec(shape, lambda i: (jnp.minimum(i, half - 1), 0, 0, 0)),
                pl.BlockSpec(shape, lambda i: (jnp.maximum(i - half, 0), 0, 0, 0)),
            ]
        out_block = pl.BlockSpec((1, units, rows, cols // 2), lambda i: (i, 0, 0, 0))
    return call(
        partial(add_split_kernel, cut, parts),
        (bit, keep, *got),
        [pl.BlockSpec(memory_space=pltpu.SMEM), in_spec, *got_specs],
        deps,
        grid=(steps,),
        out_specs=[out_block] * 2,
        out_shape=[jax.ShapeDtypeStruct(out, BF)] * 2,
        name="add_split",
    )


def assemble_kernel(layout, at_ref, *refs):
    shares, outs = refs[:4], refs[4:]
    half, cols = shares[0].shape[1:]
    for j in range(4):
        place = lax.bitwise_xor(at_ref[0], j)
        unit = 0
        for out, (deep, wide, halved) in zip(outs, layout):
            core, side = lax.rem(place, 2), lax.div(place, 2)
            if halved:
                core, side = side, core
            low = pl.multiple_of(core * half, half)
            step = cols if halved else 2 * cols
            left = pl.multiple_of(side * (wide * cols if halved else cols), cols)
            for r in range(deep):
                for c in range(wide):
                    out[pl.ds(r * 2 * half + low, half), pl.ds(c * step + left, cols)] = shares[j][
                        unit
                    ].astype(F32)
                    unit += 1


def assemble(at, shares, layout):
    _, half, cols = shares[0].shape
    vmem = pl.BlockSpec(memory_space=pltpu.VMEM)
    return call(
        partial(assemble_kernel, layout),
        (at, *shares),
        [pl.BlockSpec(memory_space=pltpu.SMEM)] + [vmem] * 4,
        out_specs=[vmem] * len(layout),
        out_shape=[
            jax.ShapeDtypeStruct((deep * 2 * half, wide * 2 * cols), F32)
            for deep, wide, _ in layout
        ],
        name="assemble",
    )


def bit_of(axis, bit):
    return ((lax.axis_index(axis) // bit) % 2).astype(jnp.int32).reshape(1)


def add_deal_kernel(groups, at_ref, *refs):
    keeps, gots, outs = refs[:groups], refs[groups : 2 * groups], refs[2 * groups :]
    for j, out in enumerate(outs):
        s = lax.bitwise_xor(at_ref[0], j)
        unit = 0
        for keep, got in zip(keeps, gots):
            n = keep.shape[1]
            out[unit : unit + n] = (keep[s].astype(F32) + got[s].astype(F32)).astype(BF)
            unit += n


def add_deal(at, keeps, gots, deps):
    vmem = pl.BlockSpec(memory_space=pltpu.VMEM)
    places, _, half, cols = keeps[0].shape
    units = sum(k.shape[1] for k in keeps)
    return call(
        partial(add_deal_kernel, len(keeps)),
        (at, *keeps, *gots),
        [pl.BlockSpec(memory_space=pltpu.SMEM)] + [vmem] * (2 * len(keeps)),
        deps,
        out_specs=[vmem] * places,
        out_shape=[jax.ShapeDtypeStruct((units, half, cols), BF)] * places,
        name="add_deal",
    )


def add_many_kernel(*refs):
    total = refs[0][...].astype(F32)
    for r in refs[1:-1]:
        total = total + r[...].astype(F32)
    refs[-1][...] = total.astype(BF)


def add_many(arrays, deps):
    vmem = pl.BlockSpec(memory_space=pltpu.VMEM)
    return call(
        add_many_kernel,
        tuple(arrays),
        [vmem] * len(arrays),
        deps,
        out_specs=vmem,
        out_shape=jax.ShapeDtypeStruct(arrays[0].shape, BF),
        name="add_many",
    )


class Reduction:
    def __init__(self, group, layout, halved=False):
        self.layout = [entry + (halved,) for entry in layout]
        bit = 2 if halved else 1
        self.states = [(group[0], [flip(send, "dp", bit) for send in group[1:]])]
        stripe_bits = bits_of(lax.axis_size("blk"))
        self.todo = [] if halved else [("dp", 2, "column")]
        self.todo += [("blk", bit, "stripe") for bit in stripe_bits]

    def step(self, deps=()):
        axis, bit, cut = self.todo.pop(0)
        keep, send = add_split(bit_of(axis, bit), *self.states[0], cut, deps)
        self.states = [(keep, [flip(send, axis, bit)])]
        return send

    def join(self, other):
        self.states += other.states
        self.layout += other.layout

    def deal(self, deps):
        at = (lax.axis_index("blk") // 2).astype(jnp.int32).reshape(1)
        keeps, gots = zip(*((keep, got[0]) for keep, got in self.states))
        sends = add_deal(at, keeps, gots, deps)
        self.states = [sends[0]] + [flip(x, "blk", 2 * j) for j, x in enumerate(sends) if j]
        self.todo = []
        return sends[0]

    def gather(self, deps):
        if isinstance(self.states[0], tuple):
            keep, (got,) = self.states[0]
            self.states = [keep[0], got[0]]
        share = add_many(self.states, deps)
        for bit in bits_of(lax.axis_size("dp"))[2:]:
            share = (share.astype(F32) + flip(share, "dp", bit).astype(F32)).astype(BF)
        self.states = [share] + [flip(share, "dp", j) for j in (1, 2, 3)]
        return share

    def result(self):
        at = (lax.axis_index("dp") % 4).astype(jnp.int32).reshape(1)
        return assemble(at, self.states, self.layout)


def gather_frames(x):
    bits = bits_of(lax.axis_size("blk"))
    shape = x.shape
    x = x.reshape((1,) * len(bits) + shape)
    for n, bit in reversed(list(enumerate(bits))):
        x = double(x, "blk", bit, len(bits) - 1 - n)
    return x.reshape((-1,) + shape[1:])


def shards(
    tokens,
    frame_seg,
    clip_class,
    class_table,
    mod_weight,
    mod_bias,
    qkv_space,
    out_space,
    qkv_time,
    out_time,
    up_weight,
    down_weight,
    cotangent,
):
    stripes = lax.axis_size("blk")
    stripe = lax.axis_index("blk")
    me = stripe.astype(jnp.int32).reshape(1)
    tokens, cotangent = tokens[0], cotangent[0]
    frames, patches, _ = tokens.shape
    per = frames // stripes
    chunks = 2
    part = patches // chunks
    classes = class_table.shape[0]

    blocks = [
        lax.dynamic_slice_in_dim(tokens, (stripe ^ j) * per, per, 0) for j in range(stripes)
    ]
    blocks = exchange(blocks)

    segment = frame_seg[0]
    clip_ids = clip_class[0]
    clip_hit = segment[:, None] == jnp.arange(clip_ids.shape[0], dtype=jnp.int32)[None, :]
    frame_class = jnp.sum(jnp.where(clip_hit, clip_ids[None, :], 0), axis=1)

    def embed(class_of):
        hit = class_of[:, None] == jnp.arange(classes, dtype=jnp.int32)[None, :]
        return hit, jnp.dot(hit.astype(F32), class_table, precision=exact_mode)

    cond = jax.nn.silu(embed(frame_class)[1]).astype(BF)
    hit_all, embedded_all = embed(jnp.concatenate(of_samples(frame_class)))
    cond_all, silu_back = jax.vjp(jax.nn.silu, embedded_all)
    slope = silu_back(jnp.ones_like(cond_all))[0]
    width, span = D // stripes, classes // stripes
    cond_own = lax.dynamic_slice_in_dim(cond_all.astype(BF), stripe * width, width, 1)
    hit_own = lax.dynamic_slice_in_dim(hit_all.astype(BF).T, stripe * span, span, 0)
    modulation = jnp.dot(cond, mod_weight, preferred_element_type=F32) + mod_bias
    modulation = modulation.reshape(frames, 9, D)
    mod_own = lax.dynamic_slice_in_dim(modulation, stripe * per, per, 0)[:, :2]
    spot_frame = jnp.repeat(jnp.arange(frames), 8)
    spot_patch = jnp.tile(jnp.arange(8), frames)
    spot_seg = jnp.repeat(segment, 8)
    bias = jnp.where(
        (spot_seg[:, None] == spot_seg[None, :]) & (spot_patch[:, None] == spot_patch[None, :]),
        0.0,
        masked_score,
    ).astype(F32)

    core = bit_of("dp", 1)
    sends, normed_one, kept_one = space_forward(blocks, mod_own, qkv_space, chunks)
    attended = [sends[0]] + [
        flip(b, "blk", j) for b, (j, _, _) in list(zip(sends, pieces(stripes, patches, chunks)))[1:]
    ]
    normed_one = normed_one.reshape(-1, D)
    normed_pair = flip(normed_one, "dp", 1)
    weights = (out_space, qkv_time, out_time, up_weight, down_weight)
    parts = []
    for c in range(chunks):
        here = slice(c * part, (c + 1) * part)
        parts.append(
            onward(
                me,
                bias,
                modulation,
                chunk_of(attended, stripes, c),
                tokens[:, here],
                cotangent[:, here],
                weights,
                c,
                [parts[-1]["n3"], normed_pair] if parts else (),
            )
        )
    output = jnp.concatenate([p["mixed"] for p in parts], 1)

    def grad_into(held, units, at, first, second, deps=()):
        return weight_grad(
            core, [p[first] for p in parts], [p[second] for p in parts], stripes, units, at, held, deps
        )

    deep, wide = up_weight.shape[1] // D, qkv_time.shape[1] // D
    group = grad_into(None, 2 * deep, 0, "n3", "dup")
    group = grad_into(group, 2 * deep, deep, "hid", "db3")
    feed = Reduction(group, ((1, deep), (deep, 1)))
    units = wide + 2
    group_time = grad_into(None, units, 0, "att2", "db2", [group[1]])
    dep = feed.step([group_time[1]])
    back = (qkv_time, out_time, out_space)
    one, two = parts
    one.update(time_back(me, bias, modulation, one, back, stripes, (), [dep]))
    two.update(
        time_back(
            me,
            bias,
            modulation,
            two,
            back,
            stripes,
            [*one["sends"][:NEAR], one["dmod_back"], one["dmod"], two["dmod"]],
        )
    )
    far = [flip(one["sends"][j], "blk", j) for j in range(NEAR, stripes)]
    rest = exchange(two["sends"])
    grads = rest[:NEAR] + far + rest[NEAR:]
    group = grad_into(group_time, units, 1, "n2", "dqkv", far)
    dep = feed.step([group[1]])
    group = grad_into(group, units, wide + 1, "att1", "db1", [dep, *rest[5:]])
    time = Reduction(group, ((1, 1), (1, wide), (1, 1)))
    dqkv_one, dqkv_own, dqkv_pair, late = space_backward(
        core, grads, kept_one, stripes, chunks, [group[1]]
    )
    dqkv_pair = flip(dqkv_pair, "dp", 1)
    dep = time.step([late])
    group = weight_grad(
        bit_of("dp", 2),
        [normed_one, normed_pair],
        [dqkv_own, dqkv_pair],
        stripes,
        wide,
        0,
        None,
        [dep],
    )
    space = Reduction(group, ((1, wide),), True)
    dvs, first_sums = space_norm(blocks, mod_own, qkv_space, dqkv_one, [group[1]])
    dvs = exchange(dvs)
    dep = feed.step([first_sums])
    dep = time.step([dep, *dvs[6:8]])
    mod_grad = pack(first_sums, late, [dep]).reshape(per, 9 * D)
    mod_grad = gather_frames(mod_grad)
    mod_grad = of_samples(mod_grad)
    dep = space.step([dep, *dvs[4:6]])
    dep = feed.step([dep])
    input_grad = finish(me, dvs, [p["dfirst"] for p in parts], [dep])
    time.join(space)
    dep = time.deal([input_grad])
    dep = feed.gather([dep])
    grad_mod_weight, grad_mod_bias, grad_table = mod_grads(
        mod_grad, mod_weight, cond_own, slope, hit_own, [dep]
    )
    share = mod_bias.shape[0] // stripes
    grad_mod_bias = lax.dynamic_slice_in_dim(grad_mod_bias.reshape(-1), stripe * share, share, 0)
    time.gather([grad_table])
    grad_up, grad_down = feed.result()
    grad_out_time, grad_qkv_time, grad_out_space, grad_qkv_space = time.result()
    return (
        output[None],
        input_grad[None],
        grad_table,
        grad_mod_weight,
        grad_mod_bias,
        grad_qkv_space,
        grad_out_space,
        grad_qkv_time,
        grad_out_time,
        grad_up,
        grad_down,
    )


def solution(mesh):
    tile = P("dp", None, "blk", None)
    row = P("blk", None)
    in_specs = (tile, P("dp", None), P("dp", None)) + (P(),) * 9 + (tile,)
    out_specs = (tile, tile, row, row, P("blk")) + (row,) * 6
    return jax.shard_map(shards, mesh=mesh, in_specs=in_specs, out_specs=out_specs, check_vma=False)
```

```python
from functools import partial

import jax
import jax.numpy as jnp
from jax import lax
from jax.experimental import pallas as pl
from jax.experimental.pallas import tpu as pltpu
from jax.sharding import PartitionSpec as P

HEADS = 12
HEAD_DIM = 64
D = HEADS * HEAD_DIM
PAIRS = HEADS // 2
BF = jnp.bfloat16
F32 = jnp.float32
exact_mode = lax.Precision.HIGHEST
masked_score = -1e30
EPS = 1e-6
GELU_C = 0.7978845608028654
GELU_A = 0.044715
VMEM_LIMIT = 60 * 1024 * 1024


def mm(a, b):
    return lax.dot_general(a, b, (((1,), (0,)), ((), ())), preferred_element_type=F32)


def mm_nt(a, b):
    return lax.dot_general(a, b, (((1,), (1,)), ((), ())), preferred_element_type=F32)


def mm_tn(a, b):
    return lax.dot_general(a, b, (((0,), (0,)), ((), ())), preferred_element_type=F32)


CHEAP = pl.CostEstimate(flops=1, bytes_accessed=1, transcendentals=0)
ANYWHERE = pl.BlockSpec(memory_space=pl.ANY)


def call(kernel, operands, in_specs, deps=(), **options):
    inputs, extra = len(operands), len(deps)

    def body(*refs):
        kernel(*refs[:inputs], *refs[inputs + extra :])

    return pl.pallas_call(
        body,
        in_specs=list(in_specs) + [ANYWHERE] * extra,
        compiler_params=pltpu.CompilerParams(vmem_limit_bytes=VMEM_LIMIT),
        cost_estimate=CHEAP,
        **options,
    )(*operands, *deps)


def first_head():
    return lax.broadcasted_iota(jnp.int32, (1, 2 * HEAD_DIM), 1) < HEAD_DIM


def norm_stats(x):
    mean = jnp.mean(x, -1, keepdims=True)
    xc = x - mean
    var = jnp.mean(xc * xc, -1, keepdims=True)
    rstd = lax.rsqrt(var + EPS)
    return xc * rstd, rstd


def norm_back(dn, xhat, rstd, scale):
    e = dn * (1.0 + scale)
    return rstd * (
        e - jnp.mean(e, -1, keepdims=True) - xhat * jnp.mean(e * xhat, -1, keepdims=True)
    )


def attend_pair(q2, k2, v2, mask, bias):
    zero, one = jnp.zeros_like(q2), jnp.ones_like(v2)
    scaled = q2 * jnp.asarray(0.125, BF)

    def head(q, v):
        s = mm_nt(q, k2)
        if bias is not None:
            s = s + bias
        top = jnp.max(s, -1, keepdims=True)
        return mm(jnp.exp(s - top).astype(BF), v), top

    ra, ma = head(jnp.where(mask, scaled, zero), jnp.where(mask, v2, one))
    rb, mb = head(jnp.where(mask, zero, scaled), jnp.where(mask, one, v2))
    total = pltpu.roll(jnp.where(mask, rb, ra), HEAD_DIM, 1)
    return jnp.where(mask, ra, rb) / total, jnp.where(mask, ma, mb) + jnp.log(total)


def pair_rows(logs):
    lane = lax.broadcasted_iota(jnp.int32, (1, 2 * HEAD_DIM), 1) % HEAD_DIM
    both = logs[0]
    for h in range(1, PAIRS):
        both = jnp.where(lane == h, logs[h], both)
    both = both.T
    return both[:8], both[HEAD_DIM : HEAD_DIM + 8]


def head_sums(att, datt):
    prod = (att.astype(F32) * datt.astype(F32)).astype(BF)
    shape = (16, D)
    row, feature = (lax.broadcasted_iota(jnp.int32, shape, n) for n in (0, 1))
    hit = feature // HEAD_DIM == row % 8 * 2 + row // 8
    return mm_nt(jnp.where(hit, 1.0, 0.0).astype(BF), prod)


def attend_pair_back(q2, k2, v2, do2, lse, inner, mask, bias):
    zero = jnp.zeros_like(q2)
    scaled = q2 * jnp.asarray(0.125, BF)

    def head(q, do, n):
        s = mm_nt(k2, q)
        if bias is not None:
            s = s + bias
        p = jnp.exp(s - lse[n])
        ds = p * (mm_nt(v2, do) - inner[n])
        return p.astype(BF), ds.astype(BF)

    qa, qb = jnp.where(mask, scaled, zero), jnp.where(mask, zero, scaled)
    da, db = jnp.where(mask, do2, zero), jnp.where(mask, zero, do2)
    ka, kb = jnp.where(mask, k2, zero), jnp.where(mask, zero, k2)
    pa, dsa = head(qa, da, 0)
    pb, dsb = head(qb, db, 1)
    dv2 = mm(pa, da) + mm(pb, db)
    dk2 = mm(dsa, qa) + mm(dsb, qb)
    if DQ_FORM == 0:
        dq2 = 0.125 * (mm_tn(dsa, ka) + mm_tn(dsb, kb))
    else:
        dq2 = 0.125 * (mm_tn(ka, dsa) + mm_tn(kb, dsb)).T
    return dq2, dk2, dv2


DQ_FORM = 1


NEAR = 4


def pieces(stripes, rows, chunks):
    part = rows // chunks
    out = [(j, 0, rows) for j in range(NEAR)]
    for c in range(chunks):
        out += [(j, c * part, (c + 1) * part) for j in range(NEAR, stripes)]
    return out


def chunk_of(blocks, stripes, c):
    far = stripes - NEAR
    return list(blocks[:NEAR]) + list(blocks[NEAR + c * far : NEAR + (c + 1) * far])


def space_forward_kernel(stripes, chunks, *refs):
    x_refs = refs[:stripes]
    mod_ref, w_ref = refs[stripes : stripes + 2]
    att_refs = refs[stripes + 2 : -4]
    n1_ref, qkv_ref, att_ref, lse_ref = refs[-4:]
    rows = x_refs[0].shape[1]
    part = rows // chunks
    for j in range(stripes):
        x = x_refs[j][0].astype(F32)
        xhat, _ = norm_stats(x)
        n1_ref[0, j * rows : (j + 1) * rows, :] = (
            xhat * (1.0 + mod_ref[0, 1:2, :]) + mod_ref[0, 0:1, :]
        ).astype(BF)
    for s in range(3):
        qkv_ref[0, :, s * D : (s + 1) * D] = mm(
            n1_ref[0], w_ref[:, s * D : (s + 1) * D]
        ).astype(BF)
    mask = first_head()
    logs = []
    for h in range(PAIRS):
        q2, k2, v2 = (
            qkv_ref[0, :, s * D + h * 128 : s * D + (h + 1) * 128] for s in range(3)
        )
        att, log = attend_pair(q2, k2, v2, mask, None)
        logs.append(log)
        att = att.astype(BF)
        att_ref[0, :, h * 128 : (h + 1) * 128] = att
        for out, (j, low, high) in zip(att_refs, pieces(stripes, rows, chunks)):
            out[0, :, h * 128 : (h + 1) * 128] = att[j * rows + low : j * rows + high]
    lse_ref[0, 0:8, :], lse_ref[0, 8:16, :] = pair_rows(logs)


def space_forward(blocks, mod_own, weight, chunks):
    stripes = len(blocks)
    frames, rows, _ = blocks[0].shape
    whole = rows * stripes
    sizes = [high - low for _, low, high in pieces(stripes, rows, chunks)] + [whole]
    outs = call(
        partial(space_forward_kernel, stripes, chunks),
        (*blocks, mod_own, weight),
        [pl.BlockSpec((1, rows, D), lambda f: (f, 0, 0))] * stripes
        + [
            pl.BlockSpec((1,) + mod_own.shape[1:], lambda f: (f, 0, 0)),
            pl.BlockSpec(weight.shape, lambda f: (0, 0)),
        ],
        grid=(frames,),
        out_specs=[pl.BlockSpec((1, n, D), lambda f: (f, 0, 0)) for n in sizes]
        + [
            pl.BlockSpec((1, whole, 3 * D), lambda f: (f, 0, 0)),
            pl.BlockSpec((1, whole, D), lambda f: (f, 0, 0)),
            pl.BlockSpec((1, 16, whole), lambda f: (f, 0, 0)),
        ],
        out_shape=[jax.ShapeDtypeStruct((frames, n, D), BF) for n in sizes]
        + [
            jax.ShapeDtypeStruct((frames, whole, 3 * D), BF),
            jax.ShapeDtypeStruct((frames, whole, D), BF),
            jax.ShapeDtypeStruct((frames, 16, whole), F32),
        ],
        name="space_forward",
    )
    return outs[:-4], outs[-4], outs[-3:]


def space_backward_kernel(stripes, rows, chunks, *refs):
    place = pieces(stripes, rows, chunks)
    d_refs, refs = refs[: len(place)], refs[len(place) :]
    sum_refs, refs = refs[:stripes], refs[stripes:]
    core_ref, qkv_ref, att_ref, lse_ref, dqkv_ref, keep_ref, send_ref, late_ref, datt_ref = refs
    for d_ref, (j, low, high) in zip(d_refs, place):
        datt_ref[j * rows + low : j * rows + high, :] = d_ref[...]

    @pl.when(pl.program_id(0) == 0)
    def _():
        late = sum_refs[0][...].astype(F32)
        for r in sum_refs[1:]:
            late = late + r[...].astype(F32)
        late_ref[...] = late

    mask = first_head()
    inner = head_sums(att_ref[0], datt_ref[...])
    for h in range(PAIRS):
        q2, k2, v2 = (
            qkv_ref[0, :, s * D + h * 128 : s * D + (h + 1) * 128] for s in range(3)
        )
        do2 = datt_ref[:, h * 128 : (h + 1) * 128]
        lse = [lse_ref[0, n : n + 1, :] for n in (h, 8 + h)]
        sums = [inner[n : n + 1] for n in (h, 8 + h)]
        grads = attend_pair_back(q2, k2, v2, do2, lse, sums, mask, None)
        for s in range(3):
            dqkv_ref[0, :, s * D + h * 128 : s * D + (h + 1) * 128] = grads[s].astype(BF)
    half = dqkv_ref.shape[-1] // 2
    for ref, side in ((keep_ref, core_ref[0]), (send_ref, 1 - core_ref[0])):
        ref[...] = dqkv_ref[0, :, pl.ds(pl.multiple_of(side * half, half), half)]


def space_backward(core, grads, kept, stripes, chunks, deps):
    frames, whole, _ = kept[0].shape
    rows = whole // stripes
    extra = frames * 8
    place = pieces(stripes, rows, chunks)
    last = list(grads[:NEAR]) + list(grads[NEAR - stripes :])
    half = pl.BlockSpec((whole, 3 * D // 2), lambda f: (f, 0))
    return call(
        partial(space_backward_kernel, stripes, rows, chunks),
        (*grads, *last, core, *kept),
        [pl.BlockSpec((high - low, D), lambda f: (f, 0)) for _, low, high in place]
        + [
            pl.BlockSpec((extra, D), lambda f, n=g.shape[0] // extra - 1: (n, 0)) for g in last
        ]
        + [
            pl.BlockSpec(memory_space=pltpu.SMEM),
            pl.BlockSpec((1, whole, 3 * D), lambda f: (f, 0, 0)),
            pl.BlockSpec((1, whole, D), lambda f: (f, 0, 0)),
            pl.BlockSpec((1, 16, whole), lambda f: (f, 0, 0)),
        ],
        deps,
        grid=(frames,),
        out_specs=[
            pl.BlockSpec((1, whole, 3 * D), lambda f: (f, 0, 0)),
            half,
            half,
            pl.BlockSpec((extra, D), lambda f: (0, 0)),
        ],
        out_shape=[
            jax.ShapeDtypeStruct((frames, whole, 3 * D), BF),
            jax.ShapeDtypeStruct((frames * whole, 3 * D // 2), BF),
            jax.ShapeDtypeStruct((frames * whole, 3 * D // 2), BF),
            jax.ShapeDtypeStruct((extra, D), F32),
        ],
        scratch_shapes=[pltpu.VMEM((whole, D), BF)],
        name="space_backward",
    )


def space_norm_kernel(stripes, *refs):
    x_refs, (mod_ref, w_ref, dqkv_ref), refs = refs[:stripes], refs[stripes : stripes + 3], refs[stripes + 3 :]
    dv_refs, dmod_ref, dn_ref = refs[:stripes], refs[stripes], refs[stripes + 1]
    rows = x_refs[0].shape[1]
    dn_ref[...] = mm_nt(dqkv_ref[0], w_ref[...])
    shift_sum = jnp.zeros((1, D), F32)
    scale_sum = jnp.zeros((1, D), F32)
    for j in range(stripes):
        xhat, rstd = norm_stats(x_refs[j][0].astype(F32))
        d = dn_ref[j * rows : (j + 1) * rows, :]
        dv_refs[j][0] = norm_back(d, xhat, rstd, mod_ref[0, 1:2, :]).astype(BF)
        shift_sum = shift_sum + jnp.sum(d, 0, keepdims=True)
        scale_sum = scale_sum + jnp.sum(d * xhat, 0, keepdims=True)
    dmod_ref[0, 0:1, :] = shift_sum
    dmod_ref[0, 1:2, :] = scale_sum


def space_norm(blocks, mod_own, weight, dqkv, deps):
    stripes = len(blocks)
    frames, rows, _ = blocks[0].shape
    whole = rows * stripes
    block = pl.BlockSpec((1, rows, D), lambda f: (f, 0, 0))
    outs = call(
        partial(space_norm_kernel, stripes),
        (*blocks, mod_own, weight, dqkv),
        [block] * stripes
        + [
            pl.BlockSpec((1,) + mod_own.shape[1:], lambda f: (f, 0, 0)),
            pl.BlockSpec(weight.shape, lambda f: (0, 0)),
            pl.BlockSpec((1, whole, 3 * D), lambda f: (f, 0, 0)),
        ],
        deps,
        grid=(frames,),
        out_specs=[block] * stripes + [pl.BlockSpec((1, 2, D), lambda f: (f, 0, 0))],
        out_shape=[jax.ShapeDtypeStruct((frames, rows, D), BF)] * stripes
        + [jax.ShapeDtypeStruct((frames, 2, D), F32)],
        scratch_shapes=[pltpu.VMEM((whole, D), F32)],
        name="space_norm",
    )
    return outs[:-1], outs[-1]


STEP = 4


def spots(i, g, rows_g):
    fs = pl.ds(i * STEP, STEP)
    at = pl.ds(pl.multiple_of(g * rows_g + i * STEP * 8, STEP * 8), STEP * 8)
    return fs, at


def as3(x):
    return x.reshape(STEP, 8, D)


def as2(x):
    return x.reshape(STEP * 8, D)


def over_patches(terms):
    total = terms[0]
    for t in terms[1:]:
        total = total + t
    return jnp.sum(total, 1, keepdims=True)


def bring(source, target, sem):
    copy = pltpu.make_async_copy(source, target, sem)
    copy.start()
    return copy


def onward_kernel(stripes, chunk, *refs):
    me_ref, bias_ref, mod_ref = refs[:3]
    a_refs = refs[3 : 3 + stripes]
    tok_ref, cot_ref = refs[3 + stripes : 5 + stripes]
    weight_refs = refs[5 + stripes : 10 + stripes]
    (
        mixed_ref,
        dmod_ref,
        lse_ref,
        att1_out,
        n2_out,
        att2_out,
        n3_out,
        dup_out,
        hid_out,
        db3_out,
        db2_out,
        first_out,
        b1_out,
        dsecond_out,
        qkv_out,
    ) = refs[10 + stripes : 25 + stripes]
    (
        wos,
        wqkv,
        wot,
        wu,
        wd,
        att1_ref,
        n2_ref,
        att2_ref,
        n3_ref,
        dup_ref,
        hid_ref,
        db3_ref,
        db2_ref,
        first_ref,
        b1_ref,
        second_ref,
        qkv_ref,
        nat_ref,
        b2_ref,
        b3_ref,
        dn_ref,
        in_sems,
        out_sems,
    ) = refs[25 + stripes :]
    frames, patches, _ = tok_ref.shape
    groups = patches // 8
    rows = frames * patches
    rows_g = frames * 8
    per = frames // stripes
    ff = wu.shape[1]
    me = me_ref[0]
    mask = first_head()
    held = (wos, wqkv, wot, wu, wd)
    loads = [bring(w, v, in_sems.at[n]) for n, (w, v) in enumerate(zip(weight_refs, held))]
    stores = []

    def send(source, target):
        stores.append(bring(source, target, out_sems.at[len(stores)]))

    for j in range(stripes):
        s = lax.bitwise_xor(me, j)
        start = pl.multiple_of(s * (per * patches), per * patches)
        low = chunk * patches if a_refs[j].shape[1] > patches else 0
        att1_ref[pl.ds(start, per * patches), :] = a_refs[j][:, low : low + patches, :].reshape(
            per * patches, D
        )
    send(att1_ref, att1_out)
    loads[0].wait()
    nat_ref[...] = mm(att1_ref[...], wos[...]).reshape(frames, patches, D)

    def stage_one(i, carry):
        for g in range(groups):
            fs, at = spots(i, g, rows_g)
            tok = tok_ref[fs].astype(F32)[:, 8 * g : 8 * g + 8]
            b1 = nat_ref[fs, 8 * g : 8 * g + 8, :]
            first = tok + mod_ref[fs, 2:3, :] * b1
            xhat, _ = norm_stats(first)
            n2 = xhat * (1.0 + mod_ref[fs, 4:5, :]) + mod_ref[fs, 3:4, :]
            b1_ref[at, :] = as2(b1)
            first_ref[at, :] = as2(first)
            n2_ref[at, :] = as2(n2).astype(BF)
        return carry

    lax.fori_loop(0, frames // STEP, stage_one, 0, unroll=8)
    send(b1_ref, b1_out)
    send(first_ref, first_out)
    send(n2_ref, n2_out)

    loads[1].wait()
    for s in range(3):
        qkv_ref[:, s * D : (s + 1) * D] = mm(n2_ref[...], wqkv[:, s * D : (s + 1) * D]).astype(BF)
    send(qkv_ref, qkv_out)

    def time_attend(g, carry):
        at = pl.ds(pl.multiple_of(g * rows_g, rows_g), rows_g)
        logs = []
        for h in range(PAIRS):
            q2, k2, v2 = (
                qkv_ref[at, s * D + h * 128 : s * D + (h + 1) * 128] for s in range(3)
            )
            att, log = attend_pair(q2, k2, v2, mask, bias_ref[...])
            logs.append(log)
            att2_ref[at, h * 128 : (h + 1) * 128] = att.astype(BF)
        lse_ref[g, 0:8, :], lse_ref[g, 8:16, :] = pair_rows(logs)
        return carry

    lax.fori_loop(0, groups, time_attend, 0)
    send(att2_ref, att2_out)
    loads[2].wait()
    b2_ref[...] = mm(att2_ref[...], wot[...])

    def stage_two(i, carry):
        for g in range(groups):
            fs, at = spots(i, g, rows_g)
            second = as3(first_ref[at, :]) + mod_ref[fs, 5:6, :] * as3(b2_ref[at, :])
            xhat, _ = norm_stats(second)
            n3 = xhat * (1.0 + mod_ref[fs, 7:8, :]) + mod_ref[fs, 6:7, :]
            cot = cot_ref[fs].astype(F32)[:, 8 * g : 8 * g + 8]
            second_ref[at, :] = as2(second)
            n3_ref[at, :] = as2(n3).astype(BF)
            db3_ref[at, :] = as2(mod_ref[fs, 8:9, :] * cot).astype(BF)
        return carry

    lax.fori_loop(0, frames // STEP, stage_two, 0, unroll=8)
    send(n3_ref, n3_out)
    send(db3_ref, db3_out)

    loads[3].wait()
    loads[4].wait()
    b3_ref[...] = jnp.zeros_like(b3_ref)
    dn_ref[...] = jnp.zeros_like(dn_ref)
    wide = FEED_COLS
    part = FEED_ROWS

    def feed(b, carry):
        cols = pl.ds(pl.multiple_of(b * wide, wide), wide)
        for r in range(rows // part):
            at = pl.ds(r * part, part)
            u = mm(n3_ref[at, :], wu[:, cols])
            dh = mm_nt(db3_ref[at, :], wd[cols, :])
            u2 = u * u
            t = jnp.tanh(u * (GELU_C + (GELU_C * GELU_A) * u2))
            half = 0.5 + 0.5 * t
            slope = half + (0.5 * u) * ((1.0 - t * t) * (GELU_C + (3.0 * GELU_C * GELU_A) * u2))
            hid = (u * half).astype(BF)
            dup = (dh * slope).astype(BF)
            hid_ref[at, cols] = hid
            dup_ref[at, cols] = dup
            b3_ref[at, :] += mm(hid, wd[cols, :])
            dn_ref[at, :] += mm_nt(dup, wu[:, cols])
        return carry

    lax.fori_loop(0, ff // wide, feed, 0)
    send(hid_ref, hid_out)
    send(dup_ref, dup_out)

    def stage_three(i, carry):
        parts = [[] for _ in range(4)]
        for g in range(groups):
            fs, at = spots(i, g, rows_g)
            cot = cot_ref[fs].astype(F32)[:, 8 * g : 8 * g + 8]
            second = as3(second_ref[at, :])
            b3 = as3(b3_ref[at, :])
            dn = as3(dn_ref[at, :])
            xhat, rstd = norm_stats(second)
            dsecond = cot + norm_back(dn, xhat, rstd, mod_ref[fs, 7:8, :])
            nat_ref[fs, 8 * g : 8 * g + 8, :] = second + mod_ref[fs, 8:9, :] * b3
            second_ref[at, :] = as2(dsecond)
            db2_ref[at, :] = as2(mod_ref[fs, 5:6, :] * dsecond).astype(BF)
            for k, t in enumerate((dsecond * as3(b2_ref[at, :]), dn, dn * xhat, cot * b3)):
                parts[k].append(t)
        fs, _ = spots(i, 0, rows_g)
        for k in range(4):
            dmod_ref[fs, k : k + 1, :] = over_patches(parts[k])
        mixed_ref[fs] = nat_ref[fs].astype(BF)
        return carry

    lax.fori_loop(0, frames // STEP, stage_three, 0, unroll=8)
    send(second_ref, dsecond_out)
    send(db2_ref, db2_out)
    for copy in stores:
        copy.wait()


FEED_COLS = 1536
FEED_ROWS = 256


def onward(me, bias, modulation, attended, tokens, cotangent, weights, chunk=0, deps=()):
    stripes = len(attended)
    frames, patches, _ = tokens.shape
    rows = frames * patches
    ff = weights[3].shape[1]
    vmem, anywhere = pl.BlockSpec(memory_space=pltpu.VMEM), pl.BlockSpec(memory_space=pl.ANY)
    kept = [(D, BF), (D, BF), (D, BF), (D, BF), (ff, BF), (ff, BF), (D, BF), (D, BF)]
    kept += [(D, F32), (D, F32), (D, F32), (3 * D, BF)]
    outs = call(
        partial(onward_kernel, stripes, chunk),
        (me, bias, modulation, *attended, tokens, cotangent, *weights),
        [pl.BlockSpec(memory_space=pltpu.SMEM)] + [vmem] * (4 + stripes) + [anywhere] * 5,
        deps,
        out_specs=[vmem] * 3 + [anywhere] * len(kept),
        out_shape=[
            jax.ShapeDtypeStruct((frames, patches, D), BF),
            jax.ShapeDtypeStruct((frames, 4, D), F32),
            jax.ShapeDtypeStruct((patches // 8, 16, frames * 8), F32),
        ]
        + [jax.ShapeDtypeStruct((rows, cols), kind) for cols, kind in kept],
        scratch_shapes=[pltpu.VMEM(w.shape, BF) for w in weights]
        + [pltpu.VMEM((rows, cols), kind) for cols, kind in kept]
        + [pltpu.VMEM((frames, patches, D), F32)]
        + [pltpu.VMEM((rows, D), F32)] * 3
        + [pltpu.SemaphoreType.DMA((5,)), pltpu.SemaphoreType.DMA((len(kept),))],
        name="onward",
    )
    names = ("mixed", "dmod", "lse", "att1", "n2", "att2", "n3", "dup", "hid", "db3")
    names += ("db2", "first", "b1", "dsecond", "qkv")
    return dict(zip(names, outs))


def time_back_kernel(stripes, frames, last, *refs):
    me_ref, bias_ref, mod_ref, qkv_ref, db2_ref, att2_ref, lse_ref = refs[:7]
    late_ins, weight_refs = refs[7:10], refs[10:13]
    others = refs[13 : 13 + (NEAR + 3 if last else 0)]
    refs = refs[13 + len(others) :]
    dfirst_ref, dmod_ref = refs[:2]
    datt_refs = refs[2 : 2 + stripes]
    dqkv_out, db1_out = refs[2 + stripes : 4 + stripes]
    (
        first_ref,
        b1_ref,
        dsecond_ref,
        wqkv,
        wot,
        wos,
        dqkv_ref,
        db1_ref,
        nat_ref,
        dn_ref,
        do_ref,
        sums_ref,
        in_sems,
        out_sems,
    ) = refs[4 + stripes :]
    patches = nat_ref.shape[1]
    groups = patches // 8
    rows_g = frames * 8
    per = frames // stripes
    me = me_ref[0]
    mask = first_head()
    held = (wot, wqkv, first_ref, b1_ref, dsecond_ref, wos)
    sources = (weight_refs[1], weight_refs[0]) + tuple(late_ins) + (weight_refs[2],)
    loads = [bring(w, v, in_sems.at[n]) for n, (w, v) in enumerate(zip(sources, held))]
    loads[0].wait()
    do_ref[...] = mm_nt(db2_ref[...], wot[...]).astype(BF)

    def attend_back(g, carry):
        at = pl.ds(pl.multiple_of(g * rows_g, rows_g), rows_g)
        inner = head_sums(att2_ref[at, :], do_ref[at, :])
        for h in range(PAIRS):
            q2, k2, v2 = (
                qkv_ref[at, s * D + h * 128 : s * D + (h + 1) * 128] for s in range(3)
            )
            do2 = do_ref[at, h * 128 : (h + 1) * 128]
            lse = [lse_ref[g, n : n + 1, :] for n in (h, 8 + h)]
            sums = [inner[n : n + 1] for n in (h, 8 + h)]
            grads = attend_pair_back(q2, k2, v2, do2, lse, sums, mask, bias_ref[...])
            for s in range(3):
                dqkv_ref[at, s * D + h * 128 : s * D + (h + 1) * 128] = grads[s].astype(BF)
        return carry

    lax.fori_loop(0, groups, attend_back, 0)
    stores = [bring(dqkv_ref, dqkv_out, out_sems.at[0])]
    for copy in loads[1:]:
        copy.wait()
    dn_ref[...] = mm_nt(dqkv_ref[...], wqkv[...])

    def stage_four(i, carry):
        parts = [[] for _ in range(3)]
        for g in range(groups):
            fs, at = spots(i, g, rows_g)
            dn = as3(dn_ref[at, :])
            xhat, rstd = norm_stats(as3(first_ref[at, :]))
            dfirst = as3(dsecond_ref[at, :]) + norm_back(dn, xhat, rstd, mod_ref[fs, 4:5, :])
            nat_ref[fs, 8 * g : 8 * g + 8, :] = dfirst
            for k, t in enumerate((dfirst * as3(b1_ref[at, :]), dn, dn * xhat)):
                parts[k].append(t)
        fs, _ = spots(i, 0, rows_g)
        for k in range(3):
            dmod_ref[fs, k : k + 1, :] = over_patches(parts[k])
        dfirst = nat_ref[fs]
        dfirst_ref[fs] = dfirst.astype(BF)
        span = STEP * patches
        db1_ref[pl.ds(pl.multiple_of(i * span, span), span), :] = (
            (mod_ref[fs, 2:3, :] * dfirst).astype(BF).reshape(span, D)
        )
        return carry

    lax.fori_loop(0, frames // STEP, stage_four, 0, unroll=8)
    stores.append(bring(db1_ref, db1_out, out_sems.at[1]))
    nat_ref[...] = mm_nt(db1_ref[...], wos[...]).reshape(frames, patches, D)
    if last:
        back, one, two = others[NEAR:]
        sums_ref[:, 0:3, :] = dmod_ref[...] + back[...]
        sums_ref[:, 3:7, :] = one[...] + two[...]
        sums_ref[:, 7:8, :] = jnp.zeros((frames, 1, D), F32)
    for j in range(stripes):
        s = lax.bitwise_xor(me, j)
        mine = nat_ref[pl.ds(s * per, per)].astype(BF)
        if last:
            width = patches
            if j < NEAR:
                width = 2 * patches
                for f in range(per):
                    datt_refs[j][f * width : f * width + patches, :] = others[j][
                        f * patches : (f + 1) * patches, :
                    ]
                    datt_refs[j][f * width + patches : (f + 1) * width, :] = mine[f]
            else:
                datt_refs[j][: per * patches, :] = mine.reshape(per * patches, D)
            datt_refs[j][per * width :, :] = sums_ref[pl.ds(s * per, per)].reshape(
                per * 8, D
            ).astype(BF)
        else:
            datt_refs[j][...] = mine.reshape(per * patches, D)
    for copy in stores:
        copy.wait()


def time_back(me, bias, modulation, onward_outs, weights, stripes, others=(), deps=()):
    o = onward_outs
    frames, patches, _ = o["mixed"].shape
    rows = frames * patches
    per = frames // stripes
    last = bool(others)
    vmem, anywhere = pl.BlockSpec(memory_space=pltpu.VMEM), pl.BlockSpec(memory_space=pl.ANY)
    bf = lambda *shape: jax.ShapeDtypeStruct(shape, BF)
    sends = [
        bf(per * (patches * (2 if j < NEAR else 1) + 8) if last else per * patches, D)
        for j in range(stripes)
    ]
    outs = call(
        partial(time_back_kernel, stripes, frames, last),
        (me, bias, modulation, o["qkv"], o["db2"], o["att2"], o["lse"], o["first"], o["b1"])
        + (o["dsecond"], *weights, *others),
        [pl.BlockSpec(memory_space=pltpu.SMEM)] + [vmem] * 6 + [anywhere] * 6 + [vmem] * len(others),
        deps,
        out_specs=[vmem] * (2 + stripes) + [anywhere] * 2,
        out_shape=[bf(frames, patches, D), jax.ShapeDtypeStruct((frames, 3, D), F32)]
        + sends
        + [bf(rows, 3 * D), bf(rows, D)],
        scratch_shapes=[pltpu.VMEM((rows, D), F32)] * 3
        + [pltpu.VMEM(w.shape, BF) for w in weights]
        + [
            pltpu.VMEM((rows, 3 * D), BF),
            pltpu.VMEM((rows, D), BF),
            pltpu.VMEM((frames, patches, D), F32),
            pltpu.VMEM((rows, D), F32),
            pltpu.VMEM((rows, D), BF),
            pltpu.VMEM((frames, 8, D), F32),
            pltpu.SemaphoreType.DMA((6,)),
            pltpu.SemaphoreType.DMA((2,)),
        ],
        name="time_back",
    )
    return dict(
        dfirst=outs[0], dmod_back=outs[1], sends=outs[2 : 2 + stripes], dqkv=outs[-2], db1=outs[-1]
    )


def finish_kernel(stripes, chunks, me_ref, *refs):
    dv_refs = refs[:stripes]
    first_refs = refs[stripes : stripes + chunks]
    out_ref = refs[-1]
    per = dv_refs[0].shape[0]
    part = first_refs[0].shape[1]
    for j in range(stripes):
        fs = pl.ds(lax.bitwise_xor(me_ref[0], j) * per, per)
        for c in range(chunks):
            spot = pl.ds(c * part, part)
            out_ref[fs, spot, :] = (
                dv_refs[j][:, spot, :].astype(F32) + first_refs[c][fs].astype(F32)
            ).astype(BF)


def finish(me, dvs, firsts, deps=()):
    stripes, chunks = len(dvs), len(firsts)
    frames, part, _ = firsts[0].shape
    vmem = pl.BlockSpec(memory_space=pltpu.VMEM)
    return call(
        partial(finish_kernel, stripes, chunks),
        (me, *dvs, *firsts),
        [pl.BlockSpec(memory_space=pltpu.SMEM)] + [vmem] * (stripes + chunks),
        deps,
        out_specs=vmem,
        out_shape=jax.ShapeDtypeStruct((frames, part * chunks, D), BF),
        name="finish",
    )


def flip(x, axis, bit):
    size = lax.axis_size(axis)
    return lax.ppermute(x, axis, [(i, i ^ bit) for i in range(size)])


def exchange(blocks):
    return [blocks[0]] + [flip(blocks[j], "blk", j) for j in range(1, len(blocks))]


def double(x, axis, bit, dim):
    own = (lax.axis_index(axis) // bit) % 2
    got = flip(x, axis, bit)
    low = jnp.where(own == 0, x, got)
    high = jnp.where(own == 0, got, x)
    return jnp.concatenate([low, high], dim)


def bits_of(size):
    return [1 << b for b in range(size.bit_length() - 1)]


def weight_grad_kernel(pairs, by_rows, held, bit_ref, *refs):
    a_refs, b_refs = refs[:pairs], refs[pairs : 2 * pairs]
    keep_ref, *send_refs, total_ref = refs[2 * pairs + held :]
    total = mm_tn(a_refs[0][...], b_refs[0][...])
    for a, b in zip(a_refs[1:], b_refs[1:]):
        total = total + mm_tn(a[...], b[...])
    total_ref[...] = total.reshape(total_ref.shape)
    bit = bit_ref[0]
    if by_rows:
        keep_ref[...] = total_ref[:, :, bit].astype(BF)
        send_refs[0][...] = total_ref[:, :, 1 - bit].astype(BF)
    else:
        keep_ref[:, 0] = total_ref[:, bit].astype(BF)
        deep = send_refs[0].shape[0]
        for n, send_ref in enumerate(send_refs):
            send_ref[:, 0] = total_ref[n * deep : (n + 1) * deep, 1 - bit].astype(BF)


def weight_grad(bit, firsts, seconds, stripes, units, at, held, deps=(), cuts=1):
    pairs = len(firsts)
    rows, cols = firsts[0].shape[1], seconds[0].shape[1]
    small = D // stripes
    half = small // 2
    by_rows = rows > D
    tall = D if cols % D == 0 else D // 2
    steps = rows // D if by_rows else cols // tall
    if by_rows:
        deep = rows // D
        wide = stripes // steps
        shape, spot = (wide, deep, half, D), lambda t: (t, at // deep, 0, 0)
        total = (wide, deep, 2, half, D)
    else:
        shape, spot = (stripes, 1, half, tall), lambda t: (0, at + t, 0, 0)
        total = (stripes, 2, half, tall)
    moving, still = (lambda t: (0, t)), (lambda t: (0, 0))
    block = pl.BlockSpec(shape, spot)
    send = pl.BlockSpec((shape[0] // cuts,) + shape[1:], spot)
    group = [jax.ShapeDtypeStruct((stripes, units, half, tall), BF)]
    group += [jax.ShapeDtypeStruct((stripes // cuts, units, half, tall), BF)] * cuts
    aliased = held is not None
    return call(
        partial(weight_grad_kernel, pairs, by_rows, 1 + cuts if aliased else 0),
        (bit, *firsts, *seconds, *(held or ())),
        [pl.BlockSpec(memory_space=pltpu.SMEM)]
        + [pl.BlockSpec((a.shape[0], D), moving if by_rows else still) for a in firsts]
        + [pl.BlockSpec((b.shape[0], tall), still if by_rows else moving) for b in seconds]
        + [ANYWHERE] * (1 + cuts if aliased else 0),
        deps,
        grid=(steps,),
        out_specs=[block] + [send] * cuts,
        scratch_shapes=[pltpu.VMEM(total, F32)],
        out_shape=group,
        input_output_aliases={2 * pairs + 1 + n: n for n in range(1 + cuts)} if aliased else {},
        name="weight_grad",
    )


def mod_grad_kernel(samples, *refs):
    g_refs, refs = refs[:samples], refs[samples:]
    w_ref, cond_ref, slope_ref, hit_ref, gw_ref, gb_ref, table_ref, g_ref, total_ref = refs
    step = pl.program_id(0)
    rows = w_ref.shape[0]

    @pl.when(step == 0)
    def _():
        at = 0
        for r in g_refs:
            g_ref[at : at + r.shape[0], :] = r[...]
            at += r.shape[0]
        for k in range(g_ref.shape[1] // D):
            cols = slice(k * D, (k + 1) * D)
            gw_ref[:, cols] = mm_tn(cond_ref[...], g_ref[:, cols])
            gb_ref[:, cols] = jnp.sum(g_ref[:, cols].astype(F32), 0, keepdims=True)

    total_ref[pl.ds(pl.multiple_of(step * rows, rows), rows), :] = mm_nt(w_ref[...], g_ref[...])

    @pl.when(step == pl.num_programs(0) - 1)
    def _():
        e = total_ref[...].T * slope_ref[...]
        high = e.astype(BF)
        low = (e - high.astype(F32)).astype(BF)
        table_ref[...] = mm(hit_ref[...], high) + mm(hit_ref[...], low)


def pack_kernel(first_ref, late_ref, out_ref):
    frames = first_ref.shape[0]
    for f in range(frames):
        both = [first_ref[f], late_ref[8 * f : 8 * f + 7, :]]
        out_ref[f] = jnp.concatenate(both, 0).astype(BF)


def pack(first_sums, late, deps):
    vmem = pl.BlockSpec(memory_space=pltpu.VMEM)
    frames = first_sums.shape[0]
    return call(
        pack_kernel,
        (first_sums, late),
        [vmem, vmem],
        deps,
        out_specs=vmem,
        out_shape=jax.ShapeDtypeStruct((frames, 9, D), BF),
        name="pack",
    )


def mod_grads(gs, weight, cond_own, slope, hit_own, deps):
    rows = slope.shape[0]
    still = lambda k: (0, 0)
    cols = weight.shape[1]
    each = 128
    wide, span = cond_own.shape[1], hit_own.shape[0]
    return call(
        partial(mod_grad_kernel, len(gs)),
        (*gs, weight, cond_own, slope, hit_own),
        [pl.BlockSpec((g.shape[0], cols), still) for g in gs]
        + [
            pl.BlockSpec((each, cols), lambda k: (k, 0)),
            pl.BlockSpec((rows, wide), still),
            pl.BlockSpec((rows, D), still),
            pl.BlockSpec((span, rows), still),
        ],
        deps,
        grid=(D // each,),
        out_specs=[
            pl.BlockSpec((wide, cols), still),
            pl.BlockSpec((1, cols), still),
            pl.BlockSpec((span, D), still),
        ],
        out_shape=[
            jax.ShapeDtypeStruct((wide, cols), F32),
            jax.ShapeDtypeStruct((1, cols), F32),
            jax.ShapeDtypeStruct((span, D), F32),
        ],
        scratch_shapes=[pltpu.VMEM((rows, cols), BF), pltpu.VMEM((D, rows), F32)],
        name="mod_grads",
    )


ORDER = (0, 2, 1, 3)


def of_four(x):
    across = flip(x, "dp", 2)
    return [x, across, flip(x, "dp", 1), flip(across, "dp", 1)]


def of_samples(x):
    if lax.axis_size("dp") == 4:
        return of_four(x)
    return [lax.all_gather(x, "dp", tiled=True)]


def add_split_kernel(cut, parts, bit_ref, keep_ref, *refs):
    got_refs, outs = refs[:parts], refs[parts:]
    bit = bit_ref[0]
    for out, side in zip(outs, (bit, 1 - bit)):
        if cut == "stripe":
            spot = (slice(None), side)
        else:
            half = keep_ref.shape[-1] // 2
            spot = (slice(None),) * 3 + (pl.ds(pl.multiple_of(side * half, half), half),)
        got = got_refs[0][spot].astype(F32)
        if parts == 2:
            low = pl.program_id(0) < pl.num_programs(0) // 2
            got = jnp.where(low, got, got_refs[1][spot].astype(F32))
        out[...] = (keep_ref[spot].astype(F32) + got).astype(BF)


def add_split(bit, keep, got, cut, deps=()):
    count, units, rows, cols = keep.shape
    parts = len(got)
    if cut == "stripe":
        keep, *got = (x.reshape(count // 2, 2, units, rows, cols) for x in (keep, *got))
        out = (count // 2, units, rows, cols)
        each = min(2, count // 2)
        steps = count // 2 // each
        in_spec = pl.BlockSpec((each, 2, units, rows, cols), lambda i: (i, 0, 0, 0, 0))
        got_specs = [in_spec]
        out_block = pl.BlockSpec((each, units, rows, cols), lambda i: (i, 0, 0, 0))
    else:
        each = 2
        steps = count // each
        out = (count, units, rows, cols // 2)
        shape = (each, units, rows, cols)
        in_spec = pl.BlockSpec(shape, lambda i: (i, 0, 0, 0))
        got_specs = [in_spec]
        if parts == 2:
            half = steps // 2
            got_specs = [
                pl.BlockSpec(shape, lambda i: (jnp.minimum(i, half - 1), 0, 0, 0)),
                pl.BlockSpec(shape, lambda i: (jnp.maximum(i - half, 0), 0, 0, 0)),
            ]
        out_block = pl.BlockSpec((each, units, rows, cols // 2), lambda i: (i, 0, 0, 0))
    return call(
        partial(add_split_kernel, cut, parts),
        (bit, keep, *got),
        [pl.BlockSpec(memory_space=pltpu.SMEM), in_spec, *got_specs],
        deps,
        grid=(steps,),
        out_specs=[out_block] * 2,
        out_shape=[jax.ShapeDtypeStruct(out, BF)] * 2,
        name="add_split",
    )


def assemble_kernel(layout, at_ref, *refs):
    shares, outs = refs[:4], refs[4:]
    half, cols = shares[0].shape[1:]
    for n, j in enumerate(ORDER):
        place = lax.bitwise_xor(at_ref[0], j)
        unit = 0
        for out, (deep, wide, halved) in zip(outs, layout):
            core, side = lax.rem(place, 2), lax.div(place, 2)
            if halved:
                core, side = side, core
            low = pl.multiple_of(core * half, half)
            step = cols if halved else 2 * cols
            left = pl.multiple_of(side * (wide * cols if halved else cols), cols)
            for r in range(deep):
                for c in range(wide):
                    out[pl.ds(r * 2 * half + low, half), pl.ds(c * step + left, cols)] = shares[n][
                        unit
                    ].astype(F32)
                    unit += 1


def assemble(at, shares, layout, deps):
    _, half, cols = shares[0].shape
    vmem = pl.BlockSpec(memory_space=pltpu.VMEM)
    return call(
        partial(assemble_kernel, layout),
        (at, *shares),
        [pl.BlockSpec(memory_space=pltpu.SMEM)] + [vmem] * 4,
        deps,
        out_specs=[vmem] * len(layout),
        out_shape=[
            jax.ShapeDtypeStruct((deep * 2 * half, wide * 2 * cols), F32)
            for deep, wide, _ in layout
        ],
        name="assemble",
    )


def bit_of(axis, bit):
    return ((lax.axis_index(axis) // bit) % 2).astype(jnp.int32).reshape(1)


def add_deal_kernel(groups, at_ref, *refs):
    keeps, gots, outs = refs[:groups], refs[groups : 2 * groups], refs[2 * groups :]
    for j, out in enumerate(outs):
        s = lax.bitwise_xor(at_ref[0], j)
        unit = 0
        for keep, got in zip(keeps, gots):
            n = keep.shape[1]
            out[unit : unit + n] = (keep[s].astype(F32) + got[s].astype(F32)).astype(BF)
            unit += n


def add_deal(at, keeps, gots, deps):
    vmem = pl.BlockSpec(memory_space=pltpu.VMEM)
    places, _, half, cols = keeps[0].shape
    units = sum(k.shape[1] for k in keeps)
    return call(
        partial(add_deal_kernel, len(keeps)),
        (at, *keeps, *gots),
        [pl.BlockSpec(memory_space=pltpu.SMEM)] + [vmem] * (2 * len(keeps)),
        deps,
        out_specs=[vmem] * places,
        out_shape=[jax.ShapeDtypeStruct((units, half, cols), BF)] * places,
        name="add_deal",
    )


def add_many_kernel(*refs):
    total = refs[0][...].astype(F32)
    for r in refs[1:-1]:
        total = total + r[...].astype(F32)
    refs[-1][...] = total.astype(BF)


def add_many(arrays, deps):
    vmem = pl.BlockSpec(memory_space=pltpu.VMEM)
    return call(
        add_many_kernel,
        tuple(arrays),
        [vmem] * len(arrays),
        deps,
        out_specs=vmem,
        out_shape=jax.ShapeDtypeStruct(arrays[0].shape, BF),
        name="add_many",
    )


class Reduction:
    def __init__(self, group, layout, halved=False):
        self.layout = [entry + (halved,) for entry in layout]
        bit = 2 if halved else 1
        self.states = [(group[0], [flip(send, "dp", bit) for send in group[1:]])]
        stripe_bits = bits_of(lax.axis_size("blk"))
        self.todo = [] if halved else [("dp", 2, "column")]
        self.todo += [("blk", bit, "stripe") for bit in stripe_bits]

    def step(self, deps=()):
        axis, bit, cut = self.todo.pop(0)
        keep, send = add_split(bit_of(axis, bit), *self.states[0], cut, deps)
        self.states = [(keep, [flip(send, axis, bit)])]
        return send

    def join(self, other):
        self.states += other.states
        self.layout += other.layout

    def deal(self, deps):
        at = (lax.axis_index("blk") // 2).astype(jnp.int32).reshape(1)
        keeps, gots = zip(*((keep, got[0]) for keep, got in self.states))
        sends = add_deal(at, keeps, gots, deps)
        self.states = [sends[0]] + [flip(x, "blk", 2 * j) for j, x in enumerate(sends) if j]
        self.todo = []
        return sends[0]

    def gather(self, deps):
        if isinstance(self.states[0], tuple):
            keep, (got,) = self.states[0]
            self.states = [keep[0], got[0]]
        share = add_many(self.states, deps)
        for bit in bits_of(lax.axis_size("dp"))[2:]:
            share = (share.astype(F32) + flip(share, "dp", bit).astype(F32)).astype(BF)
        self.states = of_four(share)
        return share

    def result(self, deps=()):
        at = (lax.axis_index("dp") % 4).astype(jnp.int32).reshape(1)
        return assemble(at, self.states, self.layout, deps)


def gather_frames(x):
    bits = bits_of(lax.axis_size("blk"))
    shape = x.shape
    x = x.reshape((1,) * len(bits) + shape)
    for n, bit in reversed(list(enumerate(bits))):
        x = double(x, "blk", bit, len(bits) - 1 - n)
    return x.reshape((-1,) + shape[1:])


def shards(
    tokens,
    frame_seg,
    clip_class,
    class_table,
    mod_weight,
    mod_bias,
    qkv_space,
    out_space,
    qkv_time,
    out_time,
    up_weight,
    down_weight,
    cotangent,
):
    stripes = lax.axis_size("blk")
    stripe = lax.axis_index("blk")
    me = stripe.astype(jnp.int32).reshape(1)
    tokens, cotangent = tokens[0], cotangent[0]
    frames, patches, _ = tokens.shape
    per = frames // stripes
    chunks = 2
    part = patches // chunks
    classes = class_table.shape[0]

    blocks = [
        lax.dynamic_slice_in_dim(tokens, (stripe ^ j) * per, per, 0) for j in range(stripes)
    ]
    blocks = exchange(blocks)

    segment = frame_seg[0]
    clip_ids = clip_class[0]
    clip_hit = segment[:, None] == jnp.arange(clip_ids.shape[0], dtype=jnp.int32)[None, :]
    frame_class = jnp.sum(jnp.where(clip_hit, clip_ids[None, :], 0), axis=1)

    def embed(class_of):
        hit = class_of[:, None] == jnp.arange(classes, dtype=jnp.int32)[None, :]
        return hit, jnp.dot(hit.astype(F32), class_table, precision=exact_mode)

    cond = jax.nn.silu(embed(frame_class)[1]).astype(BF)
    hit_all, embedded_all = embed(jnp.concatenate(of_samples(frame_class)))
    cond_all, silu_back = jax.vjp(jax.nn.silu, embedded_all)
    slope = silu_back(jnp.ones_like(cond_all))[0]
    width, span = D // stripes, classes // stripes
    cond_own = lax.dynamic_slice_in_dim(cond_all.astype(BF), stripe * width, width, 1)
    hit_own = lax.dynamic_slice_in_dim(hit_all.astype(BF).T, stripe * span, span, 0)
    modulation = jnp.dot(cond, mod_weight, preferred_element_type=F32) + mod_bias
    modulation = modulation.reshape(frames, 9, D)
    mod_own = lax.dynamic_slice_in_dim(modulation, stripe * per, per, 0)[:, :2]
    spot_frame = jnp.repeat(jnp.arange(frames), 8)
    spot_patch = jnp.tile(jnp.arange(8), frames)
    spot_seg = jnp.repeat(segment, 8)
    bias = jnp.where(
        (spot_seg[:, None] == spot_seg[None, :]) & (spot_patch[:, None] == spot_patch[None, :]),
        0.0,
        masked_score,
    ).astype(F32)

    core = bit_of("dp", 1)
    sends, normed_one, kept_one = space_forward(blocks, mod_own, qkv_space, chunks)
    attended = [sends[0]] + [
        flip(b, "blk", j) for b, (j, _, _) in list(zip(sends, pieces(stripes, patches, chunks)))[1:]
    ]
    normed_one = normed_one.reshape(-1, D)
    normed_pair = flip(normed_one, "dp", 1)
    weights = (out_space, qkv_time, out_time, up_weight, down_weight)
    parts = []
    for c in range(chunks):
        here = slice(c * part, (c + 1) * part)
        parts.append(
            onward(
                me,
                bias,
                modulation,
                chunk_of(attended, stripes, c),
                tokens[:, here],
                cotangent[:, here],
                weights,
                c,
                [parts[-1]["n3"], normed_pair] if parts else (),
            )
        )
    output = jnp.concatenate([p["mixed"] for p in parts], 1)

    def grad_into(held, units, at, first, second, deps=(), cuts=1):
        return weight_grad(
            core,
            [p[first] for p in parts],
            [p[second] for p in parts],
            stripes,
            units,
            at,
            held,
            deps,
            cuts,
        )

    deep, wide = up_weight.shape[1] // D, qkv_time.shape[1] // D
    group = grad_into(None, 2 * deep, 0, "n3", "dup")
    group = grad_into(group, 2 * deep, deep, "hid", "db3")
    feed = Reduction(group, ((1, deep), (deep, 1)))
    units = wide + 2
    group_time = grad_into(None, units, 0, "att2", "db2", [group[1]], 2)
    dep = feed.step([group_time[1]])
    back = (qkv_time, out_time, out_space)
    one, two = parts
    one.update(time_back(me, bias, modulation, one, back, stripes, (), [dep]))
    two.update(
        time_back(
            me,
            bias,
            modulation,
            two,
            back,
            stripes,
            [*one["sends"][:NEAR], one["dmod_back"], one["dmod"], two["dmod"]],
        )
    )
    far = [flip(one["sends"][j], "blk", j) for j in range(NEAR, stripes)]
    rest = exchange(two["sends"])
    grads = rest[:NEAR] + far + rest[NEAR:]
    group = grad_into(group_time, units, 1, "n2", "dqkv", far, 2)
    group = grad_into(group, units, wide + 1, "att1", "db1", rest[5:], 2)
    time = Reduction(group, ((1, 1), (1, wide), (1, 1)))
    dqkv_one, dqkv_own, dqkv_pair, late = space_backward(
        core, grads, kept_one, stripes, chunks, [group[1]]
    )
    dqkv_pair = flip(dqkv_pair, "dp", 1)
    dep = feed.step([late])
    dep = time.step([dep])
    group = weight_grad(
        bit_of("dp", 2),
        [normed_one, normed_pair],
        [dqkv_own, dqkv_pair],
        stripes,
        wide,
        0,
        None,
        [dep],
    )
    space = Reduction(group, ((1, wide),), True)
    dvs, first_sums = space_norm(blocks, mod_own, qkv_space, dqkv_one, [group[1]])
    dvs = exchange(dvs)
    dep = feed.step([first_sums])
    dep = time.step([dep, *dvs[6:8]])
    dep = space.step([dep, *dvs[4:6]])
    dep = feed.step([dep])
    time.join(space)
    dep = time.deal([dep])
    mod_grad = pack(first_sums, late, [dep]).reshape(per, 9 * D)
    mod_grad = gather_frames(mod_grad)
    dep = feed.gather([mod_grad])
    mod_grad = of_samples(mod_grad)
    input_grad = finish(me, dvs, [p["dfirst"] for p in parts], [dep])
    grad_mod_weight, grad_mod_bias, grad_table = mod_grads(
        mod_grad, mod_weight, cond_own, slope, hit_own, [input_grad]
    )
    share = mod_bias.shape[0] // stripes
    grad_mod_bias = lax.dynamic_slice_in_dim(grad_mod_bias.reshape(-1), stripe * share, share, 0)
    time.gather([grad_table])
    grad_up, grad_down = feed.result()
    grad_out_time, grad_qkv_time, grad_out_space, grad_qkv_space = time.result()
    return (
        output[None],
        input_grad[None],
        grad_table,
        grad_mod_weight,
        grad_mod_bias,
        grad_qkv_space,
        grad_out_space,
        grad_qkv_time,
        grad_out_time,
        grad_up,
        grad_down,
    )


def solution(mesh):
    tile = P("dp", None, "blk", None)
    row = P("blk", None)
    in_specs = (tile, P("dp", None), P("dp", None)) + (P(),) * 9 + (tile,)
    out_specs = (tile, tile, row, row, P("blk")) + (row,) * 6
    return jax.shard_map(shards, mesh=mesh, in_specs=in_specs, out_specs=out_specs, check_vma=False)
```

```python
from functools import partial

import jax
import jax.numpy as jnp
from jax import lax
from jax.experimental import pallas as pl
from jax.experimental.pallas import tpu as pltpu
from jax.sharding import PartitionSpec as P

HEADS = 12
HEAD_DIM = 64
D = HEADS * HEAD_DIM
PAIRS = HEADS // 2
BF = jnp.bfloat16
F32 = jnp.float32
exact_mode = lax.Precision.HIGHEST
masked_score = -1e30
EPS = 1e-6
GELU_C = 0.7978845608028654
GELU_A = 0.044715
VMEM_LIMIT = 60 * 1024 * 1024


def mm(a, b):
    return lax.dot_general(a, b, (((1,), (0,)), ((), ())), preferred_element_type=F32)


def mm_nt(a, b):
    return lax.dot_general(a, b, (((1,), (1,)), ((), ())), preferred_element_type=F32)


def mm_tn(a, b):
    return lax.dot_general(a, b, (((0,), (0,)), ((), ())), preferred_element_type=F32)


CHEAP = pl.CostEstimate(flops=1, bytes_accessed=1, transcendentals=0)
ANYWHERE = pl.BlockSpec(memory_space=pl.ANY)


def call(kernel, operands, in_specs, deps=(), **options):
    inputs, extra = len(operands), len(deps)

    def body(*refs):
        kernel(*refs[:inputs], *refs[inputs + extra :])

    return pl.pallas_call(
        body,
        in_specs=list(in_specs) + [ANYWHERE] * extra,
        compiler_params=pltpu.CompilerParams(vmem_limit_bytes=VMEM_LIMIT),
        cost_estimate=CHEAP,
        **options,
    )(*operands, *deps)


def first_head():
    return lax.broadcasted_iota(jnp.int32, (1, 2 * HEAD_DIM), 1) < HEAD_DIM


def norm_stats(x):
    mean = jnp.mean(x, -1, keepdims=True)
    xc = x - mean
    var = jnp.mean(xc * xc, -1, keepdims=True)
    rstd = lax.rsqrt(var + EPS)
    return xc * rstd, rstd


def norm_back(dn, xhat, rstd, scale):
    e = dn * (1.0 + scale)
    return rstd * (
        e - jnp.mean(e, -1, keepdims=True) - xhat * jnp.mean(e * xhat, -1, keepdims=True)
    )


def attend_pair(q2, k2, v2, mask, bias):
    zero, one = jnp.zeros_like(q2), jnp.ones_like(v2)
    scaled = q2 * jnp.asarray(0.125, BF)

    def head(q, v):
        s = mm_nt(q, k2)
        if bias is not None:
            s = s + bias
        top = jnp.max(s, -1, keepdims=True)
        return mm(jnp.exp(s - top).astype(BF), v), top

    ra, ma = head(jnp.where(mask, scaled, zero), jnp.where(mask, v2, one))
    rb, mb = head(jnp.where(mask, zero, scaled), jnp.where(mask, one, v2))
    total = pltpu.roll(jnp.where(mask, rb, ra), HEAD_DIM, 1)
    return jnp.where(mask, ra, rb) / total, jnp.where(mask, ma, mb) + jnp.log(total)


def pair_rows(logs):
    lane = lax.broadcasted_iota(jnp.int32, (1, 2 * HEAD_DIM), 1) % HEAD_DIM
    both = logs[0]
    for h in range(1, PAIRS):
        both = jnp.where(lane == h, logs[h], both)
    both = both.T
    return both[:8], both[HEAD_DIM : HEAD_DIM + 8]


def head_sums(att, datt):
    prod = (att.astype(F32) * datt.astype(F32)).astype(BF)
    shape = (16, D)
    row, feature = (lax.broadcasted_iota(jnp.int32, shape, n) for n in (0, 1))
    hit = feature // HEAD_DIM == row % 8 * 2 + row // 8
    return mm_nt(jnp.where(hit, 1.0, 0.0).astype(BF), prod)


def attend_pair_back(q2, k2, v2, do2, lse, inner, mask, bias):
    zero = jnp.zeros_like(q2)
    scaled = q2 * jnp.asarray(0.125, BF)

    def head(q, do, n):
        s = mm_nt(k2, q)
        if bias is not None:
            s = s + bias
        p = jnp.exp(s - lse[n])
        ds = p * (mm_nt(v2, do) - inner[n])
        return p.astype(BF), ds.astype(BF)

    qa, qb = jnp.where(mask, scaled, zero), jnp.where(mask, zero, scaled)
    da, db = jnp.where(mask, do2, zero), jnp.where(mask, zero, do2)
    ka, kb = jnp.where(mask, k2, zero), jnp.where(mask, zero, k2)
    pa, dsa = head(qa, da, 0)
    pb, dsb = head(qb, db, 1)
    dv2 = mm(pa, da) + mm(pb, db)
    dk2 = mm(dsa, qa) + mm(dsb, qb)
    if DQ_FORM == 0:
        dq2 = 0.125 * (mm_tn(dsa, ka) + mm_tn(dsb, kb))
    else:
        dq2 = 0.125 * (mm_tn(ka, dsa) + mm_tn(kb, dsb)).T
    return dq2, dk2, dv2


DQ_FORM = 1


NEAR = 4


def pieces(stripes, rows, chunks):
    part = rows // chunks
    out = [(j, 0, rows) for j in range(NEAR)]
    for c in range(chunks):
        out += [(j, c * part, (c + 1) * part) for j in range(NEAR, stripes)]
    return out


def chunk_of(blocks, stripes, c):
    far = stripes - NEAR
    return list(blocks[:NEAR]) + list(blocks[NEAR + c * far : NEAR + (c + 1) * far])


def space_forward_kernel(stripes, chunks, *refs):
    x_refs = refs[:stripes]
    mod_ref, w_ref = refs[stripes : stripes + 2]
    att_refs = refs[stripes + 2 : -4]
    n1_ref, qkv_ref, att_ref, lse_ref = refs[-4:]
    rows = x_refs[0].shape[1]
    part = rows // chunks
    for j in range(stripes):
        x = x_refs[j][0].astype(F32)
        xhat, _ = norm_stats(x)
        n1_ref[0, j * rows : (j + 1) * rows, :] = (
            xhat * (1.0 + mod_ref[0, 1:2, :]) + mod_ref[0, 0:1, :]
        ).astype(BF)
    for s in range(3):
        qkv_ref[0, :, s * D : (s + 1) * D] = mm(
            n1_ref[0], w_ref[:, s * D : (s + 1) * D]
        ).astype(BF)
    mask = first_head()
    logs = []
    for h in range(PAIRS):
        q2, k2, v2 = (
            qkv_ref[0, :, s * D + h * 128 : s * D + (h + 1) * 128] for s in range(3)
        )
        att, log = attend_pair(q2, k2, v2, mask, None)
        logs.append(log)
        att = att.astype(BF)
        att_ref[0, :, h * 128 : (h + 1) * 128] = att
        for out, (j, low, high) in zip(att_refs, pieces(stripes, rows, chunks)):
            out[0, :, h * 128 : (h + 1) * 128] = att[j * rows + low : j * rows + high]
    lse_ref[0, 0:8, :], lse_ref[0, 8:16, :] = pair_rows(logs)


def space_forward(blocks, mod_own, weight, chunks):
    stripes = len(blocks)
    frames, rows, _ = blocks[0].shape
    whole = rows * stripes
    sizes = [high - low for _, low, high in pieces(stripes, rows, chunks)] + [whole]
    outs = call(
        partial(space_forward_kernel, stripes, chunks),
        (*blocks, mod_own, weight),
        [pl.BlockSpec((1, rows, D), lambda f: (f, 0, 0))] * stripes
        + [
            pl.BlockSpec((1,) + mod_own.shape[1:], lambda f: (f, 0, 0)),
            pl.BlockSpec(weight.shape, lambda f: (0, 0)),
        ],
        grid=(frames,),
        out_specs=[pl.BlockSpec((1, n, D), lambda f: (f, 0, 0)) for n in sizes]
        + [
            pl.BlockSpec((1, whole, 3 * D), lambda f: (f, 0, 0)),
            pl.BlockSpec((1, whole, D), lambda f: (f, 0, 0)),
            pl.BlockSpec((1, 16, whole), lambda f: (f, 0, 0)),
        ],
        out_shape=[jax.ShapeDtypeStruct((frames, n, D), BF) for n in sizes]
        + [
            jax.ShapeDtypeStruct((frames, whole, 3 * D), BF),
            jax.ShapeDtypeStruct((frames, whole, D), BF),
            jax.ShapeDtypeStruct((frames, 16, whole), F32),
        ],
        name="space_forward",
    )
    return outs[:-4], outs[-4], outs[-3:]


def space_backward_kernel(stripes, rows, chunks, *refs):
    place = pieces(stripes, rows, chunks)
    d_refs, refs = refs[: len(place)], refs[len(place) :]
    sum_refs, refs = refs[:stripes], refs[stripes:]
    core_ref, qkv_ref, att_ref, lse_ref, dqkv_ref, keep_ref, send_ref, late_ref, datt_ref = refs
    for d_ref, (j, low, high) in zip(d_refs, place):
        datt_ref[j * rows + low : j * rows + high, :] = d_ref[...]

    @pl.when(pl.program_id(0) == 0)
    def _():
        late = sum_refs[0][...].astype(F32)
        for r in sum_refs[1:]:
            late = late + r[...].astype(F32)
        late_ref[...] = late

    mask = first_head()
    inner = head_sums(att_ref[0], datt_ref[...])
    for h in range(PAIRS):
        q2, k2, v2 = (
            qkv_ref[0, :, s * D + h * 128 : s * D + (h + 1) * 128] for s in range(3)
        )
        do2 = datt_ref[:, h * 128 : (h + 1) * 128]
        lse = [lse_ref[0, n : n + 1, :] for n in (h, 8 + h)]
        sums = [inner[n : n + 1] for n in (h, 8 + h)]
        grads = attend_pair_back(q2, k2, v2, do2, lse, sums, mask, None)
        for s in range(3):
            dqkv_ref[0, :, s * D + h * 128 : s * D + (h + 1) * 128] = grads[s].astype(BF)
    half = dqkv_ref.shape[-1] // 2
    for ref, side in ((keep_ref, core_ref[0]), (send_ref, 1 - core_ref[0])):
        ref[...] = dqkv_ref[0, :, pl.ds(pl.multiple_of(side * half, half), half)]


def space_backward(core, grads, kept, stripes, chunks, deps):
    frames, whole, _ = kept[0].shape
    rows = whole // stripes
    extra = frames * 8
    place = pieces(stripes, rows, chunks)
    last = list(grads[:NEAR]) + list(grads[NEAR - stripes :])
    half = pl.BlockSpec((whole, 3 * D // 2), lambda f: (f, 0))
    return call(
        partial(space_backward_kernel, stripes, rows, chunks),
        (*grads, *last, core, *kept),
        [pl.BlockSpec((high - low, D), lambda f: (f, 0)) for _, low, high in place]
        + [
            pl.BlockSpec((extra, D), lambda f, n=g.shape[0] // extra - 1: (n, 0)) for g in last
        ]
        + [
            pl.BlockSpec(memory_space=pltpu.SMEM),
            pl.BlockSpec((1, whole, 3 * D), lambda f: (f, 0, 0)),
            pl.BlockSpec((1, whole, D), lambda f: (f, 0, 0)),
            pl.BlockSpec((1, 16, whole), lambda f: (f, 0, 0)),
        ],
        deps,
        grid=(frames,),
        out_specs=[
            pl.BlockSpec((1, whole, 3 * D), lambda f: (f, 0, 0)),
            half,
            half,
            pl.BlockSpec((extra, D), lambda f: (0, 0)),
        ],
        out_shape=[
            jax.ShapeDtypeStruct((frames, whole, 3 * D), BF),
            jax.ShapeDtypeStruct((frames * whole, 3 * D // 2), BF),
            jax.ShapeDtypeStruct((frames * whole, 3 * D // 2), BF),
            jax.ShapeDtypeStruct((extra, D), F32),
        ],
        scratch_shapes=[pltpu.VMEM((whole, D), BF)],
        name="space_backward",
    )


def space_norm_kernel(stripes, *refs):
    x_refs, (mod_ref, w_ref, dqkv_ref), refs = refs[:stripes], refs[stripes : stripes + 3], refs[stripes + 3 :]
    dv_refs, dmod_ref, dn_ref = refs[:stripes], refs[stripes], refs[stripes + 1]
    rows = x_refs[0].shape[1]
    dn_ref[...] = mm_nt(dqkv_ref[0], w_ref[...])
    shift_sum = jnp.zeros((1, D), F32)
    scale_sum = jnp.zeros((1, D), F32)
    for j in range(stripes):
        xhat, rstd = norm_stats(x_refs[j][0].astype(F32))
        d = dn_ref[j * rows : (j + 1) * rows, :]
        dv_refs[j][0] = norm_back(d, xhat, rstd, mod_ref[0, 1:2, :]).astype(BF)
        shift_sum = shift_sum + jnp.sum(d, 0, keepdims=True)
        scale_sum = scale_sum + jnp.sum(d * xhat, 0, keepdims=True)
    dmod_ref[0, 0:1, :] = shift_sum
    dmod_ref[0, 1:2, :] = scale_sum


def space_norm(blocks, mod_own, weight, dqkv, deps):
    stripes = len(blocks)
    frames, rows, _ = blocks[0].shape
    whole = rows * stripes
    block = pl.BlockSpec((1, rows, D), lambda f: (f, 0, 0))
    outs = call(
        partial(space_norm_kernel, stripes),
        (*blocks, mod_own, weight, dqkv),
        [block] * stripes
        + [
            pl.BlockSpec((1,) + mod_own.shape[1:], lambda f: (f, 0, 0)),
            pl.BlockSpec(weight.shape, lambda f: (0, 0)),
            pl.BlockSpec((1, whole, 3 * D), lambda f: (f, 0, 0)),
        ],
        deps,
        grid=(frames,),
        out_specs=[block] * stripes + [pl.BlockSpec((1, 2, D), lambda f: (f, 0, 0))],
        out_shape=[jax.ShapeDtypeStruct((frames, rows, D), BF)] * stripes
        + [jax.ShapeDtypeStruct((frames, 2, D), F32)],
        scratch_shapes=[pltpu.VMEM((whole, D), F32)],
        name="space_norm",
    )
    return outs[:-1], outs[-1]


STEP = 4


def spots(i, g, rows_g):
    fs = pl.ds(i * STEP, STEP)
    at = pl.ds(pl.multiple_of(g * rows_g + i * STEP * 8, STEP * 8), STEP * 8)
    return fs, at


def as3(x):
    return x.reshape(STEP, 8, D)


def as2(x):
    return x.reshape(STEP * 8, D)


def over_patches(terms):
    total = terms[0]
    for t in terms[1:]:
        total = total + t
    return jnp.sum(total, 1, keepdims=True)


def bring(source, target, sem):
    copy = pltpu.make_async_copy(source, target, sem)
    copy.start()
    return copy


def onward_kernel(stripes, chunk, *refs):
    me_ref, bias_ref, mod_ref = refs[:3]
    a_refs = refs[3 : 3 + stripes]
    tok_ref, cot_ref = refs[3 + stripes : 5 + stripes]
    weight_refs = refs[5 + stripes : 10 + stripes]
    (
        mixed_ref,
        dmod_ref,
        lse_ref,
        att1_out,
        n2_out,
        att2_out,
        n3_out,
        dup_out,
        hid_out,
        db3_out,
        db2_out,
        first_out,
        b1_out,
        dsecond_out,
        qkv_out,
    ) = refs[10 + stripes : 25 + stripes]
    (
        wos,
        wqkv,
        wot,
        wu,
        wd,
        att1_ref,
        n2_ref,
        att2_ref,
        n3_ref,
        dup_ref,
        hid_ref,
        db3_ref,
        db2_ref,
        first_ref,
        b1_ref,
        second_ref,
        qkv_ref,
        nat_ref,
        b2_ref,
        b3_ref,
        dn_ref,
        in_sems,
        out_sems,
    ) = refs[25 + stripes :]
    frames, patches, _ = tok_ref.shape
    groups = patches // 8
    rows = frames * patches
    rows_g = frames * 8
    per = frames // stripes
    ff = wu.shape[1]
    me = me_ref[0]
    mask = first_head()
    held = (wos, wqkv, wot, wu, wd)
    loads = [bring(w, v, in_sems.at[n]) for n, (w, v) in enumerate(zip(weight_refs, held))]
    stores = []

    def send(source, target):
        stores.append(bring(source, target, out_sems.at[len(stores)]))

    for j in range(stripes):
        s = lax.bitwise_xor(me, j)
        start = pl.multiple_of(s * (per * patches), per * patches)
        low = chunk * patches if a_refs[j].shape[1] > patches else 0
        att1_ref[pl.ds(start, per * patches), :] = a_refs[j][:, low : low + patches, :].reshape(
            per * patches, D
        )
    send(att1_ref, att1_out)
    loads[0].wait()
    nat_ref[...] = mm(att1_ref[...], wos[...]).reshape(frames, patches, D)

    def stage_one(i, carry):
        for g in range(groups):
            fs, at = spots(i, g, rows_g)
            tok = tok_ref[fs].astype(F32)[:, 8 * g : 8 * g + 8]
            b1 = nat_ref[fs, 8 * g : 8 * g + 8, :]
            first = tok + mod_ref[fs, 2:3, :] * b1
            xhat, _ = norm_stats(first)
            n2 = xhat * (1.0 + mod_ref[fs, 4:5, :]) + mod_ref[fs, 3:4, :]
            b1_ref[at, :] = as2(b1)
            first_ref[at, :] = as2(first)
            n2_ref[at, :] = as2(n2).astype(BF)
        return carry

    lax.fori_loop(0, frames // STEP, stage_one, 0, unroll=8)
    send(b1_ref, b1_out)
    send(first_ref, first_out)
    send(n2_ref, n2_out)

    loads[1].wait()
    for s in range(3):
        qkv_ref[:, s * D : (s + 1) * D] = mm(n2_ref[...], wqkv[:, s * D : (s + 1) * D]).astype(BF)
    send(qkv_ref, qkv_out)

    def time_attend(g, carry):
        at = pl.ds(pl.multiple_of(g * rows_g, rows_g), rows_g)
        logs = []
        for h in range(PAIRS):
            q2, k2, v2 = (
                qkv_ref[at, s * D + h * 128 : s * D + (h + 1) * 128] for s in range(3)
            )
            att, log = attend_pair(q2, k2, v2, mask, bias_ref[...])
            logs.append(log)
            att2_ref[at, h * 128 : (h + 1) * 128] = att.astype(BF)
        lse_ref[g, 0:8, :], lse_ref[g, 8:16, :] = pair_rows(logs)
        return carry

    lax.fori_loop(0, groups, time_attend, 0)
    send(att2_ref, att2_out)
    loads[2].wait()
    b2_ref[...] = mm(att2_ref[...], wot[...])

    def stage_two(i, carry):
        for g in range(groups):
            fs, at = spots(i, g, rows_g)
            second = as3(first_ref[at, :]) + mod_ref[fs, 5:6, :] * as3(b2_ref[at, :])
            xhat, _ = norm_stats(second)
            n3 = xhat * (1.0 + mod_ref[fs, 7:8, :]) + mod_ref[fs, 6:7, :]
            cot = cot_ref[fs].astype(F32)[:, 8 * g : 8 * g + 8]
            second_ref[at, :] = as2(second)
            n3_ref[at, :] = as2(n3).astype(BF)
            db3_ref[at, :] = as2(mod_ref[fs, 8:9, :] * cot).astype(BF)
        return carry

    lax.fori_loop(0, frames // STEP, stage_two, 0, unroll=8)
    send(n3_ref, n3_out)
    send(db3_ref, db3_out)

    loads[3].wait()
    loads[4].wait()
    b3_ref[...] = jnp.zeros_like(b3_ref)
    dn_ref[...] = jnp.zeros_like(dn_ref)
    wide = FEED_COLS
    part = FEED_ROWS

    def feed(b, carry):
        cols = pl.ds(pl.multiple_of(b * wide, wide), wide)
        for r in range(rows // part):
            at = pl.ds(r * part, part)
            u = mm(n3_ref[at, :], wu[:, cols])
            dh = mm_nt(db3_ref[at, :], wd[cols, :])
            u2 = u * u
            t = jnp.tanh(u * (GELU_C + (GELU_C * GELU_A) * u2))
            half = 0.5 + 0.5 * t
            slope = half + (0.5 * u) * ((1.0 - t * t) * (GELU_C + (3.0 * GELU_C * GELU_A) * u2))
            hid = (u * half).astype(BF)
            dup = (dh * slope).astype(BF)
            hid_ref[at, cols] = hid
            dup_ref[at, cols] = dup
            b3_ref[at, :] += mm(hid, wd[cols, :])
            dn_ref[at, :] += mm_nt(dup, wu[:, cols])
        return carry

    lax.fori_loop(0, ff // wide, feed, 0)
    send(hid_ref, hid_out)
    send(dup_ref, dup_out)

    def stage_three(i, carry):
        parts = [[] for _ in range(4)]
        for g in range(groups):
            fs, at = spots(i, g, rows_g)
            cot = cot_ref[fs].astype(F32)[:, 8 * g : 8 * g + 8]
            second = as3(second_ref[at, :])
            b3 = as3(b3_ref[at, :])
            dn = as3(dn_ref[at, :])
            xhat, rstd = norm_stats(second)
            dsecond = cot + norm_back(dn, xhat, rstd, mod_ref[fs, 7:8, :])
            nat_ref[fs, 8 * g : 8 * g + 8, :] = second + mod_ref[fs, 8:9, :] * b3
            second_ref[at, :] = as2(dsecond)
            db2_ref[at, :] = as2(mod_ref[fs, 5:6, :] * dsecond).astype(BF)
            for k, t in enumerate((dsecond * as3(b2_ref[at, :]), dn, dn * xhat, cot * b3)):
                parts[k].append(t)
        fs, _ = spots(i, 0, rows_g)
        for k in range(4):
            dmod_ref[fs, k : k + 1, :] = over_patches(parts[k])
        mixed_ref[fs] = nat_ref[fs].astype(BF)
        return carry

    lax.fori_loop(0, frames // STEP, stage_three, 0, unroll=8)
    send(second_ref, dsecond_out)
    send(db2_ref, db2_out)
    for copy in stores:
        copy.wait()


FEED_COLS = 1536
FEED_ROWS = 256


def onward(me, bias, modulation, attended, tokens, cotangent, weights, chunk=0, deps=()):
    stripes = len(attended)
    frames, patches, _ = tokens.shape
    rows = frames * patches
    ff = weights[3].shape[1]
    vmem, anywhere = pl.BlockSpec(memory_space=pltpu.VMEM), pl.BlockSpec(memory_space=pl.ANY)
    kept = [(D, BF), (D, BF), (D, BF), (D, BF), (ff, BF), (ff, BF), (D, BF), (D, BF)]
    kept += [(D, F32), (D, F32), (D, F32), (3 * D, BF)]
    outs = call(
        partial(onward_kernel, stripes, chunk),
        (me, bias, modulation, *attended, tokens, cotangent, *weights),
        [pl.BlockSpec(memory_space=pltpu.SMEM)] + [vmem] * (4 + stripes) + [anywhere] * 5,
        deps,
        out_specs=[vmem] * 3 + [anywhere] * len(kept),
        out_shape=[
            jax.ShapeDtypeStruct((frames, patches, D), BF),
            jax.ShapeDtypeStruct((frames, 4, D), F32),
            jax.ShapeDtypeStruct((patches // 8, 16, frames * 8), F32),
        ]
        + [jax.ShapeDtypeStruct((rows, cols), kind) for cols, kind in kept],
        scratch_shapes=[pltpu.VMEM(w.shape, BF) for w in weights]
        + [pltpu.VMEM((rows, cols), kind) for cols, kind in kept]
        + [pltpu.VMEM((frames, patches, D), F32)]
        + [pltpu.VMEM((rows, D), F32)] * 3
        + [pltpu.SemaphoreType.DMA((5,)), pltpu.SemaphoreType.DMA((len(kept),))],
        name="onward",
    )
    names = ("mixed", "dmod", "lse", "att1", "n2", "att2", "n3", "dup", "hid", "db3")
    names += ("db2", "first", "b1", "dsecond", "qkv")
    return dict(zip(names, outs))


def time_back_kernel(stripes, frames, last, *refs):
    me_ref, bias_ref, mod_ref, qkv_ref, db2_ref, att2_ref, lse_ref = refs[:7]
    late_ins, weight_refs = refs[7:10], refs[10:13]
    others = refs[13 : 13 + (NEAR + 3 if last else 0)]
    refs = refs[13 + len(others) :]
    dfirst_ref, dmod_ref = refs[:2]
    datt_refs = refs[2 : 2 + stripes]
    dqkv_out, db1_out = refs[2 + stripes : 4 + stripes]
    (
        first_ref,
        b1_ref,
        dsecond_ref,
        wqkv,
        wot,
        wos,
        dqkv_ref,
        db1_ref,
        nat_ref,
        dn_ref,
        do_ref,
        sums_ref,
        in_sems,
        out_sems,
    ) = refs[4 + stripes :]
    patches = nat_ref.shape[1]
    groups = patches // 8
    rows_g = frames * 8
    per = frames // stripes
    me = me_ref[0]
    mask = first_head()
    held = (wot, wqkv, first_ref, b1_ref, dsecond_ref, wos)
    sources = (weight_refs[1], weight_refs[0]) + tuple(late_ins) + (weight_refs[2],)
    loads = [bring(w, v, in_sems.at[n]) for n, (w, v) in enumerate(zip(sources, held))]
    loads[0].wait()
    do_ref[...] = mm_nt(db2_ref[...], wot[...]).astype(BF)

    def attend_back(g, carry):
        at = pl.ds(pl.multiple_of(g * rows_g, rows_g), rows_g)
        inner = head_sums(att2_ref[at, :], do_ref[at, :])
        for h in range(PAIRS):
            q2, k2, v2 = (
                qkv_ref[at, s * D + h * 128 : s * D + (h + 1) * 128] for s in range(3)
            )
            do2 = do_ref[at, h * 128 : (h + 1) * 128]
            lse = [lse_ref[g, n : n + 1, :] for n in (h, 8 + h)]
            sums = [inner[n : n + 1] for n in (h, 8 + h)]
            grads = attend_pair_back(q2, k2, v2, do2, lse, sums, mask, bias_ref[...])
            for s in range(3):
                dqkv_ref[at, s * D + h * 128 : s * D + (h + 1) * 128] = grads[s].astype(BF)
        return carry

    lax.fori_loop(0, groups, attend_back, 0)
    stores = [bring(dqkv_ref, dqkv_out, out_sems.at[0])]
    for copy in loads[1:]:
        copy.wait()
    dn_ref[...] = mm_nt(dqkv_ref[...], wqkv[...])

    def stage_four(i, carry):
        parts = [[] for _ in range(3)]
        for g in range(groups):
            fs, at = spots(i, g, rows_g)
            dn = as3(dn_ref[at, :])
            xhat, rstd = norm_stats(as3(first_ref[at, :]))
            dfirst = as3(dsecond_ref[at, :]) + norm_back(dn, xhat, rstd, mod_ref[fs, 4:5, :])
            nat_ref[fs, 8 * g : 8 * g + 8, :] = dfirst
            for k, t in enumerate((dfirst * as3(b1_ref[at, :]), dn, dn * xhat)):
                parts[k].append(t)
        fs, _ = spots(i, 0, rows_g)
        for k in range(3):
            dmod_ref[fs, k : k + 1, :] = over_patches(parts[k])
        dfirst = nat_ref[fs]
        dfirst_ref[fs] = dfirst.astype(BF)
        span = STEP * patches
        db1_ref[pl.ds(pl.multiple_of(i * span, span), span), :] = (
            (mod_ref[fs, 2:3, :] * dfirst).astype(BF).reshape(span, D)
        )
        return carry

    lax.fori_loop(0, frames // STEP, stage_four, 0, unroll=8)
    stores.append(bring(db1_ref, db1_out, out_sems.at[1]))
    nat_ref[...] = mm_nt(db1_ref[...], wos[...]).reshape(frames, patches, D)
    if last:
        back, one, two = others[NEAR:]
        sums_ref[:, 0:3, :] = dmod_ref[...] + back[...]
        sums_ref[:, 3:7, :] = one[...] + two[...]
        sums_ref[:, 7:8, :] = jnp.zeros((frames, 1, D), F32)
    for j in range(stripes):
        s = lax.bitwise_xor(me, j)
        mine = nat_ref[pl.ds(s * per, per)].astype(BF)
        if last:
            width = patches
            if j < NEAR:
                width = 2 * patches
                for f in range(per):
                    datt_refs[j][f * width : f * width + patches, :] = others[j][
                        f * patches : (f + 1) * patches, :
                    ]
                    datt_refs[j][f * width + patches : (f + 1) * width, :] = mine[f]
            else:
                datt_refs[j][: per * patches, :] = mine.reshape(per * patches, D)
            datt_refs[j][per * width :, :] = sums_ref[pl.ds(s * per, per)].reshape(
                per * 8, D
            ).astype(BF)
        else:
            datt_refs[j][...] = mine.reshape(per * patches, D)
    for copy in stores:
        copy.wait()


def time_back(me, bias, modulation, onward_outs, weights, stripes, others=(), deps=()):
    o = onward_outs
    frames, patches, _ = o["mixed"].shape
    rows = frames * patches
    per = frames // stripes
    last = bool(others)
    vmem, anywhere = pl.BlockSpec(memory_space=pltpu.VMEM), pl.BlockSpec(memory_space=pl.ANY)
    bf = lambda *shape: jax.ShapeDtypeStruct(shape, BF)
    sends = [
        bf(per * (patches * (2 if j < NEAR else 1) + 8) if last else per * patches, D)
        for j in range(stripes)
    ]
    outs = call(
        partial(time_back_kernel, stripes, frames, last),
        (me, bias, modulation, o["qkv"], o["db2"], o["att2"], o["lse"], o["first"], o["b1"])
        + (o["dsecond"], *weights, *others),
        [pl.BlockSpec(memory_space=pltpu.SMEM)] + [vmem] * 6 + [anywhere] * 6 + [vmem] * len(others),
        deps,
        out_specs=[vmem] * (2 + stripes) + [anywhere] * 2,
        out_shape=[bf(frames, patches, D), jax.ShapeDtypeStruct((frames, 3, D), F32)]
        + sends
        + [bf(rows, 3 * D), bf(rows, D)],
        scratch_shapes=[pltpu.VMEM((rows, D), F32)] * 3
        + [pltpu.VMEM(w.shape, BF) for w in weights]
        + [
            pltpu.VMEM((rows, 3 * D), BF),
            pltpu.VMEM((rows, D), BF),
            pltpu.VMEM((frames, patches, D), F32),
            pltpu.VMEM((rows, D), F32),
            pltpu.VMEM((rows, D), BF),
            pltpu.VMEM((frames, 8, D), F32),
            pltpu.SemaphoreType.DMA((6,)),
            pltpu.SemaphoreType.DMA((2,)),
        ],
        name="time_back",
    )
    return dict(
        dfirst=outs[0], dmod_back=outs[1], sends=outs[2 : 2 + stripes], dqkv=outs[-2], db1=outs[-1]
    )


def finish_kernel(stripes, chunks, me_ref, *refs):
    dv_refs = refs[:stripes]
    first_refs = refs[stripes : stripes + chunks]
    out_ref = refs[-1]
    per = dv_refs[0].shape[0]
    part = first_refs[0].shape[1]
    for j in range(stripes):
        fs = pl.ds(lax.bitwise_xor(me_ref[0], j) * per, per)
        for c in range(chunks):
            spot = pl.ds(c * part, part)
            out_ref[fs, spot, :] = (
                dv_refs[j][:, spot, :].astype(F32) + first_refs[c][fs].astype(F32)
            ).astype(BF)


def finish(me, dvs, firsts, deps=()):
    stripes, chunks = len(dvs), len(firsts)
    frames, part, _ = firsts[0].shape
    vmem = pl.BlockSpec(memory_space=pltpu.VMEM)
    return call(
        partial(finish_kernel, stripes, chunks),
        (me, *dvs, *firsts),
        [pl.BlockSpec(memory_space=pltpu.SMEM)] + [vmem] * (stripes + chunks),
        deps,
        out_specs=vmem,
        out_shape=jax.ShapeDtypeStruct((frames, part * chunks, D), BF),
        name="finish",
    )


def flip(x, axis, bit):
    size = lax.axis_size(axis)
    return lax.ppermute(x, axis, [(i, i ^ bit) for i in range(size)])


def exchange(blocks):
    return [blocks[0]] + [flip(blocks[j], "blk", j) for j in range(1, len(blocks))]


def double(x, axis, bit, dim):
    own = (lax.axis_index(axis) // bit) % 2
    got = flip(x, axis, bit)
    low = jnp.where(own == 0, x, got)
    high = jnp.where(own == 0, got, x)
    return jnp.concatenate([low, high], dim)


def bits_of(size):
    return [1 << b for b in range(size.bit_length() - 1)]


def weight_grad_kernel(pairs, by_rows, held, bit_ref, *refs):
    a_refs, b_refs = refs[:pairs], refs[pairs : 2 * pairs]
    keep_ref, *send_refs, total_ref = refs[2 * pairs + held :]
    total = mm_tn(a_refs[0][...], b_refs[0][...])
    for a, b in zip(a_refs[1:], b_refs[1:]):
        total = total + mm_tn(a[...], b[...])
    total_ref[...] = total.reshape(total_ref.shape)
    bit = bit_ref[0]
    if by_rows:
        keep_ref[...] = total_ref[:, :, bit].astype(BF)
        send_refs[0][...] = total_ref[:, :, 1 - bit].astype(BF)
    else:
        keep_ref[:, 0] = total_ref[:, bit].astype(BF)
        deep = send_refs[0].shape[0]
        for n, send_ref in enumerate(send_refs):
            send_ref[:, 0] = total_ref[n * deep : (n + 1) * deep, 1 - bit].astype(BF)


def weight_grad(bit, firsts, seconds, stripes, units, at, held, deps=(), cuts=1):
    pairs = len(firsts)
    rows, cols = firsts[0].shape[1], seconds[0].shape[1]
    small = D // stripes
    half = small // 2
    by_rows = rows > D
    tall = D if cols % D == 0 else D // 2
    steps = rows // D if by_rows else cols // tall
    if by_rows:
        deep = rows // D
        wide = stripes // steps
        shape, spot = (wide, deep, half, D), lambda t: (t, at // deep, 0, 0)
        total = (wide, deep, 2, half, D)
    else:
        shape, spot = (stripes, 1, half, tall), lambda t: (0, at + t, 0, 0)
        total = (stripes, 2, half, tall)
    moving, still = (lambda t: (0, t)), (lambda t: (0, 0))
    block = pl.BlockSpec(shape, spot)
    send = pl.BlockSpec((shape[0] // cuts,) + shape[1:], spot)
    group = [jax.ShapeDtypeStruct((stripes, units, half, tall), BF)]
    group += [jax.ShapeDtypeStruct((stripes // cuts, units, half, tall), BF)] * cuts
    aliased = held is not None
    return call(
        partial(weight_grad_kernel, pairs, by_rows, 1 + cuts if aliased else 0),
        (bit, *firsts, *seconds, *(held or ())),
        [pl.BlockSpec(memory_space=pltpu.SMEM)]
        + [pl.BlockSpec((a.shape[0], D), moving if by_rows else still) for a in firsts]
        + [pl.BlockSpec((b.shape[0], tall), still if by_rows else moving) for b in seconds]
        + [ANYWHERE] * (1 + cuts if aliased else 0),
        deps,
        grid=(steps,),
        out_specs=[block] + [send] * cuts,
        scratch_shapes=[pltpu.VMEM(total, F32)],
        out_shape=group,
        input_output_aliases={2 * pairs + 1 + n: n for n in range(1 + cuts)} if aliased else {},
        name="weight_grad",
    )


def mod_grad_kernel(samples, *refs):
    g_refs, refs = refs[:samples], refs[samples:]
    w_ref, cond_ref, slope_ref, hit_ref, gw_ref, gb_ref, table_ref, g_ref, total_ref = refs
    step = pl.program_id(0)
    rows = w_ref.shape[0]

    @pl.when(step == 0)
    def _():
        at = 0
        for r in g_refs:
            g_ref[at : at + r.shape[0], :] = r[...]
            at += r.shape[0]
        for k in range(g_ref.shape[1] // D):
            cols = slice(k * D, (k + 1) * D)
            gw_ref[:, cols] = mm_tn(cond_ref[...], g_ref[:, cols])
            gb_ref[:, cols] = jnp.sum(g_ref[:, cols].astype(F32), 0, keepdims=True)

    total_ref[pl.ds(pl.multiple_of(step * rows, rows), rows), :] = mm_nt(w_ref[...], g_ref[...])

    @pl.when(step == pl.num_programs(0) - 1)
    def _():
        e = total_ref[...].T * slope_ref[...]
        high = e.astype(BF)
        low = (e - high.astype(F32)).astype(BF)
        table_ref[...] = mm(hit_ref[...], high) + mm(hit_ref[...], low)


def pack_kernel(first_ref, late_ref, out_ref):
    frames = first_ref.shape[0]
    for f in range(frames):
        both = [first_ref[f], late_ref[8 * f : 8 * f + 7, :]]
        out_ref[f] = jnp.concatenate(both, 0).astype(BF)


def pack(first_sums, late, deps):
    vmem = pl.BlockSpec(memory_space=pltpu.VMEM)
    frames = first_sums.shape[0]
    return call(
        pack_kernel,
        (first_sums, late),
        [vmem, vmem],
        deps,
        out_specs=vmem,
        out_shape=jax.ShapeDtypeStruct((frames, 9, D), BF),
        name="pack",
    )


def mod_grads(gs, weight, cond_own, slope, hit_own, deps):
    rows = slope.shape[0]
    still = lambda k: (0, 0)
    cols = weight.shape[1]
    each = 128
    wide, span = cond_own.shape[1], hit_own.shape[0]
    return call(
        partial(mod_grad_kernel, len(gs)),
        (*gs, weight, cond_own, slope, hit_own),
        [pl.BlockSpec((g.shape[0], cols), still) for g in gs]
        + [
            pl.BlockSpec((each, cols), lambda k: (k, 0)),
            pl.BlockSpec((rows, wide), still),
            pl.BlockSpec((rows, D), still),
            pl.BlockSpec((span, rows), still),
        ],
        deps,
        grid=(D // each,),
        out_specs=[
            pl.BlockSpec((wide, cols), still),
            pl.BlockSpec((1, cols), still),
            pl.BlockSpec((span, D), still),
        ],
        out_shape=[
            jax.ShapeDtypeStruct((wide, cols), F32),
            jax.ShapeDtypeStruct((1, cols), F32),
            jax.ShapeDtypeStruct((span, D), F32),
        ],
        scratch_shapes=[pltpu.VMEM((rows, cols), BF), pltpu.VMEM((D, rows), F32)],
        name="mod_grads",
    )


ORDER = (0, 2, 1, 3)


def of_four(x):
    across = flip(x, "dp", 2)
    return [x, across, flip(x, "dp", 1), flip(across, "dp", 1)]


def of_samples(x):
    if lax.axis_size("dp") == 4:
        return of_four(x)
    return [lax.all_gather(x, "dp", tiled=True)]


def add_split_kernel(cut, parts, bit_ref, keep_ref, *refs):
    got_refs, outs = refs[:parts], refs[parts:]
    bit = bit_ref[0]
    for out, side in zip(outs, (bit, 1 - bit)):
        if cut == "stripe":
            spot = (slice(None), side)
        else:
            half = keep_ref.shape[-1] // 2
            spot = (slice(None),) * 3 + (pl.ds(pl.multiple_of(side * half, half), half),)
        got = got_refs[0][spot].astype(F32)
        if parts == 2:
            low = pl.program_id(0) < pl.num_programs(0) // 2
            got = jnp.where(low, got, got_refs[1][spot].astype(F32))
        out[...] = (keep_ref[spot].astype(F32) + got).astype(BF)


def add_split(bit, keep, got, cut, deps=()):
    count, units, rows, cols = keep.shape
    parts = len(got)
    if cut == "stripe":
        keep, *got = (x.reshape(count // 2, 2, units, rows, cols) for x in (keep, *got))
        out = (count // 2, units, rows, cols)
        each = min(2, count // 2)
        steps = count // 2 // each
        in_spec = pl.BlockSpec((each, 2, units, rows, cols), lambda i: (i, 0, 0, 0, 0))
        got_specs = [in_spec]
        out_block = pl.BlockSpec((each, units, rows, cols), lambda i: (i, 0, 0, 0))
    else:
        each = 2
        steps = count // each
        out = (count, units, rows, cols // 2)
        shape = (each, units, rows, cols)
        in_spec = pl.BlockSpec(shape, lambda i: (i, 0, 0, 0))
        got_specs = [in_spec]
        if parts == 2:
            half = steps // 2
            got_specs = [
                pl.BlockSpec(shape, lambda i: (jnp.minimum(i, half - 1), 0, 0, 0)),
                pl.BlockSpec(shape, lambda i: (jnp.maximum(i - half, 0), 0, 0, 0)),
            ]
        out_block = pl.BlockSpec((each, units, rows, cols // 2), lambda i: (i, 0, 0, 0))
    return call(
        partial(add_split_kernel, cut, parts),
        (bit, keep, *got),
        [pl.BlockSpec(memory_space=pltpu.SMEM), in_spec, *got_specs],
        deps,
        grid=(steps,),
        out_specs=[out_block] * 2,
        out_shape=[jax.ShapeDtypeStruct(out, BF)] * 2,
        name="add_split",
    )


def assemble_kernel(layout, at_ref, *refs):
    shares, outs = refs[:4], refs[4:]
    half, cols = shares[0].shape[1:]
    for n, j in enumerate(ORDER):
        place = lax.bitwise_xor(at_ref[0], j)
        unit = 0
        for out, (deep, wide, halved) in zip(outs, layout):
            core, side = lax.rem(place, 2), lax.div(place, 2)
            if halved:
                core, side = side, core
            low = pl.multiple_of(core * half, half)
            step = cols if halved else 2 * cols
            left = pl.multiple_of(side * (wide * cols if halved else cols), cols)
            for r in range(deep):
                for c in range(wide):
                    out[pl.ds(r * 2 * half + low, half), pl.ds(c * step + left, cols)] = shares[n][
                        unit
                    ].astype(F32)
                    unit += 1


def assemble(at, shares, layout, deps):
    _, half, cols = shares[0].shape
    vmem = pl.BlockSpec(memory_space=pltpu.VMEM)
    return call(
        partial(assemble_kernel, layout),
        (at, *shares),
        [pl.BlockSpec(memory_space=pltpu.SMEM)] + [vmem] * 4,
        deps,
        out_specs=[vmem] * len(layout),
        out_shape=[
            jax.ShapeDtypeStruct((deep * 2 * half, wide * 2 * cols), F32)
            for deep, wide, _ in layout
        ],
        name="assemble",
    )


def bit_of(axis, bit):
    return ((lax.axis_index(axis) // bit) % 2).astype(jnp.int32).reshape(1)


def add_deal_kernel(groups, at_ref, *refs):
    keeps, gots, outs = refs[:groups], refs[groups : 2 * groups], refs[2 * groups :]
    for j, out in enumerate(outs):
        s = lax.bitwise_xor(at_ref[0], j)
        unit = 0
        for keep, got in zip(keeps, gots):
            n = keep.shape[1]
            out[unit : unit + n] = (keep[s].astype(F32) + got[s].astype(F32)).astype(BF)
            unit += n


def add_deal(at, keeps, gots, deps):
    vmem = pl.BlockSpec(memory_space=pltpu.VMEM)
    places, _, half, cols = keeps[0].shape
    units = sum(k.shape[1] for k in keeps)
    return call(
        partial(add_deal_kernel, len(keeps)),
        (at, *keeps, *gots),
        [pl.BlockSpec(memory_space=pltpu.SMEM)] + [vmem] * (2 * len(keeps)),
        deps,
        out_specs=[vmem] * places,
        out_shape=[jax.ShapeDtypeStruct((units, half, cols), BF)] * places,
        name="add_deal",
    )


def add_many_kernel(*refs):
    total = refs[0][...].astype(F32)
    for r in refs[1:-1]:
        total = total + r[...].astype(F32)
    refs[-1][...] = total.astype(BF)


def add_many(arrays, deps):
    vmem = pl.BlockSpec(memory_space=pltpu.VMEM)
    return call(
        add_many_kernel,
        tuple(arrays),
        [vmem] * len(arrays),
        deps,
        out_specs=vmem,
        out_shape=jax.ShapeDtypeStruct(arrays[0].shape, BF),
        name="add_many",
    )


class Reduction:
    def __init__(self, group, layout, halved=False):
        self.layout = [entry + (halved,) for entry in layout]
        bit = 2 if halved else 1
        self.states = [(group[0], [flip(send, "dp", bit) for send in group[1:]])]
        stripe_bits = bits_of(lax.axis_size("blk"))
        self.todo = [] if halved else [("dp", 2, "column")]
        self.todo += [("blk", bit, "stripe") for bit in stripe_bits]

    def step(self, deps=()):
        axis, bit, cut = self.todo.pop(0)
        keep, send = add_split(bit_of(axis, bit), *self.states[0], cut, deps)
        self.states = [(keep, [flip(send, axis, bit)])]
        return send

    def join(self, other):
        self.states += other.states
        self.layout += other.layout

    def deal(self, deps):
        at = (lax.axis_index("blk") // 2).astype(jnp.int32).reshape(1)
        keeps, gots = zip(*((keep, got[0]) for keep, got in self.states))
        sends = add_deal(at, keeps, gots, deps)
        self.states = [sends[0]] + [flip(x, "blk", 2 * j) for j, x in enumerate(sends) if j]
        self.todo = []
        return sends[0]

    def gather(self, deps):
        if isinstance(self.states[0], tuple):
            keep, (got,) = self.states[0]
            self.states = [keep[0], got[0]]
        share = add_many(self.states, deps)
        for bit in bits_of(lax.axis_size("dp"))[2:]:
            share = (share.astype(F32) + flip(share, "dp", bit).astype(F32)).astype(BF)
        self.states = of_four(share)
        return share

    def result(self, deps=()):
        at = (lax.axis_index("dp") % 4).astype(jnp.int32).reshape(1)
        return assemble(at, self.states, self.layout, deps)


def gather_frames(x):
    bits = bits_of(lax.axis_size("blk"))
    shape = x.shape
    x = x.reshape((1,) * len(bits) + shape)
    for n, bit in reversed(list(enumerate(bits))):
        x = double(x, "blk", bit, len(bits) - 1 - n)
    return x.reshape((-1,) + shape[1:])


def shards(
    tokens,
    frame_seg,
    clip_class,
    class_table,
    mod_weight,
    mod_bias,
    qkv_space,
    out_space,
    qkv_time,
    out_time,
    up_weight,
    down_weight,
    cotangent,
):
    stripes = lax.axis_size("blk")
    stripe = lax.axis_index("blk")
    me = stripe.astype(jnp.int32).reshape(1)
    tokens, cotangent = tokens[0], cotangent[0]
    frames, patches, _ = tokens.shape
    per = frames // stripes
    chunks = 2
    part = patches // chunks
    classes = class_table.shape[0]

    blocks = [
        lax.dynamic_slice_in_dim(tokens, (stripe ^ j) * per, per, 0) for j in range(stripes)
    ]
    blocks = exchange(blocks)

    segment = frame_seg[0]
    clip_ids = clip_class[0]
    clip_hit = segment[:, None] == jnp.arange(clip_ids.shape[0], dtype=jnp.int32)[None, :]
    frame_class = jnp.sum(jnp.where(clip_hit, clip_ids[None, :], 0), axis=1)

    def embed(class_of):
        hit = class_of[:, None] == jnp.arange(classes, dtype=jnp.int32)[None, :]
        return hit, jnp.dot(hit.astype(F32), class_table, precision=exact_mode)

    cond = jax.nn.silu(embed(frame_class)[1]).astype(BF)
    hit_all, embedded_all = embed(jnp.concatenate(of_samples(frame_class)))
    cond_all, silu_back = jax.vjp(jax.nn.silu, embedded_all)
    slope = silu_back(jnp.ones_like(cond_all))[0]
    width, span = D // stripes, classes // stripes
    cond_own = lax.dynamic_slice_in_dim(cond_all.astype(BF), stripe * width, width, 1)
    hit_own = lax.dynamic_slice_in_dim(hit_all.astype(BF).T, stripe * span, span, 0)
    modulation = jnp.dot(cond, mod_weight, preferred_element_type=F32) + mod_bias
    modulation = modulation.reshape(frames, 9, D)
    mod_own = lax.dynamic_slice_in_dim(modulation, stripe * per, per, 0)[:, :2]
    spot_frame = jnp.repeat(jnp.arange(frames), 8)
    spot_patch = jnp.tile(jnp.arange(8), frames)
    spot_seg = jnp.repeat(segment, 8)
    bias = jnp.where(
        (spot_seg[:, None] == spot_seg[None, :]) & (spot_patch[:, None] == spot_patch[None, :]),
        0.0,
        masked_score,
    ).astype(F32)

    core = bit_of("dp", 1)
    sends, normed_one, kept_one = space_forward(blocks, mod_own, qkv_space, chunks)
    attended = [sends[0]] + [
        flip(b, "blk", j) for b, (j, _, _) in list(zip(sends, pieces(stripes, patches, chunks)))[1:]
    ]
    normed_one = normed_one.reshape(-1, D)
    normed_pair = flip(normed_one, "dp", 1)
    weights = (out_space, qkv_time, out_time, up_weight, down_weight)
    parts = []
    for c in range(chunks):
        here = slice(c * part, (c + 1) * part)
        parts.append(
            onward(
                me,
                bias,
                modulation,
                chunk_of(attended, stripes, c),
                tokens[:, here],
                cotangent[:, here],
                weights,
                c,
                [parts[-1]["n3"], normed_pair] if parts else (),
            )
        )
    output = jnp.concatenate([p["mixed"] for p in parts], 1)

    def grad_into(held, units, at, first, second, deps=(), cuts=1):
        return weight_grad(
            core,
            [p[first] for p in parts],
            [p[second] for p in parts],
            stripes,
            units,
            at,
            held,
            deps,
            cuts,
        )

    deep, wide = up_weight.shape[1] // D, qkv_time.shape[1] // D
    group = grad_into(None, 2 * deep, 0, "n3", "dup")
    group = grad_into(group, 2 * deep, deep, "hid", "db3")
    feed = Reduction(group, ((1, deep), (deep, 1)))
    units = wide + 2
    group_time = grad_into(None, units, 0, "att2", "db2", [group[1]], 2)
    dep = group_time[1]
    back = (qkv_time, out_time, out_space)
    one, two = parts
    one.update(time_back(me, bias, modulation, one, back, stripes, (), [dep]))
    two.update(
        time_back(
            me,
            bias,
            modulation,
            two,
            back,
            stripes,
            [*one["sends"][:NEAR], one["dmod_back"], one["dmod"], two["dmod"]],
        )
    )
    far = [flip(one["sends"][j], "blk", j) for j in range(NEAR, stripes)]
    rest = exchange(two["sends"])
    grads = rest[:NEAR] + far + rest[NEAR:]
    dep = feed.step([two["db1"], *far])
    group = grad_into(group_time, units, 1, "n2", "dqkv", [dep], 2)
    group = grad_into(group, units, wide + 1, "att1", "db1", rest[5:], 2)
    time = Reduction(group, ((1, 1), (1, wide), (1, 1)))
    dqkv_one, dqkv_own, dqkv_pair, late = space_backward(
        core, grads, kept_one, stripes, chunks, [group[1]]
    )
    dqkv_pair = flip(dqkv_pair, "dp", 1)
    dep = feed.step([late])
    dep = time.step([dep])
    group = weight_grad(
        bit_of("dp", 2),
        [normed_one, normed_pair],
        [dqkv_own, dqkv_pair],
        stripes,
        wide,
        0,
        None,
        [dep],
    )
    space = Reduction(group, ((1, wide),), True)
    dvs, first_sums = space_norm(blocks, mod_own, qkv_space, dqkv_one, [group[1]])
    dvs = exchange(dvs)
    dep = feed.step([first_sums])
    dep = time.step([dep, *dvs[6:8]])
    dep = space.step([dep, *dvs[4:6]])
    dep = feed.step([dep])
    time.join(space)
    dep = time.deal([dep])
    mod_grad = pack(first_sums, late, [dep]).reshape(per, 9 * D)
    mod_grad = gather_frames(mod_grad)
    dep = feed.gather([mod_grad])
    mod_grad = of_samples(mod_grad)
    input_grad = finish(me, dvs, [p["dfirst"] for p in parts], [dep])
    grad_mod_weight, grad_mod_bias, grad_table = mod_grads(
        mod_grad, mod_weight, cond_own, slope, hit_own, [input_grad]
    )
    share = mod_bias.shape[0] // stripes
    grad_mod_bias = lax.dynamic_slice_in_dim(grad_mod_bias.reshape(-1), stripe * share, share, 0)
    time.gather([grad_table])
    grad_up, grad_down = feed.result()
    grad_out_time, grad_qkv_time, grad_out_space, grad_qkv_space = time.result()
    return (
        output[None],
        input_grad[None],
        grad_table,
        grad_mod_weight,
        grad_mod_bias,
        grad_qkv_space,
        grad_out_space,
        grad_qkv_time,
        grad_out_time,
        grad_up,
        grad_down,
    )


def solution(mesh):
    tile = P("dp", None, "blk", None)
    row = P("blk", None)
    in_specs = (tile, P("dp", None), P("dp", None)) + (P(),) * 9 + (tile,)
    out_specs = (tile, tile, row, row, P("blk")) + (row,) * 6
    return jax.shard_map(shards, mesh=mesh, in_specs=in_specs, out_specs=out_specs, check_vma=False)
```

```python
from functools import partial

import jax
import jax.numpy as jnp
from jax import lax
from jax.experimental import pallas as pl
from jax.experimental.pallas import tpu as pltpu
from jax.sharding import PartitionSpec as P

HEADS = 12
HEAD_DIM = 64
D = HEADS * HEAD_DIM
PAIRS = HEADS // 2
BF = jnp.bfloat16
F32 = jnp.float32
exact_mode = lax.Precision.HIGHEST
masked_score = -1e30
EPS = 1e-6
GELU_C = 0.7978845608028654
GELU_A = 0.044715
VMEM_LIMIT = 60 * 1024 * 1024


def mm(a, b):
    return lax.dot_general(a, b, (((1,), (0,)), ((), ())), preferred_element_type=F32)


def mm_nt(a, b):
    return lax.dot_general(a, b, (((1,), (1,)), ((), ())), preferred_element_type=F32)


def mm_tn(a, b):
    return lax.dot_general(a, b, (((0,), (0,)), ((), ())), preferred_element_type=F32)


CHEAP = pl.CostEstimate(flops=1, bytes_accessed=1, transcendentals=0)
ANYWHERE = pl.BlockSpec(memory_space=pl.ANY)


def call(kernel, operands, in_specs, deps=(), **options):
    inputs, extra = len(operands), len(deps)

    def body(*refs):
        kernel(*refs[:inputs], *refs[inputs + extra :])

    return pl.pallas_call(
        body,
        in_specs=list(in_specs) + [ANYWHERE] * extra,
        compiler_params=pltpu.CompilerParams(vmem_limit_bytes=VMEM_LIMIT),
        cost_estimate=CHEAP,
        **options,
    )(*operands, *deps)


def first_head():
    return lax.broadcasted_iota(jnp.int32, (1, 2 * HEAD_DIM), 1) < HEAD_DIM


def norm_stats(x):
    mean = jnp.mean(x, -1, keepdims=True)
    xc = x - mean
    var = jnp.mean(xc * xc, -1, keepdims=True)
    rstd = lax.rsqrt(var + EPS)
    return xc * rstd, rstd


def norm_back(dn, xhat, rstd, scale):
    e = dn * (1.0 + scale)
    return rstd * (
        e - jnp.mean(e, -1, keepdims=True) - xhat * jnp.mean(e * xhat, -1, keepdims=True)
    )


def attend_pair(q2, k2, v2, mask, bias):
    zero, one = jnp.zeros_like(q2), jnp.ones_like(v2)
    scaled = q2 * jnp.asarray(0.125, BF)

    def head(q, v):
        s = mm_nt(q, k2)
        if bias is not None:
            s = s + bias
        top = jnp.max(s, -1, keepdims=True)
        return mm(jnp.exp(s - top).astype(BF), v), top

    ra, ma = head(jnp.where(mask, scaled, zero), jnp.where(mask, v2, one))
    rb, mb = head(jnp.where(mask, zero, scaled), jnp.where(mask, one, v2))
    total = pltpu.roll(jnp.where(mask, rb, ra), HEAD_DIM, 1)
    return jnp.where(mask, ra, rb) / total, jnp.where(mask, ma, mb) + jnp.log(total)


def pair_rows(logs):
    lane = lax.broadcasted_iota(jnp.int32, (1, 2 * HEAD_DIM), 1) % HEAD_DIM
    both = logs[0]
    for h in range(1, PAIRS):
        both = jnp.where(lane == h, logs[h], both)
    both = both.T
    return both[:8], both[HEAD_DIM : HEAD_DIM + 8]


def head_sums(att, datt):
    prod = (att.astype(F32) * datt.astype(F32)).astype(BF)
    shape = (16, D)
    row, feature = (lax.broadcasted_iota(jnp.int32, shape, n) for n in (0, 1))
    hit = feature // HEAD_DIM == row % 8 * 2 + row // 8
    return mm_nt(jnp.where(hit, 1.0, 0.0).astype(BF), prod)


def attend_pair_back(q2, k2, v2, do2, lse, inner, mask, bias):
    zero = jnp.zeros_like(q2)
    scaled = q2 * jnp.asarray(0.125, BF)

    def head(q, do, n):
        s = mm_nt(k2, q)
        if bias is not None:
            s = s + bias
        p = jnp.exp(s - lse[n])
        ds = p * (mm_nt(v2, do) - inner[n])
        return p.astype(BF), ds.astype(BF)

    qa, qb = jnp.where(mask, scaled, zero), jnp.where(mask, zero, scaled)
    da, db = jnp.where(mask, do2, zero), jnp.where(mask, zero, do2)
    ka, kb = jnp.where(mask, k2, zero), jnp.where(mask, zero, k2)
    pa, dsa = head(qa, da, 0)
    pb, dsb = head(qb, db, 1)
    dv2 = mm(pa, da) + mm(pb, db)
    dk2 = mm(dsa, qa) + mm(dsb, qb)
    if DQ_FORM == 0:
        dq2 = 0.125 * (mm_tn(dsa, ka) + mm_tn(dsb, kb))
    else:
        dq2 = 0.125 * (mm_tn(ka, dsa) + mm_tn(kb, dsb)).T
    return dq2, dk2, dv2


DQ_FORM = 1


NEAR = 4


def pieces(stripes, rows, chunks):
    part = rows // chunks
    out = [(j, 0, rows) for j in range(NEAR)]
    for c in range(chunks):
        out += [(j, c * part, (c + 1) * part) for j in range(NEAR, stripes)]
    return out


def chunk_of(blocks, stripes, c):
    far = stripes - NEAR
    return list(blocks[:NEAR]) + list(blocks[NEAR + c * far : NEAR + (c + 1) * far])


def space_forward_kernel(stripes, chunks, *refs):
    x_refs = refs[:stripes]
    mod_ref, w_ref = refs[stripes : stripes + 2]
    att_refs = refs[stripes + 2 : -4]
    n1_ref, qkv_ref, att_ref, lse_ref = refs[-4:]
    rows = x_refs[0].shape[1]
    part = rows // chunks
    for j in range(stripes):
        x = x_refs[j][0].astype(F32)
        xhat, _ = norm_stats(x)
        n1_ref[0, j * rows : (j + 1) * rows, :] = (
            xhat * (1.0 + mod_ref[0, 1:2, :]) + mod_ref[0, 0:1, :]
        ).astype(BF)
    for s in range(3):
        qkv_ref[0, :, s * D : (s + 1) * D] = mm(
            n1_ref[0], w_ref[:, s * D : (s + 1) * D]
        ).astype(BF)
    mask = first_head()
    logs = []
    for h in range(PAIRS):
        q2, k2, v2 = (
            qkv_ref[0, :, s * D + h * 128 : s * D + (h + 1) * 128] for s in range(3)
        )
        att, log = attend_pair(q2, k2, v2, mask, None)
        logs.append(log)
        att = att.astype(BF)
        att_ref[0, :, h * 128 : (h + 1) * 128] = att
        for out, (j, low, high) in zip(att_refs, pieces(stripes, rows, chunks)):
            out[0, :, h * 128 : (h + 1) * 128] = att[j * rows + low : j * rows + high]
    lse_ref[0, 0:8, :], lse_ref[0, 8:16, :] = pair_rows(logs)


def space_forward(blocks, mod_own, weight, chunks):
    stripes = len(blocks)
    frames, rows, _ = blocks[0].shape
    whole = rows * stripes
    sizes = [high - low for _, low, high in pieces(stripes, rows, chunks)] + [whole]
    outs = call(
        partial(space_forward_kernel, stripes, chunks),
        (*blocks, mod_own, weight),
        [pl.BlockSpec((1, rows, D), lambda f: (f, 0, 0))] * stripes
        + [
            pl.BlockSpec((1,) + mod_own.shape[1:], lambda f: (f, 0, 0)),
            pl.BlockSpec(weight.shape, lambda f: (0, 0)),
        ],
        grid=(frames,),
        out_specs=[pl.BlockSpec((1, n, D), lambda f: (f, 0, 0)) for n in sizes]
        + [
            pl.BlockSpec((1, whole, 3 * D), lambda f: (f, 0, 0)),
            pl.BlockSpec((1, whole, D), lambda f: (f, 0, 0)),
            pl.BlockSpec((1, 16, whole), lambda f: (f, 0, 0)),
        ],
        out_shape=[jax.ShapeDtypeStruct((frames, n, D), BF) for n in sizes]
        + [
            jax.ShapeDtypeStruct((frames, whole, 3 * D), BF),
            jax.ShapeDtypeStruct((frames, whole, D), BF),
            jax.ShapeDtypeStruct((frames, 16, whole), F32),
        ],
        name="space_forward",
    )
    return outs[:-4], outs[-4], outs[-3:]


def space_backward_kernel(stripes, rows, chunks, *refs):
    place = pieces(stripes, rows, chunks)
    d_refs, refs = refs[: len(place)], refs[len(place) :]
    sum_refs, refs = refs[:stripes], refs[stripes:]
    core_ref, qkv_ref, att_ref, lse_ref, dqkv_ref, keep_ref, send_ref, late_ref, datt_ref = refs
    for d_ref, (j, low, high) in zip(d_refs, place):
        datt_ref[j * rows + low : j * rows + high, :] = d_ref[...]

    @pl.when(pl.program_id(0) == 0)
    def _():
        late = sum_refs[0][...].astype(F32)
        for r in sum_refs[1:]:
            late = late + r[...].astype(F32)
        late_ref[...] = late

    mask = first_head()
    inner = head_sums(att_ref[0], datt_ref[...])
    for h in range(PAIRS):
        q2, k2, v2 = (
            qkv_ref[0, :, s * D + h * 128 : s * D + (h + 1) * 128] for s in range(3)
        )
        do2 = datt_ref[:, h * 128 : (h + 1) * 128]
        lse = [lse_ref[0, n : n + 1, :] for n in (h, 8 + h)]
        sums = [inner[n : n + 1] for n in (h, 8 + h)]
        grads = attend_pair_back(q2, k2, v2, do2, lse, sums, mask, None)
        for s in range(3):
            dqkv_ref[0, :, s * D + h * 128 : s * D + (h + 1) * 128] = grads[s].astype(BF)
    half = dqkv_ref.shape[-1] // 2
    for ref, side in ((keep_ref, core_ref[0]), (send_ref, 1 - core_ref[0])):
        ref[...] = dqkv_ref[0, :, pl.ds(pl.multiple_of(side * half, half), half)]


def space_backward(core, grads, kept, stripes, chunks, deps):
    frames, whole, _ = kept[0].shape
    rows = whole // stripes
    extra = frames * 8
    place = pieces(stripes, rows, chunks)
    last = list(grads[:NEAR]) + list(grads[NEAR - stripes :])
    half = pl.BlockSpec((whole, 3 * D // 2), lambda f: (f, 0))
    return call(
        partial(space_backward_kernel, stripes, rows, chunks),
        (*grads, *last, core, *kept),
        [pl.BlockSpec((high - low, D), lambda f: (f, 0)) for _, low, high in place]
        + [
            pl.BlockSpec((extra, D), lambda f, n=g.shape[0] // extra - 1: (n, 0)) for g in last
        ]
        + [
            pl.BlockSpec(memory_space=pltpu.SMEM),
            pl.BlockSpec((1, whole, 3 * D), lambda f: (f, 0, 0)),
            pl.BlockSpec((1, whole, D), lambda f: (f, 0, 0)),
            pl.BlockSpec((1, 16, whole), lambda f: (f, 0, 0)),
        ],
        deps,
        grid=(frames,),
        out_specs=[
            pl.BlockSpec((1, whole, 3 * D), lambda f: (f, 0, 0)),
            half,
            half,
            pl.BlockSpec((extra, D), lambda f: (0, 0)),
        ],
        out_shape=[
            jax.ShapeDtypeStruct((frames, whole, 3 * D), BF),
            jax.ShapeDtypeStruct((frames * whole, 3 * D // 2), BF),
            jax.ShapeDtypeStruct((frames * whole, 3 * D // 2), BF),
            jax.ShapeDtypeStruct((extra, D), F32),
        ],
        scratch_shapes=[pltpu.VMEM((whole, D), BF)],
        name="space_backward",
    )


def space_norm_kernel(stripes, *refs):
    x_refs, (mod_ref, w_ref, dqkv_ref), refs = refs[:stripes], refs[stripes : stripes + 3], refs[stripes + 3 :]
    dv_refs, dmod_ref, dn_ref = refs[:stripes], refs[stripes], refs[stripes + 1]
    rows = x_refs[0].shape[1]
    dn_ref[...] = mm_nt(dqkv_ref[0], w_ref[...])
    shift_sum = jnp.zeros((1, D), F32)
    scale_sum = jnp.zeros((1, D), F32)
    for j in range(stripes):
        xhat, rstd = norm_stats(x_refs[j][0].astype(F32))
        d = dn_ref[j * rows : (j + 1) * rows, :]
        dv_refs[j][0] = norm_back(d, xhat, rstd, mod_ref[0, 1:2, :]).astype(BF)
        shift_sum = shift_sum + jnp.sum(d, 0, keepdims=True)
        scale_sum = scale_sum + jnp.sum(d * xhat, 0, keepdims=True)
    dmod_ref[0, 0:1, :] = shift_sum
    dmod_ref[0, 1:2, :] = scale_sum


def space_norm(blocks, mod_own, weight, dqkv, deps):
    stripes = len(blocks)
    frames, rows, _ = blocks[0].shape
    whole = rows * stripes
    block = pl.BlockSpec((1, rows, D), lambda f: (f, 0, 0))
    outs = call(
        partial(space_norm_kernel, stripes),
        (*blocks, mod_own, weight, dqkv),
        [block] * stripes
        + [
            pl.BlockSpec((1,) + mod_own.shape[1:], lambda f: (f, 0, 0)),
            pl.BlockSpec(weight.shape, lambda f: (0, 0)),
            pl.BlockSpec((1, whole, 3 * D), lambda f: (f, 0, 0)),
        ],
        deps,
        grid=(frames,),
        out_specs=[block] * stripes + [pl.BlockSpec((1, 2, D), lambda f: (f, 0, 0))],
        out_shape=[jax.ShapeDtypeStruct((frames, rows, D), BF)] * stripes
        + [jax.ShapeDtypeStruct((frames, 2, D), F32)],
        scratch_shapes=[pltpu.VMEM((whole, D), F32)],
        name="space_norm",
    )
    return outs[:-1], outs[-1]


STEP = 4


def spots(i, g, rows_g):
    fs = pl.ds(i * STEP, STEP)
    at = pl.ds(pl.multiple_of(g * rows_g + i * STEP * 8, STEP * 8), STEP * 8)
    return fs, at


def as3(x):
    return x.reshape(STEP, 8, D)


def as2(x):
    return x.reshape(STEP * 8, D)


def over_patches(terms):
    total = terms[0]
    for t in terms[1:]:
        total = total + t
    return jnp.sum(total, 1, keepdims=True)


def bring(source, target, sem):
    copy = pltpu.make_async_copy(source, target, sem)
    copy.start()
    return copy


def onward_kernel(stripes, chunk, *refs):
    me_ref, bias_ref, mod_ref = refs[:3]
    a_refs = refs[3 : 3 + stripes]
    tok_ref, cot_ref = refs[3 + stripes : 5 + stripes]
    weight_refs = refs[5 + stripes : 10 + stripes]
    (
        mixed_ref,
        dmod_ref,
        lse_ref,
        att1_out,
        n2_out,
        att2_out,
        n3_out,
        dup_out,
        hid_out,
        db3_out,
        db2_out,
        first_out,
        b1_out,
        dsecond_out,
        qkv_out,
    ) = refs[10 + stripes : 25 + stripes]
    (
        wos,
        wqkv,
        wot,
        wu,
        wd,
        att1_ref,
        n2_ref,
        att2_ref,
        n3_ref,
        dup_ref,
        hid_ref,
        db3_ref,
        db2_ref,
        first_ref,
        b1_ref,
        second_ref,
        qkv_ref,
        nat_ref,
        b2_ref,
        b3_ref,
        dn_ref,
        in_sems,
        out_sems,
    ) = refs[25 + stripes :]
    frames, patches, _ = tok_ref.shape
    groups = patches // 8
    rows = frames * patches
    rows_g = frames * 8
    per = frames // stripes
    ff = wu.shape[1]
    me = me_ref[0]
    mask = first_head()
    held = (wos, wqkv, wot, wu, wd)
    loads = [bring(w, v, in_sems.at[n]) for n, (w, v) in enumerate(zip(weight_refs, held))]
    stores = []

    def send(source, target):
        stores.append(bring(source, target, out_sems.at[len(stores)]))

    for j in range(stripes):
        s = lax.bitwise_xor(me, j)
        start = pl.multiple_of(s * (per * patches), per * patches)
        low = chunk * patches if a_refs[j].shape[1] > patches else 0
        att1_ref[pl.ds(start, per * patches), :] = a_refs[j][:, low : low + patches, :].reshape(
            per * patches, D
        )
    send(att1_ref, att1_out)
    loads[0].wait()
    nat_ref[...] = mm(att1_ref[...], wos[...]).reshape(frames, patches, D)

    def stage_one(i, carry):
        for g in range(groups):
            fs, at = spots(i, g, rows_g)
            tok = tok_ref[fs].astype(F32)[:, 8 * g : 8 * g + 8]
            b1 = nat_ref[fs, 8 * g : 8 * g + 8, :]
            first = tok + mod_ref[fs, 2:3, :] * b1
            xhat, _ = norm_stats(first)
            n2 = xhat * (1.0 + mod_ref[fs, 4:5, :]) + mod_ref[fs, 3:4, :]
            b1_ref[at, :] = as2(b1)
            first_ref[at, :] = as2(first)
            n2_ref[at, :] = as2(n2).astype(BF)
        return carry

    lax.fori_loop(0, frames // STEP, stage_one, 0, unroll=8)
    send(b1_ref, b1_out)
    send(first_ref, first_out)
    send(n2_ref, n2_out)

    loads[1].wait()
    for s in range(3):
        qkv_ref[:, s * D : (s + 1) * D] = mm(n2_ref[...], wqkv[:, s * D : (s + 1) * D]).astype(BF)
    send(qkv_ref, qkv_out)

    def time_attend(g, carry):
        at = pl.ds(pl.multiple_of(g * rows_g, rows_g), rows_g)
        logs = []
        for h in range(PAIRS):
            q2, k2, v2 = (
                qkv_ref[at, s * D + h * 128 : s * D + (h + 1) * 128] for s in range(3)
            )
            att, log = attend_pair(q2, k2, v2, mask, bias_ref[...])
            logs.append(log)
            att2_ref[at, h * 128 : (h + 1) * 128] = att.astype(BF)
        lse_ref[g, 0:8, :], lse_ref[g, 8:16, :] = pair_rows(logs)
        return carry

    lax.fori_loop(0, groups, time_attend, 0)
    send(att2_ref, att2_out)
    loads[2].wait()
    b2_ref[...] = mm(att2_ref[...], wot[...])

    def stage_two(i, carry):
        for g in range(groups):
            fs, at = spots(i, g, rows_g)
            second = as3(first_ref[at, :]) + mod_ref[fs, 5:6, :] * as3(b2_ref[at, :])
            xhat, _ = norm_stats(second)
            n3 = xhat * (1.0 + mod_ref[fs, 7:8, :]) + mod_ref[fs, 6:7, :]
            cot = cot_ref[fs].astype(F32)[:, 8 * g : 8 * g + 8]
            second_ref[at, :] = as2(second)
            n3_ref[at, :] = as2(n3).astype(BF)
            db3_ref[at, :] = as2(mod_ref[fs, 8:9, :] * cot).astype(BF)
        return carry

    lax.fori_loop(0, frames // STEP, stage_two, 0, unroll=8)
    send(n3_ref, n3_out)
    send(db3_ref, db3_out)

    loads[3].wait()
    loads[4].wait()
    b3_ref[...] = jnp.zeros_like(b3_ref)
    dn_ref[...] = jnp.zeros_like(dn_ref)
    wide = FEED_COLS
    part = FEED_ROWS

    def feed(b, carry):
        cols = pl.ds(pl.multiple_of(b * wide, wide), wide)
        for r in range(rows // part):
            at = pl.ds(r * part, part)
            u = mm(n3_ref[at, :], wu[:, cols])
            dh = mm_nt(db3_ref[at, :], wd[cols, :])
            u2 = u * u
            t = jnp.tanh(u * (GELU_C + (GELU_C * GELU_A) * u2))
            half = 0.5 + 0.5 * t
            slope = half + (0.5 * u) * ((1.0 - t * t) * (GELU_C + (3.0 * GELU_C * GELU_A) * u2))
            hid = (u * half).astype(BF)
            dup = (dh * slope).astype(BF)
            hid_ref[at, cols] = hid
            dup_ref[at, cols] = dup
            b3_ref[at, :] += mm(hid, wd[cols, :])
            dn_ref[at, :] += mm_nt(dup, wu[:, cols])
        return carry

    lax.fori_loop(0, ff // wide, feed, 0)
    send(hid_ref, hid_out)
    send(dup_ref, dup_out)

    def stage_three(i, carry):
        parts = [[] for _ in range(4)]
        for g in range(groups):
            fs, at = spots(i, g, rows_g)
            cot = cot_ref[fs].astype(F32)[:, 8 * g : 8 * g + 8]
            second = as3(second_ref[at, :])
            b3 = as3(b3_ref[at, :])
            dn = as3(dn_ref[at, :])
            xhat, rstd = norm_stats(second)
            dsecond = cot + norm_back(dn, xhat, rstd, mod_ref[fs, 7:8, :])
            nat_ref[fs, 8 * g : 8 * g + 8, :] = second + mod_ref[fs, 8:9, :] * b3
            second_ref[at, :] = as2(dsecond)
            db2_ref[at, :] = as2(mod_ref[fs, 5:6, :] * dsecond).astype(BF)
            for k, t in enumerate((dsecond * as3(b2_ref[at, :]), dn, dn * xhat, cot * b3)):
                parts[k].append(t)
        fs, _ = spots(i, 0, rows_g)
        for k in range(4):
            dmod_ref[fs, k : k + 1, :] = over_patches(parts[k])
        mixed_ref[fs] = nat_ref[fs].astype(BF)
        return carry

    lax.fori_loop(0, frames // STEP, stage_three, 0, unroll=8)
    send(second_ref, dsecond_out)
    send(db2_ref, db2_out)
    for copy in stores:
        copy.wait()


FEED_COLS = 1536
FEED_ROWS = 256


def onward(me, bias, modulation, attended, tokens, cotangent, weights, chunk=0, deps=()):
    stripes = len(attended)
    frames, patches, _ = tokens.shape
    rows = frames * patches
    ff = weights[3].shape[1]
    vmem, anywhere = pl.BlockSpec(memory_space=pltpu.VMEM), pl.BlockSpec(memory_space=pl.ANY)
    kept = [(D, BF), (D, BF), (D, BF), (D, BF), (ff, BF), (ff, BF), (D, BF), (D, BF)]
    kept += [(D, F32), (D, F32), (D, F32), (3 * D, BF)]
    outs = call(
        partial(onward_kernel, stripes, chunk),
        (me, bias, modulation, *attended, tokens, cotangent, *weights),
        [pl.BlockSpec(memory_space=pltpu.SMEM)] + [vmem] * (4 + stripes) + [anywhere] * 5,
        deps,
        out_specs=[vmem] * 3 + [anywhere] * len(kept),
        out_shape=[
            jax.ShapeDtypeStruct((frames, patches, D), BF),
            jax.ShapeDtypeStruct((frames, 4, D), F32),
            jax.ShapeDtypeStruct((patches // 8, 16, frames * 8), F32),
        ]
        + [jax.ShapeDtypeStruct((rows, cols), kind) for cols, kind in kept],
        scratch_shapes=[pltpu.VMEM(w.shape, BF) for w in weights]
        + [pltpu.VMEM((rows, cols), kind) for cols, kind in kept]
        + [pltpu.VMEM((frames, patches, D), F32)]
        + [pltpu.VMEM((rows, D), F32)] * 3
        + [pltpu.SemaphoreType.DMA((5,)), pltpu.SemaphoreType.DMA((len(kept),))],
        name="onward",
    )
    names = ("mixed", "dmod", "lse", "att1", "n2", "att2", "n3", "dup", "hid", "db3")
    names += ("db2", "first", "b1", "dsecond", "qkv")
    return dict(zip(names, outs))


def time_back_kernel(stripes, frames, last, *refs):
    me_ref, bias_ref, mod_ref, qkv_ref, db2_ref, att2_ref, lse_ref = refs[:7]
    late_ins, weight_refs = refs[7:10], refs[10:13]
    others = refs[13 : 13 + (NEAR + 3 if last else 0)]
    refs = refs[13 + len(others) :]
    dfirst_ref, dmod_ref = refs[:2]
    datt_refs = refs[2 : 2 + stripes]
    dqkv_out, db1_out = refs[2 + stripes : 4 + stripes]
    (
        first_ref,
        b1_ref,
        dsecond_ref,
        wqkv,
        wot,
        wos,
        dqkv_ref,
        db1_ref,
        nat_ref,
        dn_ref,
        do_ref,
        sums_ref,
        in_sems,
        out_sems,
    ) = refs[4 + stripes :]
    patches = nat_ref.shape[1]
    groups = patches // 8
    rows_g = frames * 8
    per = frames // stripes
    me = me_ref[0]
    mask = first_head()
    held = (wot, wqkv, first_ref, b1_ref, dsecond_ref, wos)
    sources = (weight_refs[1], weight_refs[0]) + tuple(late_ins) + (weight_refs[2],)
    loads = [bring(w, v, in_sems.at[n]) for n, (w, v) in enumerate(zip(sources, held))]
    loads[0].wait()
    do_ref[...] = mm_nt(db2_ref[...], wot[...]).astype(BF)

    def attend_back(g, carry):
        at = pl.ds(pl.multiple_of(g * rows_g, rows_g), rows_g)
        inner = head_sums(att2_ref[at, :], do_ref[at, :])
        for h in range(PAIRS):
            q2, k2, v2 = (
                qkv_ref[at, s * D + h * 128 : s * D + (h + 1) * 128] for s in range(3)
            )
            do2 = do_ref[at, h * 128 : (h + 1) * 128]
            lse = [lse_ref[g, n : n + 1, :] for n in (h, 8 + h)]
            sums = [inner[n : n + 1] for n in (h, 8 + h)]
            grads = attend_pair_back(q2, k2, v2, do2, lse, sums, mask, bias_ref[...])
            for s in range(3):
                dqkv_ref[at, s * D + h * 128 : s * D + (h + 1) * 128] = grads[s].astype(BF)
        return carry

    lax.fori_loop(0, groups, attend_back, 0)
    stores = [bring(dqkv_ref, dqkv_out, out_sems.at[0])]
    for copy in loads[1:]:
        copy.wait()
    dn_ref[...] = mm_nt(dqkv_ref[...], wqkv[...])

    def stage_four(i, carry):
        parts = [[] for _ in range(3)]
        for g in range(groups):
            fs, at = spots(i, g, rows_g)
            dn = as3(dn_ref[at, :])
            xhat, rstd = norm_stats(as3(first_ref[at, :]))
            dfirst = as3(dsecond_ref[at, :]) + norm_back(dn, xhat, rstd, mod_ref[fs, 4:5, :])
            nat_ref[fs, 8 * g : 8 * g + 8, :] = dfirst
            for k, t in enumerate((dfirst * as3(b1_ref[at, :]), dn, dn * xhat)):
                parts[k].append(t)
        fs, _ = spots(i, 0, rows_g)
        for k in range(3):
            dmod_ref[fs, k : k + 1, :] = over_patches(parts[k])
        dfirst = nat_ref[fs]
        dfirst_ref[fs] = dfirst.astype(BF)
        span = STEP * patches
        db1_ref[pl.ds(pl.multiple_of(i * span, span), span), :] = (
            (mod_ref[fs, 2:3, :] * dfirst).astype(BF).reshape(span, D)
        )
        return carry

    lax.fori_loop(0, frames // STEP, stage_four, 0, unroll=8)
    stores.append(bring(db1_ref, db1_out, out_sems.at[1]))
    nat_ref[...] = mm_nt(db1_ref[...], wos[...]).reshape(frames, patches, D)
    if last:
        back, one, two = others[NEAR:]
        sums_ref[:, 0:3, :] = dmod_ref[...] + back[...]
        sums_ref[:, 3:7, :] = one[...] + two[...]
        sums_ref[:, 7:8, :] = jnp.zeros((frames, 1, D), F32)
    for j in range(stripes):
        s = lax.bitwise_xor(me, j)
        mine = nat_ref[pl.ds(s * per, per)].astype(BF)
        if last:
            width = patches
            if j < NEAR:
                width = 2 * patches
                for f in range(per):
                    datt_refs[j][f * width : f * width + patches, :] = others[j][
                        f * patches : (f + 1) * patches, :
                    ]
                    datt_refs[j][f * width + patches : (f + 1) * width, :] = mine[f]
            else:
                datt_refs[j][: per * patches, :] = mine.reshape(per * patches, D)
            datt_refs[j][per * width :, :] = sums_ref[pl.ds(s * per, per)].reshape(
                per * 8, D
            ).astype(BF)
        else:
            datt_refs[j][...] = mine.reshape(per * patches, D)
    for copy in stores:
        copy.wait()


def time_back(me, bias, modulation, onward_outs, weights, stripes, others=(), deps=()):
    o = onward_outs
    frames, patches, _ = o["mixed"].shape
    rows = frames * patches
    per = frames // stripes
    last = bool(others)
    vmem, anywhere = pl.BlockSpec(memory_space=pltpu.VMEM), pl.BlockSpec(memory_space=pl.ANY)
    bf = lambda *shape: jax.ShapeDtypeStruct(shape, BF)
    sends = [
        bf(per * (patches * (2 if j < NEAR else 1) + 8) if last else per * patches, D)
        for j in range(stripes)
    ]
    outs = call(
        partial(time_back_kernel, stripes, frames, last),
        (me, bias, modulation, o["qkv"], o["db2"], o["att2"], o["lse"], o["first"], o["b1"])
        + (o["dsecond"], *weights, *others),
        [pl.BlockSpec(memory_space=pltpu.SMEM)] + [vmem] * 6 + [anywhere] * 6 + [vmem] * len(others),
        deps,
        out_specs=[vmem] * (2 + stripes) + [anywhere] * 2,
        out_shape=[bf(frames, patches, D), jax.ShapeDtypeStruct((frames, 3, D), F32)]
        + sends
        + [bf(rows, 3 * D), bf(rows, D)],
        scratch_shapes=[pltpu.VMEM((rows, D), F32)] * 3
        + [pltpu.VMEM(w.shape, BF) for w in weights]
        + [
            pltpu.VMEM((rows, 3 * D), BF),
            pltpu.VMEM((rows, D), BF),
            pltpu.VMEM((frames, patches, D), F32),
            pltpu.VMEM((rows, D), F32),
            pltpu.VMEM((rows, D), BF),
            pltpu.VMEM((frames, 8, D), F32),
            pltpu.SemaphoreType.DMA((6,)),
            pltpu.SemaphoreType.DMA((2,)),
        ],
        name="time_back",
    )
    return dict(
        dfirst=outs[0], dmod_back=outs[1], sends=outs[2 : 2 + stripes], dqkv=outs[-2], db1=outs[-1]
    )


def finish_kernel(stripes, chunks, me_ref, *refs):
    dv_refs = refs[:stripes]
    first_refs = refs[stripes : stripes + chunks]
    out_ref = refs[-1]
    per = dv_refs[0].shape[0]
    part = first_refs[0].shape[1]
    for j in range(stripes):
        fs = pl.ds(lax.bitwise_xor(me_ref[0], j) * per, per)
        for c in range(chunks):
            spot = pl.ds(c * part, part)
            out_ref[fs, spot, :] = (
                dv_refs[j][:, spot, :].astype(F32) + first_refs[c][fs].astype(F32)
            ).astype(BF)


def finish(me, dvs, firsts, deps=()):
    stripes, chunks = len(dvs), len(firsts)
    frames, part, _ = firsts[0].shape
    vmem = pl.BlockSpec(memory_space=pltpu.VMEM)
    return call(
        partial(finish_kernel, stripes, chunks),
        (me, *dvs, *firsts),
        [pl.BlockSpec(memory_space=pltpu.SMEM)] + [vmem] * (stripes + chunks),
        deps,
        out_specs=vmem,
        out_shape=jax.ShapeDtypeStruct((frames, part * chunks, D), BF),
        name="finish",
    )


def flip(x, axis, bit):
    size = lax.axis_size(axis)
    return lax.ppermute(x, axis, [(i, i ^ bit) for i in range(size)])


def exchange(blocks):
    return [blocks[0]] + [flip(blocks[j], "blk", j) for j in range(1, len(blocks))]


def double(x, axis, bit, dim):
    own = (lax.axis_index(axis) // bit) % 2
    got = flip(x, axis, bit)
    low = jnp.where(own == 0, x, got)
    high = jnp.where(own == 0, got, x)
    return jnp.concatenate([low, high], dim)


def bits_of(size):
    return [1 << b for b in range(size.bit_length() - 1)]


def weight_grad_kernel(pairs, by_rows, held, bit_ref, *refs):
    a_refs, b_refs = refs[:pairs], refs[pairs : 2 * pairs]
    keep_ref, *send_refs, total_ref = refs[2 * pairs + held :]
    total = mm_tn(a_refs[0][...], b_refs[0][...])
    for a, b in zip(a_refs[1:], b_refs[1:]):
        total = total + mm_tn(a[...], b[...])
    total_ref[...] = total.reshape(total_ref.shape)
    bit = bit_ref[0]
    if by_rows:
        keep_ref[...] = total_ref[:, :, bit].astype(BF)
        send_refs[0][...] = total_ref[:, :, 1 - bit].astype(BF)
    else:
        keep_ref[:, 0] = total_ref[:, bit].astype(BF)
        deep = send_refs[0].shape[0]
        for n, send_ref in enumerate(send_refs):
            send_ref[:, 0] = total_ref[n * deep : (n + 1) * deep, 1 - bit].astype(BF)


def weight_grad(bit, firsts, seconds, stripes, units, at, held, deps=(), cuts=1):
    pairs = len(firsts)
    rows, cols = firsts[0].shape[1], seconds[0].shape[1]
    small = D // stripes
    half = small // 2
    by_rows = rows > D
    tall = D if cols % D == 0 else D // 2
    steps = rows // D if by_rows else cols // tall
    if by_rows:
        deep = rows // D
        wide = stripes // steps
        shape, spot = (wide, deep, half, D), lambda t: (t, at // deep, 0, 0)
        total = (wide, deep, 2, half, D)
    else:
        shape, spot = (stripes, 1, half, tall), lambda t: (0, at + t, 0, 0)
        total = (stripes, 2, half, tall)
    moving, still = (lambda t: (0, t)), (lambda t: (0, 0))
    block = pl.BlockSpec(shape, spot)
    send = pl.BlockSpec((shape[0] // cuts,) + shape[1:], spot)
    group = [jax.ShapeDtypeStruct((stripes, units, half, tall), BF)]
    group += [jax.ShapeDtypeStruct((stripes // cuts, units, half, tall), BF)] * cuts
    aliased = held is not None
    return call(
        partial(weight_grad_kernel, pairs, by_rows, 1 + cuts if aliased else 0),
        (bit, *firsts, *seconds, *(held or ())),
        [pl.BlockSpec(memory_space=pltpu.SMEM)]
        + [pl.BlockSpec((a.shape[0], D), moving if by_rows else still) for a in firsts]
        + [pl.BlockSpec((b.shape[0], tall), still if by_rows else moving) for b in seconds]
        + [ANYWHERE] * (1 + cuts if aliased else 0),
        deps,
        grid=(steps,),
        out_specs=[block] + [send] * cuts,
        scratch_shapes=[pltpu.VMEM(total, F32)],
        out_shape=group,
        input_output_aliases={2 * pairs + 1 + n: n for n in range(1 + cuts)} if aliased else {},
        name="weight_grad",
    )


def mod_grad_kernel(samples, *refs):
    g_refs, refs = refs[:samples], refs[samples:]
    w_ref, cond_ref, slope_ref, hit_ref, gw_ref, gb_ref, table_ref, g_ref, total_ref = refs
    step = pl.program_id(0)
    rows = w_ref.shape[0]

    @pl.when(step == 0)
    def _():
        at = 0
        for r in g_refs:
            g_ref[at : at + r.shape[0], :] = r[...]
            at += r.shape[0]
        for k in range(g_ref.shape[1] // D):
            cols = slice(k * D, (k + 1) * D)
            gw_ref[:, cols] = mm_tn(cond_ref[...], g_ref[:, cols])
            gb_ref[:, cols] = jnp.sum(g_ref[:, cols].astype(F32), 0, keepdims=True)

    total_ref[pl.ds(pl.multiple_of(step * rows, rows), rows), :] = mm_nt(w_ref[...], g_ref[...])

    @pl.when(step == pl.num_programs(0) - 1)
    def _():
        e = total_ref[...].T * slope_ref[...]
        high = e.astype(BF)
        low = (e - high.astype(F32)).astype(BF)
        table_ref[...] = mm(hit_ref[...], high) + mm(hit_ref[...], low)


def pack_kernel(first_ref, late_ref, out_ref):
    frames = first_ref.shape[0]
    for f in range(frames):
        both = [first_ref[f], late_ref[8 * f : 8 * f + 7, :]]
        out_ref[f] = jnp.concatenate(both, 0).astype(BF)


def pack(first_sums, late, deps):
    vmem = pl.BlockSpec(memory_space=pltpu.VMEM)
    frames = first_sums.shape[0]
    return call(
        pack_kernel,
        (first_sums, late),
        [vmem, vmem],
        deps,
        out_specs=vmem,
        out_shape=jax.ShapeDtypeStruct((frames, 9, D), BF),
        name="pack",
    )


def mod_grads(gs, weight, cond_own, slope, hit_own, deps):
    rows = slope.shape[0]
    still = lambda k: (0, 0)
    cols = weight.shape[1]
    each = 256
    wide, span = cond_own.shape[1], hit_own.shape[0]
    return call(
        partial(mod_grad_kernel, len(gs)),
        (*gs, weight, cond_own, slope, hit_own),
        [pl.BlockSpec((g.shape[0], cols), still) for g in gs]
        + [
            pl.BlockSpec((each, cols), lambda k: (k, 0)),
            pl.BlockSpec((rows, wide), still),
            pl.BlockSpec((rows, D), still),
            pl.BlockSpec((span, rows), still),
        ],
        deps,
        grid=(D // each,),
        out_specs=[
            pl.BlockSpec((wide, cols), still),
            pl.BlockSpec((1, cols), still),
            pl.BlockSpec((span, D), still),
        ],
        out_shape=[
            jax.ShapeDtypeStruct((wide, cols), F32),
            jax.ShapeDtypeStruct((1, cols), F32),
            jax.ShapeDtypeStruct((span, D), F32),
        ],
        scratch_shapes=[pltpu.VMEM((rows, cols), BF), pltpu.VMEM((D, rows), F32)],
        name="mod_grads",
    )


ORDER = (0, 2, 1, 3)


def of_four(x):
    across = flip(x, "dp", 2)
    return [x, across, flip(x, "dp", 1), flip(across, "dp", 1)]


def of_samples(x):
    if lax.axis_size("dp") == 4:
        return of_four(x)
    return [lax.all_gather(x, "dp", tiled=True)]


def add_split_kernel(cut, parts, bit_ref, keep_ref, *refs):
    got_refs, outs = refs[:parts], refs[parts:]
    bit = bit_ref[0]
    for out, side in zip(outs, (bit, 1 - bit)):
        if cut == "stripe":
            spot = (slice(None), side)
        else:
            half = keep_ref.shape[-1] // 2
            spot = (slice(None),) * 3 + (pl.ds(pl.multiple_of(side * half, half), half),)
        got = got_refs[0][spot].astype(F32)
        if parts == 2:
            low = pl.program_id(0) < pl.num_programs(0) // 2
            got = jnp.where(low, got, got_refs[1][spot].astype(F32))
        out[...] = (keep_ref[spot].astype(F32) + got).astype(BF)


def add_split(bit, keep, got, cut, deps=()):
    count, units, rows, cols = keep.shape
    parts = len(got)
    if cut == "stripe":
        keep, *got = (x.reshape(count // 2, 2, units, rows, cols) for x in (keep, *got))
        out = (count // 2, units, rows, cols)
        each = min(2, count // 2)
        steps = count // 2 // each
        in_spec = pl.BlockSpec((each, 2, units, rows, cols), lambda i: (i, 0, 0, 0, 0))
        got_specs = [in_spec]
        out_block = pl.BlockSpec((each, units, rows, cols), lambda i: (i, 0, 0, 0))
    else:
        each = 2
        steps = count // each
        out = (count, units, rows, cols // 2)
        shape = (each, units, rows, cols)
        in_spec = pl.BlockSpec(shape, lambda i: (i, 0, 0, 0))
        got_specs = [in_spec]
        if parts == 2:
            half = steps // 2
            got_specs = [
                pl.BlockSpec(shape, lambda i: (jnp.minimum(i, half - 1), 0, 0, 0)),
                pl.BlockSpec(shape, lambda i: (jnp.maximum(i - half, 0), 0, 0, 0)),
            ]
        out_block = pl.BlockSpec((each, units, rows, cols // 2), lambda i: (i, 0, 0, 0))
    return call(
        partial(add_split_kernel, cut, parts),
        (bit, keep, *got),
        [pl.BlockSpec(memory_space=pltpu.SMEM), in_spec, *got_specs],
        deps,
        grid=(steps,),
        out_specs=[out_block] * 2,
        out_shape=[jax.ShapeDtypeStruct(out, BF)] * 2,
        name="add_split",
    )


def assemble_kernel(layout, at_ref, *refs):
    shares, outs = refs[:4], refs[4:]
    half, cols = shares[0].shape[1:]
    for n, j in enumerate(ORDER):
        place = lax.bitwise_xor(at_ref[0], j)
        unit = 0
        for out, (deep, wide, halved) in zip(outs, layout):
            core, side = lax.rem(place, 2), lax.div(place, 2)
            if halved:
                core, side = side, core
            low = pl.multiple_of(core * half, half)
            step = cols if halved else 2 * cols
            left = pl.multiple_of(side * (wide * cols if halved else cols), cols)
            for r in range(deep):
                for c in range(wide):
                    out[pl.ds(r * 2 * half + low, half), pl.ds(c * step + left, cols)] = shares[n][
                        unit
                    ].astype(F32)
                    unit += 1


def assemble(at, shares, layout, deps):
    _, half, cols = shares[0].shape
    vmem = pl.BlockSpec(memory_space=pltpu.VMEM)
    return call(
        partial(assemble_kernel, layout),
        (at, *shares),
        [pl.BlockSpec(memory_space=pltpu.SMEM)] + [vmem] * 4,
        deps,
        out_specs=[vmem] * len(layout),
        out_shape=[
            jax.ShapeDtypeStruct((deep * 2 * half, wide * 2 * cols), F32)
            for deep, wide, _ in layout
        ],
        name="assemble",
    )


def bit_of(axis, bit):
    return ((lax.axis_index(axis) // bit) % 2).astype(jnp.int32).reshape(1)


def add_deal_kernel(groups, at_ref, *refs):
    keeps, gots, outs = refs[:groups], refs[groups : 2 * groups], refs[2 * groups :]
    for j, out in enumerate(outs):
        s = lax.bitwise_xor(at_ref[0], j)
        unit = 0
        for keep, got in zip(keeps, gots):
            n = keep.shape[1]
            out[unit : unit + n] = (keep[s].astype(F32) + got[s].astype(F32)).astype(BF)
            unit += n


def add_deal(at, keeps, gots, deps):
    vmem = pl.BlockSpec(memory_space=pltpu.VMEM)
    places, _, half, cols = keeps[0].shape
    units = sum(k.shape[1] for k in keeps)
    return call(
        partial(add_deal_kernel, len(keeps)),
        (at, *keeps, *gots),
        [pl.BlockSpec(memory_space=pltpu.SMEM)] + [vmem] * (2 * len(keeps)),
        deps,
        out_specs=[vmem] * places,
        out_shape=[jax.ShapeDtypeStruct((units, half, cols), BF)] * places,
        name="add_deal",
    )


def add_many_kernel(*refs):
    total = refs[0][...].astype(F32)
    for r in refs[1:-1]:
        total = total + r[...].astype(F32)
    refs[-1][...] = total.astype(BF)


def add_many(arrays, deps):
    vmem = pl.BlockSpec(memory_space=pltpu.VMEM)
    return call(
        add_many_kernel,
        tuple(arrays),
        [vmem] * len(arrays),
        deps,
        out_specs=vmem,
        out_shape=jax.ShapeDtypeStruct(arrays[0].shape, BF),
        name="add_many",
    )


class Reduction:
    def __init__(self, group, layout, halved=False):
        self.layout = [entry + (halved,) for entry in layout]
        bit = 2 if halved else 1
        self.states = [(group[0], [flip(send, "dp", bit) for send in group[1:]])]
        stripe_bits = bits_of(lax.axis_size("blk"))
        self.todo = [] if halved else [("dp", 2, "column")]
        self.todo += [("blk", bit, "stripe") for bit in stripe_bits]

    def step(self, deps=()):
        axis, bit, cut = self.todo.pop(0)
        keep, send = add_split(bit_of(axis, bit), *self.states[0], cut, deps)
        self.states = [(keep, [flip(send, axis, bit)])]
        return send

    def join(self, other):
        self.states += other.states
        self.layout += other.layout

    def deal(self, deps):
        at = (lax.axis_index("blk") // 2).astype(jnp.int32).reshape(1)
        keeps, gots = zip(*((keep, got[0]) for keep, got in self.states))
        sends = add_deal(at, keeps, gots, deps)
        self.states = [sends[0]] + [flip(x, "blk", 2 * j) for j, x in enumerate(sends) if j]
        self.todo = []
        return sends[0]

    def gather(self, deps):
        if isinstance(self.states[0], tuple):
            keep, (got,) = self.states[0]
            self.states = [keep[0], got[0]]
        share = add_many(self.states, deps)
        for bit in bits_of(lax.axis_size("dp"))[2:]:
            share = (share.astype(F32) + flip(share, "dp", bit).astype(F32)).astype(BF)
        self.states = of_four(share)
        return share

    def result(self, deps=()):
        at = (lax.axis_index("dp") % 4).astype(jnp.int32).reshape(1)
        return assemble(at, self.states, self.layout, deps)


def gather_frames(x):
    bits = bits_of(lax.axis_size("blk"))
    shape = x.shape
    x = x.reshape((1,) * len(bits) + shape)
    for n, bit in reversed(list(enumerate(bits))):
        x = double(x, "blk", bit, len(bits) - 1 - n)
    return x.reshape((-1,) + shape[1:])


def shards(
    tokens,
    frame_seg,
    clip_class,
    class_table,
    mod_weight,
    mod_bias,
    qkv_space,
    out_space,
    qkv_time,
    out_time,
    up_weight,
    down_weight,
    cotangent,
):
    stripes = lax.axis_size("blk")
    stripe = lax.axis_index("blk")
    me = stripe.astype(jnp.int32).reshape(1)
    tokens, cotangent = tokens[0], cotangent[0]
    frames, patches, _ = tokens.shape
    per = frames // stripes
    chunks = 2
    part = patches // chunks
    classes = class_table.shape[0]

    blocks = [
        lax.dynamic_slice_in_dim(tokens, (stripe ^ j) * per, per, 0) for j in range(stripes)
    ]
    blocks = exchange(blocks)

    segment = frame_seg[0]
    clip_ids = clip_class[0]
    clip_hit = segment[:, None] == jnp.arange(clip_ids.shape[0], dtype=jnp.int32)[None, :]
    frame_class = jnp.sum(jnp.where(clip_hit, clip_ids[None, :], 0), axis=1)

    def embed(class_of):
        hit = class_of[:, None] == jnp.arange(classes, dtype=jnp.int32)[None, :]
        return hit, jnp.dot(hit.astype(F32), class_table, precision=exact_mode)

    cond = jax.nn.silu(embed(frame_class)[1]).astype(BF)
    hit_all, embedded_all = embed(jnp.concatenate(of_samples(frame_class)))
    cond_all, silu_back = jax.vjp(jax.nn.silu, embedded_all)
    slope = silu_back(jnp.ones_like(cond_all))[0]
    width, span = D // stripes, classes // stripes
    cond_own = lax.dynamic_slice_in_dim(cond_all.astype(BF), stripe * width, width, 1)
    hit_own = lax.dynamic_slice_in_dim(hit_all.astype(BF).T, stripe * span, span, 0)
    modulation = jnp.dot(cond, mod_weight, preferred_element_type=F32) + mod_bias
    modulation = modulation.reshape(frames, 9, D)
    mod_own = lax.dynamic_slice_in_dim(modulation, stripe * per, per, 0)[:, :2]
    spot_frame = jnp.repeat(jnp.arange(frames), 8)
    spot_patch = jnp.tile(jnp.arange(8), frames)
    spot_seg = jnp.repeat(segment, 8)
    bias = jnp.where(
        (spot_seg[:, None] == spot_seg[None, :]) & (spot_patch[:, None] == spot_patch[None, :]),
        0.0,
        masked_score,
    ).astype(F32)

    core = bit_of("dp", 1)
    sends, normed_one, kept_one = space_forward(blocks, mod_own, qkv_space, chunks)
    attended = [sends[0]] + [
        flip(b, "blk", j) for b, (j, _, _) in list(zip(sends, pieces(stripes, patches, chunks)))[1:]
    ]
    normed_one = normed_one.reshape(-1, D)
    normed_pair = flip(normed_one, "dp", 1)
    weights = (out_space, qkv_time, out_time, up_weight, down_weight)
    parts = []
    for c in range(chunks):
        here = slice(c * part, (c + 1) * part)
        parts.append(
            onward(
                me,
                bias,
                modulation,
                chunk_of(attended, stripes, c),
                tokens[:, here],
                cotangent[:, here],
                weights,
                c,
                [parts[-1]["n3"], normed_pair] if parts else (),
            )
        )
    output = jnp.concatenate([p["mixed"] for p in parts], 1)

    def grad_into(held, units, at, first, second, deps=(), cuts=1):
        return weight_grad(
            core,
            [p[first] for p in parts],
            [p[second] for p in parts],
            stripes,
            units,
            at,
            held,
            deps,
            cuts,
        )

    deep, wide = up_weight.shape[1] // D, qkv_time.shape[1] // D
    group = grad_into(None, 2 * deep, 0, "n3", "dup")
    group = grad_into(group, 2 * deep, deep, "hid", "db3")
    feed = Reduction(group, ((1, deep), (deep, 1)))
    units = wide + 2
    group_time = grad_into(None, units, 0, "att2", "db2", [group[1]], 2)
    dep = group_time[1]
    back = (qkv_time, out_time, out_space)
    one, two = parts
    one.update(time_back(me, bias, modulation, one, back, stripes, (), [dep]))
    two.update(
        time_back(
            me,
            bias,
            modulation,
            two,
            back,
            stripes,
            [*one["sends"][:NEAR], one["dmod_back"], one["dmod"], two["dmod"]],
        )
    )
    far = [flip(one["sends"][j], "blk", j) for j in range(NEAR, stripes)]
    rest = exchange(two["sends"])
    grads = rest[:NEAR] + far + rest[NEAR:]
    dep = feed.step([two["db1"], *far])
    group = grad_into(group_time, units, 1, "n2", "dqkv", [dep], 2)
    group = grad_into(group, units, wide + 1, "att1", "db1", rest[5:], 2)
    time = Reduction(group, ((1, 1), (1, wide), (1, 1)))
    dqkv_one, dqkv_own, dqkv_pair, late = space_backward(
        core, grads, kept_one, stripes, chunks, [group[1]]
    )
    dqkv_pair = flip(dqkv_pair, "dp", 1)
    dep = feed.step([late])
    dep = time.step([dep])
    group = weight_grad(
        bit_of("dp", 2),
        [normed_one, normed_pair],
        [dqkv_own, dqkv_pair],
        stripes,
        wide,
        0,
        None,
        [dep],
    )
    space = Reduction(group, ((1, wide),), True)
    dvs, first_sums = space_norm(blocks, mod_own, qkv_space, dqkv_one, [group[1]])
    dvs = exchange(dvs)
    dep = feed.step([first_sums])
    dep = time.step([dep, *dvs[6:8]])
    dep = space.step([dep, *dvs[4:6]])
    dep = feed.step([dep])
    time.join(space)
    dep = time.deal([dep])
    mod_grad = pack(first_sums, late, [dep]).reshape(per, 9 * D)
    mod_grad = gather_frames(mod_grad)
    dep = feed.gather([mod_grad])
    mod_grad = of_samples(mod_grad)
    input_grad = finish(me, dvs, [p["dfirst"] for p in parts], [dep])
    grad_mod_weight, grad_mod_bias, grad_table = mod_grads(
        mod_grad, mod_weight, cond_own, slope, hit_own, [input_grad]
    )
    share = mod_bias.shape[0] // stripes
    grad_mod_bias = lax.dynamic_slice_in_dim(grad_mod_bias.reshape(-1), stripe * share, share, 0)
    time.gather([grad_table])
    grad_up, grad_down = feed.result()
    grad_out_time, grad_qkv_time, grad_out_space, grad_qkv_space = time.result()
    return (
        output[None],
        input_grad[None],
        grad_table,
        grad_mod_weight,
        grad_mod_bias,
        grad_qkv_space,
        grad_out_space,
        grad_qkv_time,
        grad_out_time,
        grad_up,
        grad_down,
    )


def solution(mesh):
    tile = P("dp", None, "blk", None)
    row = P("blk", None)
    in_specs = (tile, P("dp", None), P("dp", None)) + (P(),) * 9 + (tile,)
    out_specs = (tile, tile, row, row, P("blk")) + (row,) * 6
    return jax.shard_map(shards, mesh=mesh, in_specs=in_specs, out_specs=out_specs, check_vma=False)
```
